128 devices in a mesh: dp: 32 (over y, z_lo, x), mp: 4 (over z_hi, core).
Axes of the slice: x: 4, y: 4, z: 4 (z_hi: 2, z_lo: 2; z = z_hi * 2 + z_lo), core: 2. Of those that a mesh axis runs over, the one named last changes fastest.
Arguments:
- tokens: bfloat16 [64, 384, 1536], P('dp'), may hold values from -6 to 6
- cotangent: bfloat16 [64, 384, 1536], P('dp'), may hold values from -6 to 6
- lengths: int32 [64], replicated, may hold values from 96 to 384, as said below
- dealing: int32 [64], replicated, may hold values from 0 to 63, each once
- adapter_choice: int32 [64], replicated, may hold values from 0 to 7
- attention_gain: float32 [1536], replicated, may hold values from 0.5 to 1.5
- feedforward_gain: float32 [1536], replicated, may hold values from 0.5 to 1.5
- query_weight: bfloat16 [1536, 1536], P('dp', 'mp'), may hold values from -0.15625 to 0.15625
- key_weight: bfloat16 [1536, 768], P('dp', 'mp'), may hold values from -0.15625 to 0.15625
- value_weight: bfloat16 [1536, 768], P('dp', 'mp'), may hold values from -0.15625 to 0.15625
- output_weight: bfloat16 [1536, 1536], P('mp', 'dp'), may hold values from -0.4375 to 0.4375
- gate_weight: bfloat16 [1536, 4096], P('dp', 'mp'), may hold values from -0.15625 to 0.15625
- up_weight: bfloat16 [1536, 4096], P('dp', 'mp'), may hold values from -0.15625 to 0.15625
- down_weight: bfloat16 [4096, 1536], P('mp', 'dp'), may hold values from -0.09375 to 0.09375
- entry_qkv: bfloat16 [1536, 384], P('dp'), may hold values from -0.15625 to 0.15625
- exit_query: bfloat16 [128, 1536], P('dp', 'mp'), may hold values from -1.5 to 1.5
- exit_key: bfloat16 [128, 768], P('dp', 'mp'), may hold values from -1.5 to 1.5
- exit_value: bfloat16 [128, 768], P('dp', 'mp'), may hold values from -1.5 to 1.5
- entry_out: bfloat16 [1536, 128], P('mp', 'dp'), may hold values from -0.4375 to 0.4375
- exit_out: bfloat16 [128, 1536], P('dp'), may hold values from -1.5 to 1.5
- entry_gate_up: bfloat16 [1536, 256], P('dp'), may hold values from -0.15625 to 0.15625
- exit_gate: bfloat16 [128, 4096], P('dp', 'mp'), may hold values from -1.5 to 1.5
- exit_up: bfloat16 [128, 4096], P('dp', 'mp'), may hold values from -1.5 to 1.5
- entry_down: bfloat16 [4096, 128], P('mp', 'dp'), may hold values from -0.09375 to 0.09375
- exit_down: bfloat16 [128, 1536], P('dp'), may hold values from -1.5 to 1.5
Outputs:
- mixed: bfloat16 [64, 384, 1536], P('dp')
- input_grad: bfloat16 [64, 384, 1536], P('dp')
- grad_entry_qkv: float32 [1536, 384], P('dp')
- grad_exit_query: float32 [128, 1536], P('dp', 'mp')
- grad_exit_key: float32 [128, 768], P('dp', 'mp')
- grad_exit_value: float32 [128, 768], P('dp', 'mp')
- grad_entry_out: float32 [1536, 128], P('mp', 'dp')
- grad_exit_out: float32 [128, 1536], P('dp')
- grad_entry_gate_up: float32 [1536, 256], P('dp')
- grad_exit_gate: float32 [128, 4096], P('dp', 'mp')
- grad_exit_up: float32 [128, 4096], P('dp', 'mp')
- grad_entry_down: float32 [4096, 128], P('mp', 'dp')
- grad_exit_down: float32 [128, 1536], P('dp')
The draws below stay inside these ranges and needn't reach their ends.
Inputs may be any that keep to these rules, and one draw needn't show every extreme that they name: `lengths`: each sequence has at least 96 tokens and some sequence exactly 384. `dealing`: each slot number appears once.
All inputs are finite; a program needn't handle non-finite values.
Results may differ from the reference program's by a relative error of at most 0.025.
Values may be sent and summed in bfloat16 or wider, within the bound.
No kernel may reach another device: no remote copies, remote signals or barrier semaphores. Data moves between devices by JAX's collectives and lax.ppermute only.
A program may use at most 192 MiB of HBM per device.

```python
import jax
import jax.numpy as jnp
from jax import lax

D = 1536
HEADS = 16
KV_HEADS = 8
HEAD_DIM = 96
FF = 4096
RANK = 16
ADAPTERS = 8
BLOCK = 384
MIN_LEN = 96
SLOTS = 64


def draw_lengths(key, part):
    key = jax.random.fold_in(key, 7)
    first, second = jax.random.split(key)
    drawn = jax.random.randint(first, (SLOTS,), MIN_LEN, BLOCK + 1)
    chosen = jax.random.randint(second, (), 0, SLOTS)
    return jnp.where(jnp.arange(SLOTS) == chosen, BLOCK, drawn).astype(jnp.int32)


def set_ends(values, own_key, smallest, top_value):
    shape = values.shape
    index_at = [jax.random.randint(jax.random.fold_in(own_key, axis), (), 0, shape[axis]) for axis in range(len(shape))]
    values = values.at[tuple(index_at)].set(smallest)
    longest = shape.index(max(shape))
    index_at[longest] = (index_at[longest] + 1) % shape[longest]
    return values.at[tuple(index_at)].set(top_value)


def block_scale(rng, extent, pieces, smallest, high):
    gain = 1.0
    for dim, shards_of in pieces:
        draws = jax.random.uniform(jax.random.fold_in(jax.random.fold_in(rng, 6), dim), (shards_of,), jnp.float32, smallest / len(pieces), high / len(pieces))
        gain = gain * jnp.repeat(jnp.exp(draws), extent[dim] // shards_of).reshape((-1,) + (1,) * (len(extent) - 1 - dim))
    return gain


def centred(own_key, shape, scale, reach, shards=(), held_as=jnp.bfloat16):
    level = block_scale(own_key, shape, shards, -0.22, 0.18) if shards else 1.0
    values = jax.random.normal(own_key, shape, jnp.float32) * scale * level
    return jnp.minimum(jnp.maximum(values, -reach), reach).astype(held_as)


def setup_inputs(seed: int = 0) -> dict:
    arg_keys = jax.random.split(jax.random.key(seed), 26)
    tokens = centred(arg_keys[0], (SLOTS, BLOCK, D), 1.0, 6.0, ((0, 32),))
    cotangent = centred(arg_keys[1], (SLOTS, BLOCK, D), 1.0, 6.0, ((0, 32),))
    lengths = draw_lengths(jax.random.fold_in(arg_keys[25], 71), 0)
    dealing = jax.random.permutation(arg_keys[3], SLOTS).astype(jnp.int32)
    adapter_choice = set_ends(jax.random.randint(arg_keys[4], (SLOTS,), 0, ADAPTERS), jax.random.fold_in(arg_keys[4], 1), 0, ADAPTERS - 1).astype(jnp.int32)
    attention_gain = jnp.clip(jax.random.uniform(arg_keys[5], (D,), jnp.float32, 0.5, 1.5), 0.5, 1.5)
    feedforward_gain = jnp.clip(jax.random.uniform(arg_keys[6], (D,), jnp.float32, 0.5, 1.5), 0.5, 1.5)
    query_weight = centred(arg_keys[7], (D, HEADS * HEAD_DIM), D ** -0.5, 0.15625, ((0, 32), (1, 4)))
    key_weight = centred(arg_keys[8], (D, KV_HEADS * HEAD_DIM), D ** -0.5, 0.15625, ((0, 32), (1, 4)))
    value_weight = centred(arg_keys[9], (D, KV_HEADS * HEAD_DIM), D ** -0.5, 0.15625, ((0, 32), (1, 4)))
    output_weight = centred(arg_keys[10], (HEADS * HEAD_DIM, D), (HEADS * HEAD_DIM // 8) ** -0.5, 0.4375, ((0, 4), (1, 32)))
    gate_weight = centred(arg_keys[11], (D, FF), D ** -0.5, 0.15625, ((0, 32), (1, 4)))
    up_weight = centred(arg_keys[12], (D, FF), D ** -0.5, 0.15625, ((0, 32), (1, 4)))
    down_weight = centred(arg_keys[13], (FF, D), FF ** -0.5, 0.09375, ((0, 4), (1, 32)))
    entry_qkv = centred(arg_keys[14], (D, 3 * ADAPTERS * RANK), D ** -0.5, 0.15625, ((0, 32),))
    exit_query = centred(arg_keys[15], (ADAPTERS * RANK, HEADS * HEAD_DIM), RANK ** -0.5, 1.5, ((0, 32), (1, 4)))
    exit_key = centred(arg_keys[16], (ADAPTERS * RANK, KV_HEADS * HEAD_DIM), RANK ** -0.5, 1.5, ((0, 32), (1, 4)))
    exit_value = centred(arg_keys[17], (ADAPTERS * RANK, KV_HEADS * HEAD_DIM), RANK ** -0.5, 1.5, ((0, 32), (1, 4)))
    entry_out = centred(arg_keys[18], (HEADS * HEAD_DIM, ADAPTERS * RANK), (HEADS * HEAD_DIM // 8) ** -0.5, 0.4375, ((0, 4), (1, 32)))
    exit_out = centred(arg_keys[19], (ADAPTERS * RANK, D), RANK ** -0.5, 1.5, ((0, 32),))
    entry_gate_up = centred(arg_keys[20], (D, 2 * ADAPTERS * RANK), D ** -0.5, 0.15625, ((0, 32),))
    exit_gate = centred(arg_keys[21], (ADAPTERS * RANK, FF), RANK ** -0.5, 1.5, ((0, 32), (1, 4)))
    exit_up = centred(arg_keys[22], (ADAPTERS * RANK, FF), RANK ** -0.5, 1.5, ((0, 32), (1, 4)))
    entry_down = centred(arg_keys[23], (FF, ADAPTERS * RANK), FF ** -0.5, 0.09375, ((0, 4), (1, 32)))
    exit_down = centred(arg_keys[24], (ADAPTERS * RANK, D), RANK ** -0.5, 1.5, ((0, 32),))
    return {"tokens": tokens, "cotangent": cotangent, "lengths": lengths, "dealing": dealing, "adapter_choice": adapter_choice, "attention_gain": attention_gain, "feedforward_gain": feedforward_gain, "query_weight": query_weight, "key_weight": key_weight, "value_weight": value_weight, "output_weight": output_weight, "gate_weight": gate_weight, "up_weight": up_weight, "down_weight": down_weight, "entry_qkv": entry_qkv, "exit_query": exit_query, "exit_key": exit_key, "exit_value": exit_value, "entry_out": entry_out, "exit_out": exit_out, "entry_gate_up": entry_gate_up, "exit_gate": exit_gate, "exit_up": exit_up, "entry_down": entry_down, "exit_down": exit_down}


@jax.custom_vjp
def low(v):
    return lax.optimization_barrier(v.astype(jnp.bfloat16)).astype(jnp.float32)

@jax.custom_vjp
def low_back(v):
    return v

def low_keep(v):
    return (low(v), None)

def low_pass(kept, grad):
    return (grad,)

def back_keep(v):
    return (v, None)

def back_low(kept, grad):
    return (low(grad),)
low.defvjp(low_keep, low_pass)
low_back.defvjp(back_keep, back_low)
EPS = 1e-05
THETA = 100000.0
HIGHEST = lax.Precision.HIGHEST

def matmul(left, right):
    return jnp.dot(left, right, precision=HIGHEST, preferred_element_type=jnp.float32)

def rope_tables(count_rows):
    half = HEAD_DIM // 2
    freq = jnp.power(THETA, -2.0 * jnp.arange(half, dtype=jnp.float32) / HEAD_DIM)
    angle = jnp.arange(count_rows, dtype=jnp.float32)[:, None] * freq[None, :]
    return (jnp.cos(angle), jnp.sin(angle))

def rotate(values, cosine, sine):
    half = values.shape[-1] // 2
    first = values[..., :half]
    second = values[..., half:]
    cosine = cosine[:, None, :]
    sine = sine[:, None, :]
    return jnp.concatenate([first * cosine - second * sine, second * cosine + first * sine], axis=-1)

def rms_scale(values):
    return lax.rsqrt(lax.optimization_barrier(jnp.mean(values * values, axis=-1, keepdims=True)) + EPS)

def slot_forward(rows, length, chosen, attention_gain, feedforward_gain, frozen, adjusted):
    query_weight, key_weight, value_weight, output_weight, gate_weight, up_weight, down_weight = frozen
    entry_qkv, exit_query, exit_key, exit_value, entry_out, exit_out, entry_gate_up, exit_gate, exit_up, entry_down, exit_down = adjusted
    count_rows = rows.shape[0]
    width = exit_query.shape[0]
    positions = jnp.arange(count_rows)
    live = positions < length
    select = (jnp.arange(width) // RANK == chosen).astype(jnp.float32)
    normed = low(rows * rms_scale(rows) * attention_gain)
    rank_qkv = low(low_back(matmul(normed, entry_qkv) * jnp.tile(select, 3)))
    queries = low_back(matmul(normed, query_weight) + matmul(rank_qkv[:, :width], exit_query))
    keys = low_back(matmul(normed, key_weight) + matmul(rank_qkv[:, width:2 * width], exit_key))
    values = low(low_back(matmul(normed, value_weight) + matmul(rank_qkv[:, 2 * width:], exit_value)))
    cosine, sine = rope_tables(count_rows)
    queries = low(rotate(queries.reshape(count_rows, HEADS, HEAD_DIM), cosine, sine))
    keys = low(rotate(keys.reshape(count_rows, KV_HEADS, HEAD_DIM), cosine, sine))
    grouped = queries.reshape(count_rows, KV_HEADS, HEADS // KV_HEADS, HEAD_DIM)
    raw = jnp.einsum('qjgd,kjd->jgqk', grouped, keys, precision=HIGHEST)
    scores = low_back(raw * HEAD_DIM ** (-0.5))
    allowed = (positions[None, :] <= positions[:, None]) & live[None, :]
    probs = low(jax.nn.softmax(jnp.where(allowed, scores, -1e+30), axis=-1))
    attended = jnp.einsum('jgqk,kjd->qjgd', probs, values.reshape(count_rows, KV_HEADS, HEAD_DIM), precision=HIGHEST)
    attended = low(low_back(attended.reshape(count_rows, HEADS * HEAD_DIM)))
    rank_out = low(low_back(matmul(attended, entry_out) * select))
    middle = rows + low_back(matmul(attended, output_weight) + matmul(rank_out, exit_out))
    hidden_in = low(middle * rms_scale(middle) * feedforward_gain)
    rank_gate_up = low(low_back(matmul(hidden_in, entry_gate_up) * jnp.tile(select, 2)))
    gate = low_back(matmul(hidden_in, gate_weight) + matmul(rank_gate_up[:, :width], exit_gate))
    up = low_back(matmul(hidden_in, up_weight) + matmul(rank_gate_up[:, width:], exit_up))
    activated = low(jax.nn.silu(gate) * up)
    rank_down = low(low_back(matmul(activated, entry_down) * select))
    result = middle + low_back(matmul(activated, down_weight) + matmul(rank_down, exit_down))
    return jnp.where(live[:, None], result, 0.0)

def reference(tokens, cotangent, lengths, dealing, adapter_choice, attention_gain, feedforward_gain, query_weight, key_weight, value_weight, output_weight, gate_weight, up_weight, down_weight, entry_qkv, exit_query, exit_key, exit_value, entry_out, exit_out, entry_gate_up, exit_gate, exit_up, entry_down, exit_down):
    slot_length = jnp.take(lengths, dealing)
    slot_adapter = jnp.take(adapter_choice, dealing)
    frozen = tuple((weight.astype(jnp.float32) for weight in (query_weight, key_weight, value_weight, output_weight, gate_weight, up_weight, down_weight)))
    adjusted = tuple((weight.astype(jnp.float32) for weight in (entry_qkv, exit_query, exit_key, exit_value, entry_out, exit_out, entry_gate_up, exit_gate, exit_up, entry_down, exit_down)))

    def whole(inputs, adapters):

        def single(item):
            return slot_forward(item[0], item[1], item[2], attention_gain, feedforward_gain, frozen, adapters)
        return lax.map(jax.checkpoint(single), (inputs, slot_length, slot_adapter))
    mixed, pull = jax.vjp(whole, tokens.astype(jnp.float32), adjusted)
    grad_in, grad_adjusted = pull(cotangent.astype(jnp.float32))
    return (mixed.astype(jnp.bfloat16), grad_in.astype(jnp.bfloat16), grad_adjusted[0], grad_adjusted[1], grad_adjusted[2], grad_adjusted[3], grad_adjusted[4], grad_adjusted[5], grad_adjusted[6], grad_adjusted[7], grad_adjusted[8], grad_adjusted[9], grad_adjusted[10])
```

```python
import jax
import jax.numpy as jnp
from jax import lax
from jax.experimental import pallas as pl
from jax.experimental.pallas import tpu as pltpu
from jax.sharding import Mesh, PartitionSpec as P

HEAD_DIM = 96
RANK = 16
EPS = 1e-05
THETA = 100000.0
BF = jnp.bfloat16
F32 = jnp.float32

AXES = ("y", "zl", "x", "zh", "c")
SIZES = (4, 2, 4, 2, 2)
ORDERS = ("xyz", "yzx", "zxy")
ATTN, GATE_UP, DOWN = 2048, 2048, 1024
WIDTHS = (ATTN, GATE_UP, DOWN)


def device_index(y, z, x, c):
    return (((y * 2 + z % 2) * 4 + x) * 2 + z // 2) * 2 + c


def flip_pairs(axis, flips):
    pairs = []
    for y in range(4):
        for z in range(4):
            for x in range(4):
                for c in range(2):
                    at = {"x": x, "y": y, "z": z}
                    to = dict(at)
                    to[axis] ^= flips[c]
                    pairs.append(
                        (device_index(y, z, x, c), device_index(to["y"], to["z"], to["x"], c))
                    )
    return pairs


def core_swap(value):
    pairs = [(i, i ^ 1) for i in range(128)]
    return lax.ppermute(value, AXES, pairs)


class Links:
    def __init__(self, depth):
        self.depth = depth
        self.sent = {axis: [] for axis in depth}

    def __call__(self, value, axis, flips):
        sent, depth = self.sent[axis], self.depth[axis]
        if len(sent) >= depth:
            value, _ = lax.optimization_barrier((value, sent[-depth]))
        out = lax.ppermute(value, AXES, flip_pairs(axis, flips))
        sent.append(out)
        return out


def ring_stage(send, blocks, stage, forward):
    axes = [order[stage] for order in ORDERS]
    near = [send(b, a, (1, 3)) for b, a in zip(blocks, axes)]
    far = [send(b, a, (3, 1)) for b, a in zip(blocks, axes)]
    if not forward:
        across = [send(b, a, (2, 2)) for b, a in zip(blocks, axes)]
        return [[b, n, o, f] for b, n, o, f in zip(blocks, near, across, far)]
    half = blocks[0].shape[0] // 2
    low = [send(n[:half], a, (3, 1)) for n, a in zip(near, axes)]
    high = [send(f[half:], a, (1, 3)) for f, a in zip(far, axes)]
    return [[b, n, lo, hi, f] for b, n, lo, hi, f in zip(blocks, near, low, high, far)]


def place_kernel(widths, coords, *refs):
    pieces, outs, sem = refs[:15], refs[15 : 15 + len(widths)], refs[-1]
    own = {"y": coords[0], "z": coords[1], "x": coords[2]}
    core = coords[3]

    def relative(j):
        return j if j % 2 == 0 else jnp.where(core == 0, j, 4 - j)

    at = {axis: [own[axis] ^ relative(j) for j in range(4)] for axis in "xyz"}
    row = {
        "y": [v * 384 for v in at["y"]],
        "z": [lax.rem(v, 2) * 192 for v in at["z"]],
        "x": [v * 48 for v in at["x"]],
    }
    high = [lax.div(v, 2) for v in at["z"]]
    for part, order in enumerate(ORDERS):
        for q, (j3, k0, count) in enumerate(
            ((0, 0, 16), (1, 0, 16), (2, 0, 8), (2, 8, 8), (3, 0, 16))
        ):
            piece = pieces[part * 5 + q]
            for k in range(count):
                j = {order[2]: j3, order[1]: (k0 + k) // 4, order[0]: (k0 + k) % 4}
                first = row["y"][j["y"]] + row["z"][j["z"]] + row["x"][j["x"]] + part * 16
                first = pl.multiple_of(first, 16)
                start = 0
                for g, width in enumerate(widths):
                    pltpu.make_async_copy(
                        piece.at[k, :, pl.ds(start, width)],
                        outs[g].at[high[j["z"]], pl.ds(first, 16), :],
                        sem.at[g],
                    ).start()
                    start += width
    for g in range(len(widths)):
        pltpu.make_async_copy(outs[g], outs[g], sem.at[g]).wait()


def place(pieces, coords, widths):
    return pl.pallas_call(
        lambda *refs: place_kernel(widths, *refs),
        out_shape=[jax.ShapeDtypeStruct((2, 1536, w), BF) for w in widths],
        in_specs=[pl.BlockSpec(memory_space=pltpu.SMEM)]
        + [pl.BlockSpec(memory_space=pl.ANY)] * len(pieces),
        out_specs=[pl.BlockSpec(memory_space=pl.ANY)] * len(widths),
        scratch_shapes=[pltpu.SemaphoreType.DMA((len(widths),))],
    )(coords, *pieces)


def matmul(left, right):
    return jnp.dot(left, right, preferred_element_type=F32)


def inner_rows(left, right):
    return lax.dot_general(left, right, (((0,), (0,)), ((), ())), preferred_element_type=F32)


def inner_cols(left, right):
    return lax.dot_general(left, right, (((1,), (1,)), ((), ())), preferred_element_type=F32)


def lookup(table, index):
    return jnp.sum(jnp.where(jnp.arange(table.shape[0]) == index, table, 0))


def rope_tables(count_rows):
    half = HEAD_DIM // 2
    freq = jnp.power(THETA, -2.0 * jnp.arange(half, dtype=F32) / HEAD_DIM)
    angle = jnp.arange(count_rows, dtype=F32)[:, None] * freq[None, :]
    return (jnp.cos(angle), jnp.sin(angle))


def rotate(values, cosine, sine):
    half = values.shape[-1] // 2
    first = values[..., :half]
    second = values[..., half:]
    cosine = cosine[:, None, :]
    sine = sine[:, None, :]
    return jnp.concatenate(
        [first * cosine - second * sine, second * cosine + first * sine], axis=-1
    )


def rms_scale(values):
    return lax.rsqrt(jnp.mean(values * values, axis=-1, keepdims=True) + EPS)


def norm_back(inputs, scale, gain, grad):
    weighted = gain * grad
    return scale * weighted - inputs * scale**3 * jnp.mean(
        inputs * weighted, axis=-1, keepdims=True
    )


def both(parts):
    widths = [p.shape[1] for p in parts]
    sent = jnp.concatenate([p.astype(BF) for p in parts], axis=1)
    got, at, outs = core_swap(sent), 0, []
    for p, w in zip(parts, widths):
        outs.append(p + got[:, at : at + w].astype(F32))
        at += w
    return outs


def per_device(
    tokens,
    cotangent,
    lengths,
    dealing,
    adapter_choice,
    attention_gain,
    feedforward_gain,
    query_weight,
    key_weight,
    value_weight,
    output_weight,
    gate_weight,
    up_weight,
    down_weight,
    entry_qkv,
    exit_query,
    exit_key,
    exit_value,
    entry_out,
    exit_out,
    entry_gate_up,
    exit_gate,
    exit_up,
    entry_down,
    exit_down,
):
    y, zl, x, zh, core = (lax.axis_index(a) for a in AXES)
    own_high = zh == 0
    entries = jnp.concatenate([entry_qkv, entry_gate_up], axis=1)
    entries = jnp.where(own_high, entries[:, :320], entries[:, 320:])
    exits = jnp.concatenate(
        [
            exit_query,
            exit_key,
            exit_value,
            exit_gate,
            exit_up,
            entry_out.T,
            entry_down.T,
            jnp.where(own_high, exit_out, exit_down),
            jnp.zeros((4, 384), BF),
        ],
        axis=1,
    ).reshape(48, 512)
    payload = jnp.concatenate(
        [
            query_weight,
            key_weight,
            value_weight,
            output_weight.T,
            entries,
            jnp.zeros((48, 64), BF),
            exits,
            gate_weight,
            up_weight,
            down_weight.T,
        ],
        axis=1,
    )
    send = Links({"x": 2, "y": 1, "z": 2})
    blocks = [payload[None, 16 * i : 16 * i + 16] for i in range(3)]
    blocks = [jnp.concatenate(p, 0) for p in ring_stage(send, blocks, 0, False)]
    blocks = [jnp.concatenate(p, 0) for p in ring_stage(send, blocks, 1, True)]
    pieces = sum(ring_stage(send, blocks, 2, True), [])
    coords = jnp.stack([y, zh * 2 + zl, x, core]).astype(jnp.int32)
    attn_w, gate_up_w, down_w = place(pieces, coords, WIDTHS)

    slot = ((y * 2 + zl) * 4 + x) * 2 + zh
    sequence = lookup(dealing, slot)
    length = lookup(lengths, sequence)
    chosen = lookup(adapter_choice, sequence)
    rows = lax.dynamic_index_in_dim(tokens, zh, 0, keepdims=False)
    cot = lax.dynamic_index_in_dim(cotangent, zh, 0, keepdims=False)
    count = rows.shape[0]

    def own16(wide, parts):
        return jnp.concatenate(
            [
                lax.dynamic_slice_in_dim(wide[:, i * 128 : i * 128 + 128], chosen * RANK, RANK, 1)
                for i in range(parts)
            ],
            axis=1,
        )

    qkv_w = [attn_w[h, :, :768] for h in range(2)]
    out_w = [attn_w[h, :, 768:1152] for h in range(2)]
    gate_w = [gate_up_w[h, :, :1024] for h in range(2)]
    up_w = [gate_up_w[h, :, 1024:] for h in range(2)]
    entry = jnp.concatenate([attn_w[0, :, 1152:1472], attn_w[1, :, 1152:1472]], axis=1)
    entry_a = own16(entry, 5)
    ent_qkv, ent_gu = entry_a[:, :48], entry_a[:, 48:]
    mine = lax.dynamic_slice(attn_w, (0, chosen * 192, 1536), (2, 192, 512)).reshape(2, RANK, 6144)
    x_q = [mine[h, :, :384] for h in range(2)]
    x_k = [mine[h, :, 384:576] for h in range(2)]
    x_v = [mine[h, :, 576:768] for h in range(2)]
    x_gate = [mine[h, :, 768:1792] for h in range(2)]
    x_up = [mine[h, :, 1792:2816] for h in range(2)]
    e_out = [mine[h, :, 2816:3200] for h in range(2)]
    e_down = [mine[h, :, 3200:4224] for h in range(2)]
    x_out, x_down = mine[0, :, 4224:5760], mine[1, :, 4224:5760]

    positions = jnp.arange(count)
    live = positions < length
    allowed = (positions[None, :] <= positions[:, None]) & live[None, :]
    inputs = rows.astype(F32)
    scale_attn = rms_scale(inputs)
    normed = (inputs * scale_attn * attention_gain).astype(BF)
    rank_qkv = matmul(normed, ent_qkv).astype(BF)
    r_q, r_k, r_v = rank_qkv[:, :16], rank_qkv[:, 16:32], rank_qkv[:, 32:]
    q_parts, k_parts, v_parts = [], [], []
    for h in range(2):
        qkv = matmul(normed, qkv_w[h])
        q_parts.append(qkv[:, :384] + matmul(r_q, x_q[h]))
        k_parts.append(qkv[:, 384:576] + matmul(r_k, x_k[h]))
        v_parts.append(qkv[:, 576:] + matmul(r_v, x_v[h]))
    cosine, sine = rope_tables(count)

    def heads(parts):
        return jnp.concatenate(parts, axis=1).reshape(count, -1, HEAD_DIM)

    queries = rotate(heads(q_parts), cosine, sine).astype(BF)
    keys = rotate(heads(k_parts), cosine, sine).astype(BF)
    values = heads(v_parts).astype(BF)
    kv = keys.shape[1]
    grouped = queries.reshape(count, kv, -1, HEAD_DIM)
    factor = HEAD_DIM ** (-0.5)
    raw = jnp.einsum("qjgd,kjd->jgqk", grouped, keys, preferred_element_type=F32)
    scores = jnp.where(allowed, raw * factor, -1e30)
    top = jnp.max(scores, axis=-1, keepdims=True)
    expd = jnp.exp(scores - top)
    probs = expd / jnp.sum(expd, axis=-1, keepdims=True)
    probs16 = probs.astype(BF)
    attended = jnp.einsum("jgqk,kjd->qjgd", probs16, values, preferred_element_type=F32)
    attended = attended.reshape(count, -1).astype(BF)
    att = [attended[:, :384], attended[:, 384:]]
    projected, rank_part = both(
        [
            inner_cols(att[0], out_w[0]) + inner_cols(att[1], out_w[1]),
            inner_cols(att[0], e_out[0]) + inner_cols(att[1], e_out[1]),
        ]
    )
    rank_out = rank_part.astype(BF)
    middle = inputs + projected + matmul(rank_out, x_out)
    scale_mlp = rms_scale(middle)
    hidden_in = (middle * scale_mlp * feedforward_gain).astype(BF)
    rank_gu = matmul(hidden_in, ent_gu).astype(BF)
    r_gate, r_up = rank_gu[:, :16], rank_gu[:, 16:]

    grad_out = jnp.where(live[:, None], cot.astype(F32), 0.0)
    g2 = grad_out.astype(BF)
    drank_down = inner_cols(g2, x_down).astype(BF)
    act, g_gate, g_up = [], [], []
    for h in range(2):
        gate = matmul(hidden_in, gate_w[h]) + matmul(r_gate, x_gate[h])
        up = matmul(hidden_in, up_w[h]) + matmul(r_up, x_up[h])
        sigma = jax.nn.sigmoid(gate)
        act.append((gate * sigma * up).astype(BF))
        grad_act = matmul(g2, down_w[h]) + matmul(drank_down, e_down[h])
        g_up.append((grad_act * gate * sigma).astype(BF))
        g_gate.append((grad_act * up * sigma * (1.0 + gate * (1.0 - sigma))).astype(BF))
    reduced, rank_part = both(
        [
            inner_cols(act[0], down_w[0]) + inner_cols(act[1], down_w[1]),
            inner_cols(act[0], e_down[0]) + inner_cols(act[1], e_down[1]),
        ]
    )
    rank_down = rank_part.astype(BF)
    result = middle + reduced + matmul(rank_down, x_down)
    mixed = jnp.where(live[:, None], result, 0.0).astype(BF)

    grad_hidden, drank_gate, drank_up = both(
        [
            sum(inner_cols(g_gate[h], gate_w[h]) + inner_cols(g_up[h], up_w[h]) for h in range(2)),
            sum(inner_cols(g_gate[h], x_gate[h]) for h in range(2)),
            sum(inner_cols(g_up[h], x_up[h]) for h in range(2)),
        ]
    )
    drank_gu = jnp.concatenate([drank_gate, drank_up], axis=1).astype(BF)
    grad_hidden = grad_hidden + inner_cols(drank_gu, ent_gu)
    grad_middle = grad_out + norm_back(middle, scale_mlp, feedforward_gain, grad_hidden)
    g1 = grad_middle.astype(BF)
    drank_out = inner_cols(g1, x_out).astype(BF)
    grad_att = [(matmul(g1, out_w[h]) + matmul(drank_out, e_out[h])).astype(BF) for h in range(2)]
    g_grouped = jnp.concatenate(grad_att, axis=1).reshape(count, kv, -1, HEAD_DIM)
    grad_probs = jnp.einsum("qjgd,kjd->jgqk", g_grouped, values, preferred_element_type=F32)
    delta = jnp.sum(probs * grad_probs, axis=-1, keepdims=True)
    grad_scores = (probs * (grad_probs - delta)).astype(BF)
    g_rq = jnp.einsum("jgqk,kjd->qjgd", grad_scores, keys, preferred_element_type=F32) * factor
    g_rk = jnp.einsum("jgqk,qjgd->kjd", grad_scores, grouped, preferred_element_type=F32) * factor
    g_v = jnp.einsum("jgqk,qjgd->kjd", probs16, g_grouped, preferred_element_type=F32)
    g_q = rotate(g_rq.reshape(count, -1, HEAD_DIM), cosine, -sine).reshape(count, -1).astype(BF)
    g_k = rotate(g_rk, cosine, -sine).reshape(count, -1).astype(BF)
    g_v = g_v.reshape(count, -1).astype(BF)
    gq = [g_q[:, :384], g_q[:, 384:]]
    gk = [g_k[:, :192], g_k[:, 192:]]
    gv = [g_v[:, :192], g_v[:, 192:]]
    gqkv = [jnp.concatenate([gq[h], gk[h], gv[h]], axis=1) for h in range(2)]
    grad_normed, d_q, d_k, d_v = both(
        [
            inner_cols(gqkv[0], qkv_w[0]) + inner_cols(gqkv[1], qkv_w[1]),
            inner_cols(gq[0], x_q[0]) + inner_cols(gq[1], x_q[1]),
            inner_cols(gk[0], x_k[0]) + inner_cols(gk[1], x_k[1]),
            inner_cols(gv[0], x_v[0]) + inner_cols(gv[1], x_v[1]),
        ]
    )
    drank_qkv = jnp.concatenate([d_q, d_k, d_v], axis=1).astype(BF)
    grad_normed = grad_normed + inner_cols(drank_qkv, ent_qkv)
    grad_in = grad_middle + norm_back(inputs, scale_attn, attention_gain, grad_normed)
    grad_in = grad_in.astype(BF)

    columns = jnp.stack(
        [
            jnp.concatenate(
                [
                    inner_rows(r_q, gq[h]),
                    inner_rows(r_k, gk[h]),
                    inner_rows(r_v, gv[h]),
                    inner_rows(r_gate, g_gate[h]),
                    inner_rows(r_up, g_up[h]),
                    inner_rows(drank_out, att[h]),
                    inner_rows(drank_down, act[h]),
                ],
                axis=1,
            )
            for h in range(2)
        ]
    ).astype(BF)
    shared = jnp.concatenate([inner_rows(rank_out, g1), inner_rows(rank_down, g2)], axis=1)
    shared = shared.astype(BF)
    wide = jnp.concatenate(
        [
            inner_rows(normed, drank_qkv),
            inner_rows(hidden_in, drank_gu),
            jnp.zeros((1536, 48), F32),
        ],
        axis=1,
    ).astype(BF)
    lines = jnp.concatenate(
        [
            columns.reshape(2, 4, 132, 128),
            jnp.broadcast_to(shared.reshape(1, 4, 96, 128), (2, 4, 96, 128)),
            jnp.broadcast_to(
                wide.reshape(8, 4, 48, 128).transpose(1, 0, 2, 3).reshape(1, 4, 384, 128),
                (2, 4, 384, 128),
            ),
        ],
        axis=2,
    ).reshape(8, 612, 128)
    got = lax.all_to_all(lines, ("zh", "x"), 0, 0, tiled=True)
    peers = ((y * 2 + zl) * 4 + jnp.tile(jnp.arange(4), 2)) * 2 + jnp.repeat(jnp.arange(2), 4)
    match = (jnp.arange(64)[None, :] == peers[:, None]).astype(jnp.int32)
    peer_seq = jnp.sum(match * dealing[None, :], axis=1)
    match = (jnp.arange(64)[None, :] == peer_seq[:, None]).astype(jnp.int32)
    peer_adapter = jnp.sum(match * adapter_choice[None, :], axis=1)
    one_hot = (jnp.arange(8)[:, None] == peer_adapter[None, :]).astype(BF)
    summed = jnp.einsum("as,slk->alk", one_hot, got, preferred_element_type=F32).astype(BF)
    second = jnp.concatenate(
        [
            summed[:, :228],
            summed[:, 228:].reshape(8, 8, 48, 128).transpose(1, 0, 2, 3).reshape(8, 384, 128),
        ],
        axis=1,
    )
    final = lax.all_to_all(second, ("y", "zl"), 0, 0, tiled=True)
    final = jnp.sum(final.astype(F32), axis=0)
    cols = final[:132].reshape(4, 4224)
    shared = final[132:228].reshape(4, 3072)
    wide = final[228:].reshape(8, 48, 128).transpose(1, 2, 0)
    wide_qkv = wide[:, :48].reshape(48, 3, 16, 8).transpose(0, 1, 3, 2).reshape(48, 384)
    wide_gu = wide[:, 48:80].reshape(48, 2, 16, 8).transpose(0, 1, 3, 2).reshape(48, 256)

    def share(value):
        other = lax.ppermute(value, AXES, flip_pairs("z", (2, 2)))
        return jnp.stack([jnp.where(own_high, value, other), jnp.where(own_high, other, value)])

    return (
        share(mixed),
        share(grad_in),
        wide_qkv,
        cols[:, :384],
        cols[:, 384:576],
        cols[:, 576:768],
        cols[:, 2816:3200].T,
        shared[:, :1536],
        wide_gu,
        cols[:, 768:1792],
        cols[:, 1792:2816],
        cols[:, 3200:].T,
        shared[:, 1536:],
    )


def solution(mesh):
    fine = Mesh(mesh.devices.reshape(SIZES), AXES)
    dp, mp = ("y", "zl", "x"), ("zh", "c")
    return jax.shard_map(
        per_device,
        mesh=fine,
        in_specs=(
            P(dp, None, None),
            P(dp, None, None),
            P(),
            P(),
            P(),
            P(),
            P(),
            P(dp, mp),
            P(dp, mp),
            P(dp, mp),
            P(mp, dp),
            P(dp, mp),
            P(dp, mp),
            P(mp, dp),
            P(dp, None),
            P(dp, mp),
            P(dp, mp),
            P(dp, mp),
            P(mp, dp),
            P(dp, None),
            P(dp, None),
            P(dp, mp),
            P(dp, mp),
            P(mp, dp),
            P(dp, None),
        ),
        out_specs=(
            P(dp, None, None),
            P(dp, None, None),
            P(dp, None),
            P(dp, mp),
            P(dp, mp),
            P(dp, mp),
            P(mp, dp),
            P(dp, None),
            P(dp, None),
            P(dp, mp),
            P(dp, mp),
            P(mp, dp),
            P(dp, None),
        ),
        check_vma=False,
    )
```

```python
import jax
import jax.numpy as jnp
from jax import lax
from jax.experimental import pallas as pl
from jax.experimental.pallas import tpu as pltpu
from jax.sharding import Mesh, PartitionSpec as P

HEAD_DIM = 96
RANK = 16
EPS = 1e-05
THETA = 100000.0
BF = jnp.bfloat16
F32 = jnp.float32

AXES = ("y", "zl", "x", "zh", "c")
SIZES = (4, 2, 4, 2, 2)
PARTS = (
    (0, 32, (("z", "y"), ("y", "x"), ("x", "z")), ((1, 1), (3, 3))),
    (32, 16, (("x", "x"), ("z", "z"), ("y", "y")), ((1, 3), (3, 1))),
)
ATTN, GATE_UP, DOWN = 2048, 2048, 1024
WIDTHS = (ATTN, GATE_UP, DOWN)
DEPTH = (3, 2)


def device_index(y, z, x, c):
    return (((y * 2 + z % 2) * 4 + x) * 2 + z // 2) * 2 + c


def flip_pairs(axes, flips):
    pairs = []
    for y in range(4):
        for z in range(4):
            for x in range(4):
                for c in range(2):
                    to = {"x": x, "y": y, "z": z}
                    to[axes[c]] ^= flips[c]
                    pairs.append(
                        (device_index(y, z, x, c), device_index(to["y"], to["z"], to["x"], c))
                    )
    return pairs


def core_swap(value):
    pairs = [(i, i ^ 1) for i in range(128)]
    return lax.ppermute(value, AXES, pairs)


class Links:
    def __init__(self, depth):
        self.depth = depth
        self.sent = [[] for _ in depth]

    def __call__(self, part, value, axes, flips):
        sent, depth = self.sent[part], self.depth[part]
        if len(sent) >= depth:
            value, _ = lax.optimization_barrier((value, sent[-depth]))
        out = lax.ppermute(value, AXES, flip_pairs(axes, flips))
        sent.append(out)
        return out


def ring_stage(send, blocks, stage, forward):
    outs = []
    every = range(len(blocks))
    axes = [PARTS[p][2][stage] for p in every]
    steps = [PARTS[p][3] for p in every]
    near = [send(p, blocks[p], axes[p], steps[p][0]) for p in every]
    far = [send(p, blocks[p], axes[p], steps[p][1]) for p in every]
    if not forward:
        across = [send(p, blocks[p], axes[p], (2, 2)) for p in every]
        return [[blocks[p], near[p], across[p], far[p]] for p in every]
    half = blocks[0].shape[0] // 2
    low = [send(p, near[p][:half], axes[p], steps[p][1]) for p in every]
    high = [send(p, far[p][half:], axes[p], steps[p][0]) for p in every]
    return [[blocks[p], near[p], low[p], high[p], far[p]] for p in every]


def fetch(coords, pieces, out, sem):
    own = {"y": coords[0], "z": coords[1], "x": coords[2]}
    core = coords[3]

    def choose(first, second):
        return jnp.where(core == 0, first, second)

    def row(axis, j):
        at = own[axis] ^ j
        if axis == "z":
            return lax.rem(at, 2) * 192
        return at * (384 if axis == "y" else 48)

    for part, (start, count, axes, steps) in enumerate(PARTS):
        rows, highs = [], []
        for axis in axes:
            swapped = steps[0][1] == 3
            far = [(j, (4 - j) % 4 if swapped else j) for j in range(4)]
            rows.append([choose(row(axis[0], u), row(axis[1], v)) for u, v in far])
            highs.append(
                [
                    choose(
                        lax.div(own["z"] ^ u, 2) if axis[0] == "z" else 0,
                        lax.div(own["z"] ^ v, 2) if axis[1] == "z" else 0,
                    )
                    for u, v in far
                ]
            )
        for q, (j3, k0, many) in enumerate(
            ((0, 0, 16), (1, 0, 16), (2, 0, 8), (2, 8, 8), (3, 0, 16))
        ):
            for k in range(many):
                j2, j1 = (k0 + k) // 4, (k0 + k) % 4
                first = rows[0][j1] + rows[1][j2] + rows[2][j3] + start
                high = highs[0][j1] + highs[1][j2] + highs[2][j3]
                pltpu.make_async_copy(
                    pieces[part * 5 + q].at[k],
                    out.at[high, pl.ds(pl.multiple_of(first, 16), count), :],
                    sem,
                ).start()


def place_kernel(coords, *refs):
    pieces, out, sem = refs[:10], refs[10], refs[11]
    fetch(coords, pieces, out, sem)
    pltpu.make_async_copy(out, out, sem).wait()


def place(pieces, coords, width):
    return pl.pallas_call(
        place_kernel,
        out_shape=jax.ShapeDtypeStruct((2, 1536, width), BF),
        in_specs=[pl.BlockSpec(memory_space=pltpu.SMEM)]
        + [pl.BlockSpec(memory_space=pl.ANY)] * len(pieces),
        out_specs=pl.BlockSpec(memory_space=pltpu.VMEM),
        scratch_shapes=[pltpu.SemaphoreType.DMA(())],
        compiler_params=pltpu.CompilerParams(vmem_limit_bytes=20 << 20),
        cost_estimate=pl.CostEstimate(
            flops=0, transcendentals=0, bytes_accessed=2 * 2 * 2 * 1536 * width
        ),
    )(coords, *pieces)


def ones_where(condition):
    return jnp.where(condition, 1.0, 0.0).astype(BF)


def iota2(rows, cols):
    return (
        lax.broadcasted_iota(jnp.int32, (rows, cols), 0),
        lax.broadcasted_iota(jnp.int32, (rows, cols), 1),
    )


def attention_weights(coords, *refs):
    pieces = refs[:10]
    w_qkv, w_out, ent_qkv, ent_gu, x_qkv, x_gu, e_out, e_down, x_od = refs[10:19]
    raw, sem = refs[19:]
    fetch(coords, pieces, raw, sem)
    chosen = coords[4]
    i, j = iota2(384, 512)
    spread = ones_where(j == i + 16 * lax.div(i, 48))
    i, j = iota2(384, 128)
    picks = []
    for h in range(2):
        col = i + 320 * h
        third, rank = lax.div(col, 128), lax.rem(col, 16)
        ours = (lax.div(lax.rem(col, 128), 16) == chosen) & (i < 320)
        picks.append(
            (
                ones_where(ours & (third < 3) & (j == third * 16 + rank)),
                ones_where(ours & (third >= 3) & (j == (third - 3) * 16 + rank)),
            )
        )
    pltpu.make_async_copy(raw, raw, sem).wait()

    @pl.loop(0, 3)
    def _(n):
        rows = pl.ds(pl.multiple_of(n * 512, 512), 512)
        for h in range(2):
            for b in range(2):
                w_qkv[h, rows, b * 512 : b * 512 + 512] = matmul(
                    raw[h, rows, b * 384 : b * 384 + 384], spread
                ).astype(BF)
            w_out[h, rows, :] = matmul(raw[h, rows, 768:1152], spread).astype(BF)
        for out, which in ((ent_qkv, 0), (ent_gu, 1)):
            out[rows, :] = sum(
                matmul(raw[h, rows, 1152:1536], picks[h][which]) for h in range(2)
            ).astype(BF)

    i, j = iota2(128, 192)
    lane = lax.broadcasted_iota(jnp.int32, (128, 512), 1)
    mine = pl.ds(pl.multiple_of(chosen * 192, 16), 192)

    for h in range(2):
        block = raw[h, mine, 1536:2048]

        def line(t, first):
            take = ones_where((j == 12 * (i - first) + t) & (i >= first) & (i < first + 16))
            return matmul(take, block).astype(BF)

        for t in range(2):
            x_gu[h, :, t * 512 : t * 512 + 512] = line(t, 0)
            x_gu[h, :, 1024 + t * 512 : 1536 + t * 512] = line(2 + t, 16)
            e_down[h, :, t * 512 : t * 512 + 512] = line(4 + t, 0)
        for t in range(3):
            x_od[h, :, t * 512 : t * 512 + 512] = line(6 + t, 0)
        x_qkv[h, :, :512] = matmul(line(9, 0)[:, :384], spread).astype(BF)
        key = matmul(line(10, 16)[:, :384], spread)
        value = matmul(line(10, 32)[:, :384], spread)
        x_qkv[h, :, 512:] = jnp.where(lane < 256, key, value).astype(BF)
        e_out[h] = matmul(line(11, 0)[:, :384], spread).astype(BF)


def place_attention(pieces, coords):
    outs = (
        shaped(2, WIDE, 1024),
        shaped(2, WIDE, 512),
        shaped(WIDE, LANES),
        shaped(WIDE, LANES),
        shaped(2, LANES, 1024),
        shaped(2, LANES, 2048),
        shaped(2, LANES, 512),
        shaped(2, LANES, 1024),
        shaped(2, LANES, WIDE),
    )
    return pl.pallas_call(
        attention_weights,
        out_shape=list(outs),
        in_specs=[pl.BlockSpec(memory_space=pltpu.SMEM)]
        + [pl.BlockSpec(memory_space=pl.ANY)] * len(pieces),
        out_specs=[pl.BlockSpec(memory_space=pltpu.VMEM)] * len(outs),
        scratch_shapes=[pltpu.VMEM((2, WIDE, ATTN), BF), pltpu.SemaphoreType.DMA(())],
        compiler_params=pltpu.CompilerParams(vmem_limit_bytes=44 << 20),
        cost_estimate=pl.CostEstimate(flops=6 * 10**9, transcendentals=0, bytes_accessed=24 << 20),
    )(coords, *pieces)


def matmul(left, right):
    return jnp.dot(left, right, preferred_element_type=F32)


def inner_rows(left, right):
    return lax.dot_general(left, right, (((0,), (0,)), ((), ())), preferred_element_type=F32)


def inner_cols(left, right):
    return lax.dot_general(left, right, (((1,), (1,)), ((), ())), preferred_element_type=F32)


ROWS = 384
WIDE = 1536
LANES = 128
PART = WIDE + LANES
FACTOR = HEAD_DIM ** (-0.5)


def row_blocks(body):
    @pl.loop(0, ROWS // 128)
    def _(i):
        body(pl.ds(pl.multiple_of(i * 128, 128), 128))


def row_scale(values):
    return lax.rsqrt(jnp.mean(values * values, axis=-1, keepdims=True) + EPS)


def back_of_norm(inputs, gain, grad):
    scale = row_scale(inputs)
    weighted = gain * grad
    return scale * weighted - inputs * (
        scale * scale * scale * jnp.mean(inputs * weighted, axis=-1, keepdims=True)
    )


def live_rows(length, rows):
    at = lax.broadcasted_iota(jnp.int32, (128, 1), 0) + rows.start
    return at < length


def spin(values, cosine, sine):
    return values * cosine + pltpu.roll(values, 64, 1) * sine


def project_cols(out, parts, rank_parts):
    @pl.loop(0, WIDE // 256)
    def _(n):
        cols = pl.ds(pl.multiple_of(n * 256, 256), 256)
        out[:, cols] = sum(inner_cols(left(), right(cols)) for left, right in parts).astype(BF)

    out[:, WIDE:] = sum(inner_cols(left(), right()) for left, right in rank_parts).astype(BF)


def attention_forward(
    scalars, tok, gain, ent, exits, entry_o, cosine, sine, w, ot,
    normed, ranks, q, k, v, probs, att, part,
):
    def start(rows):
        x = tok[rows, :].astype(F32)
        normed[rows, :] = (x * row_scale(x) * gain[...]).astype(BF)

    row_blocks(start)
    ranks[...] = matmul(normed[...], ent[...]).astype(BF)
    for h in range(2):
        for n in range(4):
            cols = slice(n * 256, n * 256 + 256)
            t = matmul(normed[...], w[h, :, cols]) + matmul(ranks[...], exits[h, :, cols])
            for i in range(2):
                head = t[:, i * 128 : i * 128 + 128]
                if n < 2:
                    q[h * 4 + n * 2 + i] = spin(head, cosine[...], sine[...]).astype(BF)
                elif n == 2:
                    k[h * 2 + i] = spin(head, cosine[...], sine[...]).astype(BF)
                else:
                    v[h * 2 + i] = head.astype(BF)
    length = scalars[0]
    at_q = lax.broadcasted_iota(jnp.int32, (ROWS, ROWS), 0)
    at_k = lax.broadcasted_iota(jnp.int32, (ROWS, ROWS), 1)
    allowed = (at_k <= at_q) & (at_k < length)
    for h in range(2):

        @pl.loop(0, 4)
        def _(i):
            g = h * 2 + i // 2
            s = inner_cols(q[h * 4 + i], k[g]) * FACTOR
            s = jnp.where(allowed, s, -1e30)
            e = jnp.exp(s - jnp.max(s, axis=-1, keepdims=True))
            p = e / jnp.sum(e, axis=-1, keepdims=True)
            probs[h * 4 + i] = p
            att[h, :, pl.ds(pl.multiple_of(i * 128, 128), 128)] = matmul(p.astype(BF), v[g]).astype(BF)

    project_cols(
        part,
        [(lambda h=h: att[h], lambda cols, h=h: ot[h, cols, :]) for h in range(2)],
        [(lambda h=h: att[h], lambda h=h: entry_o[h]) for h in range(2)],
    )


def mlp_forward(
    tok, own, other, gain, exit_o, ent, exits, w,
    middle, rank_out, hidden, ranks, slope_up, slope_gate, act,
):
    def start(rows):
        total = own[rows, :].astype(F32) + other[rows, :].astype(F32)
        r = total[:, WIDE:].astype(BF)
        rank_out[rows, :] = r
        mid = tok[rows, :].astype(F32) + total[:, :WIDE] + matmul(r, exit_o[...])
        middle[rows, :] = mid
        hidden[rows, :] = (mid * row_scale(mid) * gain[...]).astype(BF)

    row_blocks(start)
    ranks[...] = matmul(hidden[...], ent[...]).astype(BF)
    for h in range(2):

        @pl.loop(0, 4)
        def _(n):
            cols = pl.ds(pl.multiple_of(n * 256, 256), 256)
            ups = pl.ds(pl.multiple_of(n * 256 + 1024, 256), 256)
            gate = matmul(hidden[...], w[h, :, cols]) + matmul(ranks[...], exits[h, :, cols])
            up = matmul(hidden[...], w[h, :, ups]) + matmul(ranks[...], exits[h, :, ups])
            sigma = 1.0 / (1.0 + jnp.exp(-gate))
            silu = gate * sigma
            act[h, :, cols] = (silu * up).astype(BF)
            slope_up[h, :, cols] = silu.astype(BF)
            slope_gate[h, :, cols] = (up * sigma * (1.0 + gate * (1.0 - sigma))).astype(BF)


def mlp_backward(
    scalars, cot, exit_d, entry_d, exits, slope_up, slope_gate, down, w,
    g2, drank, grads, part,
):
    def start(rows):
        g2[rows, :] = jnp.where(live_rows(scalars[0], rows), cot[rows, :].astype(F32), 0.0).astype(BF)

    row_blocks(start)
    drank[...] = inner_cols(g2[...], exit_d[...]).astype(BF)
    for h in range(2):

        @pl.loop(0, 4)
        def _(n):
            cols = pl.ds(pl.multiple_of(n * 256, 256), 256)
            ups = pl.ds(pl.multiple_of(n * 256 + 1024, 256), 256)
            grad = matmul(g2[...], down[h, :, cols]) + matmul(drank[...], entry_d[h, :, cols])
            grads[h, :, cols] = (grad * slope_gate[h, :, cols].astype(F32)).astype(BF)
            grads[h, :, ups] = (grad * slope_up[h, :, cols].astype(F32)).astype(BF)

    project_cols(
        part,
        [(lambda h=h: grads[h], lambda cols, h=h: w[h, cols, :]) for h in range(2)],
        [(lambda h=h: grads[h], lambda h=h: exits[h]) for h in range(2)],
    )


def mlp_finish(act, entry_d, ranks, grads, drank, down, part, exit_grads, entry_grads):
    project_cols(
        part,
        [(lambda h=h: act[h], lambda cols, h=h: down[h, cols, :]) for h in range(2)],
        [(lambda h=h: act[h], lambda h=h: entry_d[h]) for h in range(2)],
    )
    for h in range(2):
        exit_grads[h] = inner_rows(ranks[...], grads[h])[:32].astype(BF)
        entry_grads[h] = inner_rows(drank[...], act[h])[:16].astype(BF)


def attention_backward(
    cot, own, other, middle, gain, ent, exit_o, entry_o, exits, cosine, sine, q, k, v, probs, scalars, ot, w,
    grad_middle, g1, drank_gu, drank_out, grads, part,
    grad_att, sum_k, sum_v,
):
    def start(rows):
        total = own[rows, :].astype(F32) + other[rows, :].astype(F32)
        d = total[:, WIDE:].astype(BF)
        drank_gu[rows, :] = d
        hidden = total[:, :WIDE] + inner_cols(d, ent[...])
        out = jnp.where(live_rows(scalars[0], rows), cot[rows, :].astype(F32), 0.0)
        mid = out + back_of_norm(middle[rows, :], gain[...], hidden)
        grad_middle[rows, :] = mid
        g1[rows, :] = mid.astype(BF)

    row_blocks(start)
    drank_out[...] = inner_cols(g1[...], exit_o[...]).astype(BF)
    for h in range(2):
        for n in range(2):
            cols = slice(n * 256, n * 256 + 256)
            t = matmul(g1[...], ot[h, :, cols]) + matmul(drank_out[...], entry_o[h, :, cols])
            for i in range(2):
                grad_att[h * 4 + n * 2 + i] = t[:, i * 128 : i * 128 + 128].astype(BF)
    for h in range(2):

        @pl.loop(0, 2)
        def _(j):
            g = h * 2 + j
            for i in range(2):
                head = h * 4 + j * 2 + i
                p = probs[head]
                ga = grad_att[head]
                gp = inner_cols(ga, v[g])
                delta = jnp.sum(p * gp, axis=-1, keepdims=True)
                gs = (p * (gp - delta)).astype(BF)
                gq = matmul(gs, k[g]) * FACTOR
                grads[h, :, pl.ds(pl.multiple_of((j * 2 + i) * 128, 128), 128)] = spin(
                    gq, cosine[...], -sine[...]
                ).astype(BF)
                gk = inner_rows(gs, q[head])
                gv = inner_rows(p.astype(BF), ga)
                if i == 0:
                    sum_k[...] = gk
                    sum_v[...] = gv
                else:
                    gk = (sum_k[...] + gk) * FACTOR
                    gv = sum_v[...] + gv
                    grads[h, :, pl.ds(pl.multiple_of(512 + j * 128, 128), 128)] = spin(
                        gk, cosine[...], -sine[...]
                    ).astype(BF)
                    grads[h, :, pl.ds(pl.multiple_of(768 + j * 128, 128), 128)] = gv.astype(BF)

    project_cols(
        part,
        [(lambda h=h: grads[h], lambda cols, h=h: w[h, cols, :]) for h in range(2)],
        [(lambda h=h: grads[h], lambda h=h: exits[h]) for h in range(2)],
    )


def middle_finish(
    scalars, middle, own, other, exit_d, g2, g1, rank_out, hidden, drank_gu, ranks, grads, drank_out, att,
    mixed, exit_grads, entry_grads, shared, wide,
    rank_down,
):
    def start(rows):
        total = own[rows, :].astype(F32) + other[rows, :].astype(F32)
        r = total[:, WIDE:].astype(BF)
        rank_down[rows, :] = r
        result = middle[rows, :] + total[:, :WIDE] + matmul(r, exit_d[...])
        mixed[rows, :] = jnp.where(live_rows(scalars[0], rows), result, 0.0).astype(BF)

    row_blocks(start)
    for h in range(2):
        exit_grads[h] = inner_rows(ranks[...], grads[h])[:48].astype(BF)
        entry_grads[h] = inner_rows(drank_out[...], att[h])[:16].astype(BF)
    shared[0] = inner_rows(rank_out[...], g1[...])[:16].astype(BF)
    shared[1] = inner_rows(rank_down[...], g2[...])[:16].astype(BF)
    wide[...] = inner_rows(drank_gu[...], hidden[...])[:32].astype(BF)


def input_backward(
    tok, own, other, grad_middle, gain, ent, normed,
    grad_in, wide,
    drank,
):
    def start(rows):
        total = own[rows, :].astype(F32) + other[rows, :].astype(F32)
        d = total[:, WIDE:].astype(BF)
        drank[rows, :] = d
        grad = total[:, :WIDE] + inner_cols(d, ent[...])
        back = back_of_norm(tok[rows, :].astype(F32), gain[...], grad)
        grad_in[rows, :] = (grad_middle[rows, :] + back).astype(BF)

    row_blocks(start)
    wide[...] = inner_rows(drank[...], normed[...])[:48].astype(BF)


def shaped(*extent, dtype=BF):
    return jax.ShapeDtypeStruct(extent, dtype)


def call(body, args, outs, flops, megabytes, scratch=(), scalars=()):
    whole = pl.BlockSpec(memory_space=pltpu.VMEM)
    small = pl.BlockSpec(memory_space=pltpu.SMEM)
    return pl.pallas_call(
        body,
        out_shape=list(outs),
        in_specs=[small if i in scalars else whole for i in range(len(args))],
        out_specs=[whole] * len(outs),
        scratch_shapes=list(scratch),
        compiler_params=pltpu.CompilerParams(vmem_limit_bytes=megabytes << 20),
        cost_estimate=pl.CostEstimate(
            flops=int(flops),
            transcendentals=0,
            bytes_accessed=sum(a.size * a.dtype.itemsize for a in args),
        ),
    )(*args)


def lookup(table, index):
    return jnp.sum(jnp.where(jnp.arange(table.shape[0]) == index, table, 0))


def rope_tables():
    half = HEAD_DIM // 2
    freq = jnp.power(THETA, -2.0 * jnp.arange(half, dtype=F32) / HEAD_DIM)
    angle = jnp.arange(ROWS, dtype=F32)[:, None] * freq[None, :]
    cosine, sine, pad = jnp.cos(angle), jnp.sin(angle), jnp.zeros((ROWS, 16), F32)
    return (
        jnp.concatenate([cosine, pad, cosine, pad], axis=1),
        jnp.concatenate([-sine, pad, sine, pad], axis=1),
    )


def cut_heads(array):
    lead = array.shape[:-1]
    return array.reshape(*lead, -1, 64)[..., :48].reshape(*lead, -1)


def per_device(
    tokens,
    cotangent,
    lengths,
    dealing,
    adapter_choice,
    attention_gain,
    feedforward_gain,
    query_weight,
    key_weight,
    value_weight,
    output_weight,
    gate_weight,
    up_weight,
    down_weight,
    entry_qkv,
    exit_query,
    exit_key,
    exit_value,
    entry_out,
    exit_out,
    entry_gate_up,
    exit_gate,
    exit_up,
    entry_down,
    exit_down,
):
    y, zl, x, zh, core = (lax.axis_index(a) for a in AXES)
    own_high = zh == 0
    entries = jnp.concatenate([entry_qkv, entry_gate_up], axis=1)
    entries = jnp.where(own_high, entries[:, :320], entries[:, 320:])
    pad = jnp.zeros((4, 128), BF)
    exits = jnp.concatenate(
        [
            exit_gate,
            exit_up,
            entry_down.T,
            jnp.where(own_high, exit_out, exit_down),
            exit_query,
            pad,
            exit_key,
            exit_value,
            pad,
            entry_out.T,
            pad,
        ],
        axis=1,
    ).reshape(48, 512)
    payload = jnp.concatenate(
        [
            query_weight,
            key_weight,
            value_weight,
            output_weight.T,
            entries,
            jnp.zeros((48, 64), BF),
            exits,
            gate_weight,
            up_weight,
            down_weight.T,
        ],
        axis=1,
    )
    slot = ((y * 2 + zl) * 4 + x) * 2 + zh
    sequence = lookup(dealing, slot)
    length = lookup(lengths, sequence)
    chosen = lookup(adapter_choice, sequence)
    coords = jnp.stack([y, zh * 2 + zl, x, core, chosen]).astype(jnp.int32)

    send = Links(DEPTH)
    blocks = [payload[None, first : first + count] for first, count, _, _ in PARTS]
    blocks = [jnp.concatenate(p, 0) for p in ring_stage(send, blocks, 0, False)]
    second = ring_stage(send, blocks, 1, True)
    groups, start = [], 0
    for width in WIDTHS:
        group = [
            jnp.concatenate([q[:, :, start : start + width] for q in p], 0) for p in second
        ]
        groups.append(sum(ring_stage(send, group, 2, True), []))
        start += width
    w_qkv, w_out, ent_qkv, ent_gu, x_qkv, x_gu, e_out, e_down, x_od = place_attention(
        groups[0], coords
    )
    gate_up_w = place(groups[1], coords, WIDTHS[1])
    down_w = place(groups[2], coords, WIDTHS[2])
    x_out, x_down = x_od[0], x_od[1]

    rows = lax.dynamic_index_in_dim(tokens, zh, 0, keepdims=False)
    cot = lax.dynamic_index_in_dim(cotangent, zh, 0, keepdims=False)

    cosine, sine = rope_tables()
    scalars = jnp.stack([length, chosen]).astype(jnp.int32)
    gain1, gain2 = attention_gain[None], feedforward_gain[None]

    normed, ranks, q, k, v, probs, att, part = call(
        attention_forward,
        (scalars, rows, gain1, ent_qkv, x_qkv, e_out, cosine, sine, w_qkv, w_out),
        (
            shaped(ROWS, WIDE),
            shaped(ROWS, LANES),
            shaped(8, ROWS, LANES),
            shaped(4, ROWS, LANES),
            shaped(4, ROWS, LANES),
            shaped(8, ROWS, ROWS, dtype=F32),
            shaped(2, ROWS, 512),
            shaped(ROWS, PART),
        ),
        6e9,
        48,
        scalars=(0,),
    )
    middle, rank_out, hidden, ranks_gu, slope_up, slope_gate, act = call(
        mlp_forward,
        (rows, part, core_swap(part), gain2, x_out, ent_gu, x_gu, gate_up_w),
        (
            shaped(ROWS, WIDE, dtype=F32),
            shaped(ROWS, LANES),
            shaped(ROWS, WIDE),
            shaped(ROWS, LANES),
            shaped(2, ROWS, 1024),
            shaped(2, ROWS, 1024),
            shaped(2, ROWS, 1024),
        ),
        5e9,
        48,
    )
    g2, drank_down, grads_gu, part_gu = call(
        mlp_backward,
        (scalars, cot, x_down, e_down, x_gu, slope_up, slope_gate, down_w, gate_up_w),
        (shaped(ROWS, WIDE), shaped(ROWS, LANES), shaped(2, ROWS, 2048), shaped(ROWS, PART)),
        8e9,
        48,
        scalars=(0,),
    )
    other_gu = core_swap(part_gu)
    part_down, gx_gu, ge_down = call(
        mlp_finish,
        (act, e_down, ranks_gu, grads_gu, drank_down, down_w),
        (shaped(ROWS, PART), shaped(2, 32, 2048), shaped(2, 16, 1024)),
        3e9,
        40,
    )
    other_down = core_swap(part_down)
    grad_middle, g1, drank_gu, drank_out, grads_qkv, part_qkv = call(
        attention_backward,
        (
            cot, part_gu, other_gu, middle, gain2, ent_gu, x_out, e_out, x_qkv, cosine, sine,
            q, k, v, probs, scalars, w_out, w_qkv,
        ),
        (
            shaped(ROWS, WIDE, dtype=F32),
            shaped(ROWS, WIDE),
            shaped(ROWS, LANES),
            shaped(ROWS, LANES),
            shaped(2, ROWS, 1024),
            shaped(ROWS, PART),
        ),
        8e9,
        48,
        scratch=(
            pltpu.VMEM((8, ROWS, LANES), BF),
            pltpu.VMEM((ROWS, LANES), F32),
            pltpu.VMEM((ROWS, LANES), F32),
        ),
        scalars=(15,),
    )
    other_qkv = core_swap(part_qkv)
    mixed, gx_qkv, ge_out, shared, wide_gu = call(
        middle_finish,
        (
            scalars, middle, part_down, other_down, x_down, g2, g1, rank_out, hidden, drank_gu,
            ranks, grads_qkv, drank_out, att,
        ),
        (
            shaped(ROWS, WIDE),
            shaped(2, 48, 1024),
            shaped(2, 16, 512),
            shaped(2, 16, WIDE),
            shaped(32, WIDE),
        ),
        1e9,
        40,
        scratch=(pltpu.VMEM((ROWS, LANES), BF),),
        scalars=(0,),
    )
    grad_in, wide_qkv = call(
        input_backward,
        (rows, part_qkv, other_qkv, grad_middle, gain1, ent_qkv, normed),
        (shaped(ROWS, WIDE), shaped(48, WIDE)),
        1e9,
        30,
        scratch=(pltpu.VMEM((ROWS, LANES), BF),),
    )

    columns = jnp.concatenate(
        [
            cut_heads(gx_qkv[:, :16, :512]),
            cut_heads(gx_qkv[:, 16:32, 512:768]),
            cut_heads(gx_qkv[:, 32:48, 768:]),
            gx_gu[:, :16, :1024],
            gx_gu[:, 16:, 1024:],
            cut_heads(ge_out),
            ge_down,
        ],
        axis=2,
    )
    shared = jnp.concatenate([shared[0], shared[1]], axis=1)
    wide = jnp.concatenate([wide_qkv.T, wide_gu.T, jnp.zeros((1536, 48), BF)], axis=1)
    lines = jnp.concatenate(
        [
            columns.reshape(2, 4, 132, 128),
            jnp.broadcast_to(shared.reshape(1, 4, 96, 128), (2, 4, 96, 128)),
            jnp.broadcast_to(
                wide.reshape(8, 4, 48, 128).transpose(1, 0, 2, 3).reshape(1, 4, 384, 128),
                (2, 4, 384, 128),
            ),
        ],
        axis=2,
    ).reshape(8, 612, 128)
    got = lax.all_to_all(lines, ("zh", "x"), 0, 0, tiled=True)
    peers = ((y * 2 + zl) * 4 + jnp.tile(jnp.arange(4), 2)) * 2 + jnp.repeat(jnp.arange(2), 4)
    match = (jnp.arange(64)[None, :] == peers[:, None]).astype(jnp.int32)
    peer_seq = jnp.sum(match * dealing[None, :], axis=1)
    match = (jnp.arange(64)[None, :] == peer_seq[:, None]).astype(jnp.int32)
    peer_adapter = jnp.sum(match * adapter_choice[None, :], axis=1)
    one_hot = (jnp.arange(8)[:, None] == peer_adapter[None, :]).astype(BF)
    summed = jnp.einsum("as,slk->alk", one_hot, got, preferred_element_type=F32).astype(BF)
    second = jnp.concatenate(
        [
            summed[:, :228],
            summed[:, 228:].reshape(8, 8, 48, 128).transpose(1, 0, 2, 3).reshape(8, 384, 128),
        ],
        axis=1,
    )
    final = lax.all_to_all(second, ("y", "zl"), 0, 0, tiled=True)
    final = jnp.sum(final.astype(F32), axis=0)
    cols = final[:132].reshape(4, 4224)
    shared = final[132:228].reshape(4, 3072)
    wide = final[228:].reshape(8, 48, 128).transpose(1, 2, 0)
    wide_qkv = wide[:, :48].reshape(48, 3, 16, 8).transpose(0, 1, 3, 2).reshape(48, 384)
    wide_gu = wide[:, 48:80].reshape(48, 2, 16, 8).transpose(0, 1, 3, 2).reshape(48, 256)

    def share(value):
        half = lax.dynamic_slice_in_dim(value, core * 192, 192, 0)
        got = lax.ppermute(half, AXES, flip_pairs("zz", (2, 2)))
        rest = core_swap(got)
        first, second = jnp.where(core == 0, got, rest), jnp.where(core == 0, rest, got)
        other = jnp.concatenate([first, second], axis=0)
        return jnp.stack([jnp.where(own_high, value, other), jnp.where(own_high, other, value)])

    return (
        share(mixed),
        share(grad_in),
        wide_qkv,
        cols[:, :384],
        cols[:, 384:576],
        cols[:, 576:768],
        cols[:, 2816:3200].T,
        shared[:, :1536],
        wide_gu,
        cols[:, 768:1792],
        cols[:, 1792:2816],
        cols[:, 3200:].T,
        shared[:, 1536:],
    )


def solution(mesh):
    fine = Mesh(mesh.devices.reshape(SIZES), AXES)
    dp, mp = ("y", "zl", "x"), ("zh", "c")
    return jax.shard_map(
        per_device,
        mesh=fine,
        in_specs=(
            P(dp, None, None),
            P(dp, None, None),
            P(),
            P(),
            P(),
            P(),
            P(),
            P(dp, mp),
            P(dp, mp),
            P(dp, mp),
            P(mp, dp),
            P(dp, mp),
            P(dp, mp),
            P(mp, dp),
            P(dp, None),
            P(dp, mp),
            P(dp, mp),
            P(dp, mp),
            P(mp, dp),
            P(dp, None),
            P(dp, None),
            P(dp, mp),
            P(dp, mp),
            P(mp, dp),
            P(dp, None),
        ),
        out_specs=(
            P(dp, None, None),
            P(dp, None, None),
            P(dp, None),
            P(dp, mp),
            P(dp, mp),
            P(dp, mp),
            P(mp, dp),
            P(dp, None),
            P(dp, None),
            P(dp, mp),
            P(dp, mp),
            P(mp, dp),
            P(dp, None),
        ),
        check_vma=False,
    )
```

```python
import jax
import jax.numpy as jnp
from jax import lax
from jax.experimental import pallas as pl
from jax.experimental.pallas import tpu as pltpu
from jax.sharding import Mesh, PartitionSpec as P

HEAD_DIM = 96
RANK = 16
EPS = 1e-05
THETA = 100000.0
BF = jnp.bfloat16
F32 = jnp.float32

AXES = ("y", "zl", "x", "zh", "c")
SIZES = (4, 2, 4, 2, 2)
PARTS = (
    (0, 32, (("z", "y"), ("y", "x"), ("x", "z")), ((1, 1), (3, 3))),
    (32, 16, (("x", "x"), ("z", "z"), ("y", "y")), ((1, 3), (3, 1))),
)
ATTN, MLP = 2048, 3072
WIDTHS = (ATTN, MLP)


def device_index(y, z, x, c):
    return (((y * 2 + z % 2) * 4 + x) * 2 + z // 2) * 2 + c


def flip_pairs(axes, flips):
    pairs = []
    for y in range(4):
        for z in range(4):
            for x in range(4):
                for c in range(2):
                    to = {"x": x, "y": y, "z": z}
                    to[axes[c]] ^= flips[c]
                    pairs.append(
                        (device_index(y, z, x, c), device_index(to["y"], to["z"], to["x"], c))
                    )
    return pairs


def core_swap(value):
    pairs = [(i, i ^ 1) for i in range(128)]
    return lax.ppermute(value, AXES, pairs)


class Links:
    def __init__(self):
        self.last = ()

    def __call__(self, values, axes, flips):
        values, _ = lax.optimization_barrier((tuple(values), self.last))
        out = tuple(
            lax.ppermute(v, AXES, flip_pairs(a, f)) for v, a, f in zip(values, axes, flips)
        )
        self.last = out
        return out


def ring_stage(send, blocks, stage, forward, between=None):
    a, b = blocks
    (p, q) = (PARTS[i][2][stage] for i in range(2))
    (s0, s1), (t0, t1) = (PARTS[i][3] for i in range(2))
    if not forward:
        an, bn, af, bf, ao, bo = send(
            (a, b, a, b, a, b), (p, q, p, q, p, q), (s0, t0, s1, t1, (2, 2), (2, 2))
        )
        return [[a, an, ao, af], [b, bn, bo, bf]]
    an, af, bn, bf = send((a, a, b, b), (p, p, q, q), (s0, s1, t0, t1))
    if between is not None:
        send.last = (send.last, between())
    half = a.shape[0] // 2
    al, ah, bl, bh = send(
        (an[:half], af[half:], bn[:half], bf[half:]), (p, p, q, q), (s1, s0, t1, t0)
    )
    return [[a, an, al, ah, af], [b, bn, bl, bh, bf]]


def fetch(coords, pieces, out, sem):
    own = {"y": coords[0], "z": coords[1], "x": coords[2]}
    core = coords[3]

    def choose(first, second):
        return jnp.where(core == 0, first, second)

    def row(axis, j):
        at = own[axis] ^ j
        if axis == "z":
            return lax.rem(at, 2) * 192
        return at * (384 if axis == "y" else 48)

    for part, (start, count, axes, steps) in enumerate(PARTS):
        rows, highs = [], []
        for axis in axes:
            swapped = steps[0][1] == 3
            far = [(j, (4 - j) % 4 if swapped else j) for j in range(4)]
            rows.append([choose(row(axis[0], u), row(axis[1], v)) for u, v in far])
            highs.append(
                [
                    choose(
                        lax.div(own["z"] ^ u, 2) if axis[0] == "z" else 0,
                        lax.div(own["z"] ^ v, 2) if axis[1] == "z" else 0,
                    )
                    for u, v in far
                ]
            )
        for q, (j3, k0, many) in enumerate(
            ((0, 0, 16), (1, 0, 16), (2, 0, 8), (2, 8, 8), (3, 0, 16))
        ):
            for k in range(many):
                j2, j1 = (k0 + k) // 4, (k0 + k) % 4
                first = rows[0][j1] + rows[1][j2] + rows[2][j3] + start
                high = highs[0][j1] + highs[1][j2] + highs[2][j3]
                pltpu.make_async_copy(
                    pieces[part * 5 + q].at[k],
                    out.at[high, pl.ds(pl.multiple_of(first, 16), count), :],
                    sem,
                ).start()


def ones_where(condition):
    return jnp.where(condition, 1.0, 0.0).astype(BF)


def iota2(rows, cols):
    return (
        lax.broadcasted_iota(jnp.int32, (rows, cols), 0),
        lax.broadcasted_iota(jnp.int32, (rows, cols), 1),
    )


def matmul(left, right):
    return jnp.dot(left, right, preferred_element_type=F32)


def inner_rows(left, right):
    return lax.dot_general(left, right, (((0,), (0,)), ((), ())), preferred_element_type=F32)


def inner_cols(left, right):
    return lax.dot_general(left, right, (((1,), (1,)), ((), ())), preferred_element_type=F32)


ROWS = 384
WIDE = 1536
LANES = 128
PART = WIDE + LANES
FACTOR = HEAD_DIM ** (-0.5)


def row_blocks(body):
    @pl.loop(0, ROWS // 128)
    def _(i):
        body(pl.ds(pl.multiple_of(i * 128, 128), 128))


def row_scale(values):
    return lax.rsqrt(jnp.mean(values * values, axis=-1, keepdims=True) + EPS)


def back_of_norm(inputs, gain, grad):
    scale = row_scale(inputs)
    weighted = gain * grad
    return scale * weighted - inputs * (
        scale * scale * scale * jnp.mean(inputs * weighted, axis=-1, keepdims=True)
    )


def live_rows(length, rows):
    at = lax.broadcasted_iota(jnp.int32, (128, 1), 0) + rows.start
    return at < length


def spin(values, cosine, sine):
    return values * cosine + pltpu.roll(values, 64, 1) * sine


def project_cols(out, parts, rank_parts):
    @pl.loop(0, WIDE // 256)
    def _(n):
        cols = pl.ds(pl.multiple_of(n * 256, 256), 256)
        out[:, cols] = sum(inner_cols(left(), right(cols)) for left, right in parts).astype(BF)

    out[:, WIDE:] = sum(inner_cols(left(), right()) for left, right in rank_parts).astype(BF)


def attention_forward(ready, flush, coords, tok, gain, cosine, sine, *refs):
    pieces = refs[:10]
    w_far, ot_far, probs_far, ent, ent_gu, exits, x_gu, entry_o, e_down, x_od = refs[10:20]
    normed, ranks, q, k, v, att, part = refs[20:27]
    raw, w, ot, probs, sem = refs[27:]
    fetch(coords, pieces, raw, sem.at[0])
    chosen, length = coords[4], coords[5]

    def start(rows):
        x = tok[rows, :].astype(F32)
        normed[rows, :] = (x * row_scale(x) * gain[...]).astype(BF)

    row_blocks(start)
    i, j = iota2(384, 512)
    spread = ones_where(j == i + 16 * lax.div(i, 48))
    i, j = iota2(384, 128)
    picks = []
    for h in range(2):
        col = i + 320 * h
        third, rank = lax.div(col, 128), lax.rem(col, 16)
        ours = (lax.div(lax.rem(col, 128), 16) == chosen) & (i < 320)
        picks.append(
            (
                ones_where(ours & (third < 3) & (j == third * 16 + rank)),
                ones_where(ours & (third >= 3) & (j == (third - 3) * 16 + rank)),
            )
        )
    pltpu.make_async_copy(raw, raw, sem.at[0]).wait()

    @pl.loop(0, 3)
    def _(n):
        rows = pl.ds(pl.multiple_of(n * 512, 512), 512)
        for h in range(2):
            for b in range(2):
                w[h, rows, b * 512 : b * 512 + 512] = matmul(
                    raw[h, rows, b * 384 : b * 384 + 384], spread
                ).astype(BF)
            ot[h, rows, :] = matmul(raw[h, rows, 768:1152], spread).astype(BF)
        for out, which in ((ent, 0), (ent_gu, 1)):
            out[rows, :] = sum(
                matmul(raw[h, rows, 1152:1536], picks[h][which]) for h in range(2)
            ).astype(BF)

    keep = [
        pltpu.make_async_copy(w, w_far, sem.at[1]),
        pltpu.make_async_copy(ot, ot_far, sem.at[2]),
    ]
    for copy in keep:
        copy.start()
    i, j = iota2(128, 192)
    lane = lax.broadcasted_iota(jnp.int32, (128, 512), 1)
    mine = pl.ds(pl.multiple_of(chosen * 192, 16), 192)
    for h in range(2):
        block = raw[h, mine, 1536:2048]

        def line(t, first):
            take = ones_where((j == 12 * (i - first) + t) & (i >= first) & (i < first + 16))
            return matmul(take, block).astype(BF)

        for t in range(2):
            x_gu[h, :, t * 512 : t * 512 + 512] = line(t, 0)
            x_gu[h, :, 1024 + t * 512 : 1536 + t * 512] = line(2 + t, 16)
            e_down[h, :, t * 512 : t * 512 + 512] = line(4 + t, 0)
        for t in range(3):
            x_od[h, :, t * 512 : t * 512 + 512] = line(6 + t, 0)
        exits[h, :, :512] = matmul(line(9, 0)[:, :384], spread).astype(BF)
        key = matmul(line(10, 16)[:, :384], spread)
        value = matmul(line(10, 32)[:, :384], spread)
        exits[h, :, 512:] = jnp.where(lane < 256, key, value).astype(BF)
        entry_o[h] = matmul(line(11, 0)[:, :384], spread).astype(BF)

    ranks[...] = matmul(normed[...], ent[...]).astype(BF)
    for h in range(2):
        for n in range(4):
            cols = slice(n * 256, n * 256 + 256)
            t = matmul(normed[...], w[h, :, cols]) + matmul(ranks[...], exits[h, :, cols])
            for i in range(2):
                head = t[:, i * 128 : i * 128 + 128]
                if n < 2:
                    q[h * 4 + n * 2 + i] = spin(head, cosine[...], sine[...]).astype(BF)
                elif n == 2:
                    k[h * 2 + i] = spin(head, cosine[...], sine[...]).astype(BF)
                else:
                    v[h * 2 + i] = head.astype(BF)
    at_q, at_k = iota2(ROWS, ROWS)
    allowed = (at_k <= at_q) & (at_k < length)
    for h in range(2):

        @pl.loop(0, 4)
        def _(i):
            g = h * 2 + i // 2
            s = inner_cols(q[h * 4 + i], k[g]) * FACTOR
            s = jnp.where(allowed, s, -1e30)
            e = jnp.exp(s - jnp.max(s, axis=-1, keepdims=True))
            p = e / jnp.sum(e, axis=-1, keepdims=True)
            probs[h * 4 + i] = p
            att[h, :, pl.ds(pl.multiple_of(i * 128, 128), 128)] = matmul(p.astype(BF), v[g]).astype(BF)

    flush(*range(3, 16))
    keep.append(pltpu.make_async_copy(probs, probs_far, sem.at[3]))
    keep[-1].start()
    project_cols(
        part,
        [(lambda h=h: att[h], lambda cols, h=h: ot[h, cols, :]) for h in range(2)],
        [(lambda h=h: att[h], lambda h=h: entry_o[h]) for h in range(2)],
    )
    for copy in keep:
        copy.wait()


def mlp(ready, flush, coords, tok, own, other, cot, gain, exit_o, ent, exits, exit_d, entry_d, *refs):
    pieces = refs[:10]
    middle, rank_out, hidden, g2, parts, exit_grads, entry_grads = refs[10:17]
    ranks, drank, grads, act, w, sem = refs[17:]
    fetch(coords, pieces, w, sem)
    ready(0)

    def start(rows):
        total = own[rows, :].astype(F32) + other[rows, :].astype(F32)
        r = total[:, WIDE:].astype(BF)
        rank_out[rows, :] = r
        mid = tok[rows, :].astype(F32) + total[:, :WIDE] + matmul(r, exit_o[...])
        middle[rows, :] = mid
        hidden[rows, :] = (mid * row_scale(mid) * gain[...]).astype(BF)
        g2[rows, :] = jnp.where(live_rows(coords[5], rows), cot[rows, :].astype(F32), 0.0).astype(BF)

    row_blocks(start)
    ready(1)
    ranks[...] = matmul(hidden[...], ent[...]).astype(BF)
    drank[...] = inner_cols(g2[...], exit_d[...]).astype(BF)
    flush(0, 1, 2, 3)
    pltpu.make_async_copy(w, w, sem).wait()
    for h in range(2):

        @pl.loop(0, 4)
        def _(n):
            cols = pl.ds(pl.multiple_of(n * 256, 256), 256)
            ups = pl.ds(pl.multiple_of(n * 256 + 1024, 256), 256)
            downs = pl.ds(pl.multiple_of(n * 256 + 2048, 256), 256)
            gate = matmul(hidden[...], w[h, :, cols]) + matmul(ranks[...], exits[h, :, cols])
            up = matmul(hidden[...], w[h, :, ups]) + matmul(ranks[...], exits[h, :, ups])
            grad = matmul(g2[...], w[h, :, downs]) + matmul(drank[...], entry_d[h, :, cols])
            sigma = 1.0 / (1.0 + jnp.exp(-gate))
            silu = gate * sigma
            act[h, :, cols] = (silu * up).astype(BF)
            grads[h, :, ups] = (grad * silu).astype(BF)
            grads[h, :, cols] = (grad * (up * sigma * (1.0 + gate - silu))).astype(BF)

    project_cols(
        parts.at[0],
        [(lambda h=h: grads[h], lambda cols, h=h: w[h, cols, :2048]) for h in range(2)],
        [(lambda h=h: grads[h], lambda h=h: exits[h]) for h in range(2)],
    )
    project_cols(
        parts.at[1],
        [(lambda h=h: act[h], lambda cols, h=h: w[h, cols, 2048:]) for h in range(2)],
        [(lambda h=h: act[h], lambda h=h: entry_d[h]) for h in range(2)],
    )
    for h in range(2):
        exit_grads[h] = inner_rows(ranks[...], grads[h])[:32].astype(BF)
        entry_grads[h] = inner_rows(drank[...], act[h])[:16].astype(BF)


def attention_backward(
    ready, flush, g2, own, other, middle, gain, ent, exit_o, entry_o, exits, cosine, sine, q, k, v, probs, ot, w,
    grad_middle, g1, drank_gu, drank_out, grads, part,
    grad_att, sum_k, sum_v,
):
    ready(0)

    def start(rows):
        total = own[rows, :].astype(F32) + other[rows, :].astype(F32)
        d = total[:, WIDE:].astype(BF)
        drank_gu[rows, :] = d
        hidden = total[:, :WIDE] + inner_cols(d, ent[...])
        mid = g2[rows, :].astype(F32) + back_of_norm(middle[rows, :], gain[...], hidden)
        grad_middle[rows, :] = mid
        g1[rows, :] = mid.astype(BF)

    row_blocks(start)
    ready(1)
    drank_out[...] = inner_cols(g1[...], exit_o[...]).astype(BF)
    flush(0, 1, 2, 3)
    for h in range(2):
        for n in range(2):
            cols = slice(n * 256, n * 256 + 256)
            t = matmul(g1[...], ot[h, :, cols]) + matmul(drank_out[...], entry_o[h, :, cols])
            for i in range(2):
                grad_att[h * 4 + n * 2 + i] = t[:, i * 128 : i * 128 + 128].astype(BF)
    ready(2)
    for h in range(2):

        @pl.loop(0, 2)
        def _(j):
            g = h * 2 + j
            for i in range(2):
                head = h * 4 + j * 2 + i
                p = probs[head]
                ga = grad_att[head]
                gp = inner_cols(ga, v[g])
                delta = jnp.sum(p * gp, axis=-1, keepdims=True)
                gs = (p * (gp - delta)).astype(BF)
                gq = matmul(gs, k[g]) * FACTOR
                grads[h, :, pl.ds(pl.multiple_of((j * 2 + i) * 128, 128), 128)] = spin(
                    gq, cosine[...], -sine[...]
                ).astype(BF)
                gk = inner_rows(gs, q[head])
                gv = inner_rows(p.astype(BF), ga)
                if i == 0:
                    sum_k[...] = gk
                    sum_v[...] = gv
                else:
                    gk = (sum_k[...] + gk) * FACTOR
                    gv = sum_v[...] + gv
                    grads[h, :, pl.ds(pl.multiple_of(512 + j * 128, 128), 128)] = spin(
                        gk, cosine[...], -sine[...]
                    ).astype(BF)
                    grads[h, :, pl.ds(pl.multiple_of(768 + j * 128, 128), 128)] = gv.astype(BF)

    flush(4)
    ready(3)
    project_cols(
        part,
        [(lambda h=h: grads[h], lambda cols, h=h: w[h, cols, :]) for h in range(2)],
        [(lambda h=h: grads[h], lambda h=h: exits[h]) for h in range(2)],
    )


def middle_finish(
    ready, flush, scalars, middle, own, other, exit_d, g2, g1, rank_out, hidden, drank_gu, ranks, grads, drank_out, att,
    mixed, exit_grads, entry_grads, shared, wide,
    rank_down,
):
    ready(0)

    def start(rows):
        total = own[rows, :].astype(F32) + other[rows, :].astype(F32)
        r = total[:, WIDE:].astype(BF)
        rank_down[rows, :] = r
        result = middle[rows, :] + total[:, :WIDE] + matmul(r, exit_d[...])
        mixed[rows, :] = jnp.where(live_rows(scalars[0], rows), result, 0.0).astype(BF)

    row_blocks(start)
    flush(0)
    ready(1)
    for h in range(2):
        exit_grads[h] = inner_rows(ranks[...], grads[h])[:48].astype(BF)
        entry_grads[h] = inner_rows(drank_out[...], att[h])[:16].astype(BF)
    shared[0] = inner_rows(rank_out[...], g1[...])[:16].astype(BF)
    shared[1] = inner_rows(rank_down[...], g2[...])[:16].astype(BF)
    wide[...] = inner_rows(drank_gu[...], hidden[...])[:32].astype(BF)


def input_backward(
    ready, flush, tok, own, other, grad_middle, gain, ent, normed,
    grad_in, wide,
    drank,
):
    ready(0)

    def start(rows):
        total = own[rows, :].astype(F32) + other[rows, :].astype(F32)
        d = total[:, WIDE:].astype(BF)
        drank[rows, :] = d
        grad = total[:, :WIDE] + inner_cols(d, ent[...])
        back = back_of_norm(tok[rows, :].astype(F32), gain[...], grad)
        grad_in[rows, :] = (grad_middle[rows, :] + back).astype(BF)

    row_blocks(start)
    flush(0)
    ready(1)
    wide[...] = inner_rows(drank[...], normed[...])[:48].astype(BF)


def gather_gradients(ready, flush, final, g_q, g_k, g_v, g_gate, g_up, g_eo, g_ed, g_xo, g_xd, wide_qkv, wide_gu, total, kv):
    @pl.loop(0, 3)
    def _(i):
        rows = pl.ds(pl.multiple_of(i * 208, 16), 208)
        total[rows, :] = sum(final[g, rows, :].astype(F32) for g in range(8))

    at = 0
    for out, blocks in ((g_q, 3), (kv, 3), (g_gate, 8), (g_up, 8), (g_eo, 3), (g_ed, 8)):
        for n in range(blocks):
            for r in range(4):
                line = r * 33 + at + n
                out[r : r + 1, n * 128 : n * 128 + 128] = total[line : line + 1, :]
        at += blocks
    both_kv = kv[...]
    g_k[...] = both_kv[:, :192]
    g_v[...] = both_kv[:, 192:]
    for m, out in enumerate((g_xo, g_xd)):
        for n in range(12):
            for r in range(4):
                line = 132 + r * 24 + m * 12 + n
                out[r : r + 1, n * 128 : n * 128 + 128] = total[line : line + 1, :]
    lane = lax.broadcasted_iota(jnp.int32, (48, 128), 1)
    for third in range(5):
        columns = jnp.zeros((48, 128), F32)
        for a in range(8):
            block = total[228 + 48 * a : 276 + 48 * a, :]
            moved = pltpu.roll(block, (a * 16 - third * 16) % 128, 1)
            columns = jnp.where((lane >= a * 16) & (lane < a * 16 + 16), moved, columns)
        out, n = (wide_qkv, third) if third < 3 else (wide_gu, third - 3)
        out[:, n * 128 : n * 128 + 128] = columns


def shaped(*extent, dtype=BF):
    return jax.ShapeDtypeStruct(extent, dtype)


def call(
    body, args, outs, flops, megabytes, scratch=(), scalars=(), far_in=(), far_out=(), late=None, sent=()
):
    whole = pl.BlockSpec(memory_space=pltpu.VMEM)
    small = pl.BlockSpec(memory_space=pltpu.SMEM)
    far = pl.BlockSpec(memory_space=pltpu.HBM)
    late = late or {}
    order = sorted(late, key=lambda i: late[i])
    block = [a[1] if isinstance(a, tuple) else None for a in args]
    args = [a[0] if isinstance(a, tuple) else a for a in args]
    shapes = [a.shape if i is None else a.shape[1:] for a, i in zip(args, block)]
    extra = len(order) + len(sent) + 2

    def kernel(*refs):
        spare, sem, out_sem = refs[len(refs) - extra : -2], refs[-2], refs[-1]
        refs = list(refs[: len(refs) - extra])
        copies = []
        for n, i in enumerate(order):
            source = refs[i] if block[i] is None else refs[i].at[block[i]]
            copies.append(pltpu.make_async_copy(source, spare[n], sem.at[n]))
            copies[-1].start()
            refs[i] = spare[n]
        leaving = {}
        for n, i in enumerate(sent):
            held = spare[len(order) + n]
            leaving[i] = pltpu.make_async_copy(held, refs[len(args) + i], out_sem.at[n])
            refs[len(args) + i] = held

        def ready(group):
            for n, i in enumerate(order):
                if late[i] == group:
                    copies[n].wait()

        started = []

        def flush(*which):
            for i in which:
                leaving[i].start()
                started.append(i)

        body(ready, flush, *refs)
        flush(*(i for i in sent if i not in started))
        for i in sent:
            leaving[i].wait()

    spares = [pltpu.VMEM(shapes[i], args[i].dtype) for i in order]
    spares += [pltpu.VMEM(outs[i].shape, outs[i].dtype) for i in sent]
    spares.append(pltpu.SemaphoreType.DMA((max(1, len(order)),)))
    spares.append(pltpu.SemaphoreType.DMA((max(1, len(sent)),)))
    return pl.pallas_call(
        kernel,
        out_shape=list(outs),
        in_specs=[
            small if i in scalars else far if i in far_in or i in late else whole
            for i in range(len(args))
        ],
        out_specs=[far if i in far_out or i in sent else whole for i in range(len(outs))],
        scratch_shapes=[*scratch, *spares],
        compiler_params=pltpu.CompilerParams(vmem_limit_bytes=59 << 20),
        cost_estimate=pl.CostEstimate(
            flops=int(flops),
            transcendentals=0,
            bytes_accessed=sum(a.size * a.dtype.itemsize for a in args),
        ),
    )(*args)


def lookup(table, index):
    return jnp.sum(jnp.where(jnp.arange(table.shape[0]) == index, table, 0))


def rope_tables():
    half = HEAD_DIM // 2
    freq = jnp.power(THETA, -2.0 * jnp.arange(half, dtype=F32) / HEAD_DIM)
    angle = jnp.arange(ROWS, dtype=F32)[:, None] * freq[None, :]
    cosine, sine, pad = jnp.cos(angle), jnp.sin(angle), jnp.zeros((ROWS, 16), F32)
    return (
        jnp.concatenate([cosine, pad, cosine, pad], axis=1),
        jnp.concatenate([-sine, pad, sine, pad], axis=1),
    )


def cut_heads(array):
    lead = array.shape[:-1]
    return array.reshape(*lead, -1, 64)[..., :48].reshape(*lead, -1)


def per_device(
    tokens,
    cotangent,
    lengths,
    dealing,
    adapter_choice,
    attention_gain,
    feedforward_gain,
    query_weight,
    key_weight,
    value_weight,
    output_weight,
    gate_weight,
    up_weight,
    down_weight,
    entry_qkv,
    exit_query,
    exit_key,
    exit_value,
    entry_out,
    exit_out,
    entry_gate_up,
    exit_gate,
    exit_up,
    entry_down,
    exit_down,
):
    y, zl, x, zh, core = (lax.axis_index(a) for a in AXES)
    own_high = zh == 0
    entries = jnp.concatenate([entry_qkv, entry_gate_up], axis=1)
    entries = jnp.where(own_high, entries[:, :320], entries[:, 320:])
    pad = jnp.zeros((4, 128), BF)
    exits = jnp.concatenate(
        [
            exit_gate,
            exit_up,
            entry_down.T,
            jnp.where(own_high, exit_out, exit_down),
            exit_query,
            pad,
            exit_key,
            exit_value,
            pad,
            entry_out.T,
            pad,
        ],
        axis=1,
    ).reshape(48, 512)
    payload = jnp.concatenate(
        [
            query_weight,
            key_weight,
            value_weight,
            output_weight.T,
            entries,
            jnp.zeros((48, 64), BF),
            exits,
            gate_weight,
            up_weight,
            down_weight.T,
        ],
        axis=1,
    )
    slot = ((y * 2 + zl) * 4 + x) * 2 + zh
    sequence = lookup(dealing, slot)
    length = lookup(lengths, sequence)
    chosen = lookup(adapter_choice, sequence)
    coords = jnp.stack([y, zh * 2 + zl, x, core, chosen, length]).astype(jnp.int32)

    send = Links()
    blocks = [payload[None, first : first + count] for first, count, _, _ in PARTS]
    blocks = [jnp.concatenate(p, 0) for p in ring_stage(send, blocks, 0, False)]
    second = ring_stage(send, blocks, 1, True)

    def group(start, width):
        return [jnp.concatenate([q[:, :, start : start + width] for q in p], 0) for p in second]

    attn_pieces = sum(ring_stage(send, group(0, ATTN), 2, True), [])
    rows = lax.dynamic_index_in_dim(tokens, zh, 0, keepdims=False)
    cot = lax.dynamic_index_in_dim(cotangent, zh, 0, keepdims=False)

    cosine, sine = rope_tables()
    scalars = jnp.stack([length, chosen]).astype(jnp.int32)
    gain1, gain2 = attention_gain[None], feedforward_gain[None]

    (
        w_qkv, w_out, probs, ent_qkv, ent_gu, x_qkv, x_gu, e_out, e_down, x_od,
        normed, ranks, q, k, v, att, part,
    ) = call(
        attention_forward,
        (coords, rows, gain1, cosine, sine, *attn_pieces),
        (
            shaped(2, WIDE, 1024),
            shaped(2, WIDE, 512),
            shaped(8, ROWS, ROWS, dtype=F32),
            shaped(WIDE, LANES),
            shaped(WIDE, LANES),
            shaped(2, LANES, 1024),
            shaped(2, LANES, 2048),
            shaped(2, LANES, 512),
            shaped(2, LANES, 1024),
            shaped(2, LANES, WIDE),
            shaped(ROWS, WIDE),
            shaped(ROWS, LANES),
            shaped(8, ROWS, LANES),
            shaped(4, ROWS, LANES),
            shaped(4, ROWS, LANES),
            shaped(2, ROWS, 512),
            shaped(ROWS, PART),
        ),
        12e9,
        50,
        scratch=(
            pltpu.VMEM((2, WIDE, ATTN), BF),
            pltpu.VMEM((2, WIDE, 1024), BF),
            pltpu.VMEM((2, WIDE, 512), BF),
            pltpu.VMEM((8, ROWS, ROWS), F32),
            pltpu.SemaphoreType.DMA((4,)),
        ),
        scalars=(0,),
        far_in=tuple(range(5, 15)),
        far_out=(0, 1, 2),
        sent=tuple(range(3, 17)),
    )
    x_out, x_down = x_od[0], x_od[1]
    mlp_pieces = sum(ring_stage(send, group(ATTN, MLP), 2, True, lambda: part), [])
    middle, rank_out, hidden, g2, parts, gx_gu, ge_down = call(
        mlp,
        (
            coords, rows, part, core_swap(part), cot, gain2, x_out, ent_gu, x_gu, x_down, e_down,
            *mlp_pieces,
        ),
        (
            shaped(ROWS, WIDE, dtype=F32),
            shaped(ROWS, LANES),
            shaped(ROWS, WIDE),
            shaped(ROWS, WIDE),
            shaped(2, ROWS, PART),
            shaped(2, 32, 2048),
            shaped(2, 16, 1024),
        ),
        15e9,
        50,
        scratch=(
            pltpu.VMEM((ROWS, LANES), BF),
            pltpu.VMEM((ROWS, LANES), BF),
            pltpu.VMEM((2, ROWS, 2048), BF),
            pltpu.VMEM((2, ROWS, 1024), BF),
            pltpu.VMEM((2, WIDE, MLP), BF),
            pltpu.SemaphoreType.DMA(()),
        ),
        scalars=(0,),
        far_in=tuple(range(11, 21)),
        late={1: 0, 2: 0, 3: 0, 4: 0, 6: 0, 7: 1, 8: 1, 9: 1, 10: 1},
        sent=(0, 1, 2, 3, 4, 5, 6),
    )
    others = core_swap(parts)
    grad_middle, g1, drank_gu, drank_out, grads_qkv, part_qkv = call(
        attention_backward,
        (
            g2, (parts, 0), (others, 0), middle, gain2, ent_gu, x_out, e_out, x_qkv, cosine, sine,
            q, k, v, probs, w_out, w_qkv,
        ),
        (
            shaped(ROWS, WIDE, dtype=F32),
            shaped(ROWS, WIDE),
            shaped(ROWS, LANES),
            shaped(ROWS, LANES),
            shaped(2, ROWS, 1024),
            shaped(ROWS, PART),
        ),
        8e9,
        46,
        scratch=(
            pltpu.VMEM((8, ROWS, LANES), BF),
            pltpu.VMEM((ROWS, LANES), F32),
            pltpu.VMEM((ROWS, LANES), F32),
        ),
        late={
            0: 0, 1: 0, 2: 0, 3: 0, 5: 0, 6: 1, 7: 1, 15: 1, 9: 2, 10: 2, 11: 2, 12: 2, 13: 2, 14: 2, 8: 3, 16: 3,
        },
        sent=(0, 1, 2, 3, 4, 5),
    )
    other_qkv = core_swap(part_qkv)
    mixed, gx_qkv, ge_out, shared, wide_gu = call(
        middle_finish,
        (
            scalars, middle, (parts, 1), (others, 1), x_down, g2, g1, rank_out, hidden, drank_gu,
            ranks, grads_qkv, drank_out, att,
        ),
        (
            shaped(ROWS, WIDE),
            shaped(2, 48, 1024),
            shaped(2, 16, 512),
            shaped(2, 16, WIDE),
            shaped(32, WIDE),
        ),
        1e9,
        40,
        scratch=(pltpu.VMEM((ROWS, LANES), BF),),
        scalars=(0,),
        sent=(0, 1, 2, 3, 4),
        late={1: 0, 2: 0, 3: 0, 4: 0, 5: 1, 6: 1, 7: 1, 8: 1, 9: 1, 10: 1, 11: 1, 12: 1, 13: 1},
    )
    grad_in, wide_qkv = call(
        input_backward,
        (rows, part_qkv, other_qkv, grad_middle, gain1, ent_qkv, normed),
        (shaped(ROWS, WIDE), shaped(48, WIDE)),
        1e9,
        40,
        scratch=(pltpu.VMEM((ROWS, LANES), BF),),
        late={0: 0, 1: 0, 2: 0, 3: 0, 5: 0, 6: 1},
        sent=(0, 1),
    )

    def to_other_chip(value):
        half = lax.dynamic_slice_in_dim(value, core * 192, 192, 0)
        return lax.ppermute(half, AXES, flip_pairs("zz", (2, 2)))

    sent_mixed, sent_in = to_other_chip(mixed), to_other_chip(grad_in)

    columns = jnp.concatenate(
        [
            cut_heads(gx_qkv[:, :16, :512]),
            cut_heads(gx_qkv[:, 16:32, 512:768]),
            cut_heads(gx_qkv[:, 32:48, 768:]),
            gx_gu[:, :16, :1024],
            gx_gu[:, 16:, 1024:],
            cut_heads(ge_out),
            ge_down,
        ],
        axis=2,
    )
    shared = jnp.concatenate([shared[0], shared[1]], axis=1)
    wide = jnp.concatenate([wide_qkv.T, wide_gu.T, jnp.zeros((1536, 48), BF)], axis=1)
    lines = jnp.concatenate(
        [
            columns.reshape(2, 4, 132, 128),
            jnp.broadcast_to(shared.reshape(1, 4, 96, 128), (2, 4, 96, 128)),
            jnp.broadcast_to(
                wide.reshape(8, 4, 48, 128).transpose(1, 0, 2, 3).reshape(1, 4, 384, 128),
                (2, 4, 384, 128),
            ),
            jnp.zeros((2, 4, 12, 128), BF),
        ],
        axis=2,
    ).reshape(8, 624, 128)
    lines, sent_mixed = lax.optimization_barrier((lines, sent_mixed))
    got = lax.all_to_all(lines, ("zh", "x"), 0, 0, tiled=True)
    peers = ((y * 2 + zl) * 4 + jnp.tile(jnp.arange(4), 2)) * 2 + jnp.repeat(jnp.arange(2), 4)
    match = (jnp.arange(64)[None, :] == peers[:, None]).astype(jnp.int32)
    peer_seq = jnp.sum(match * dealing[None, :], axis=1)
    match = (jnp.arange(64)[None, :] == peer_seq[:, None]).astype(jnp.int32)
    peer_adapter = jnp.sum(match * adapter_choice[None, :], axis=1)
    one_hot = (jnp.arange(8)[:, None] == peer_adapter[None, :]).astype(BF)
    summed = jnp.einsum("as,slk->alk", one_hot, got, preferred_element_type=F32).astype(BF)
    second = jnp.concatenate(
        [
            summed[:, :228],
            summed[:, 228:612].reshape(8, 8, 48, 128).transpose(1, 0, 2, 3).reshape(8, 384, 128),
            summed[:, 612:],
        ],
        axis=1,
    )
    second, sent_in = lax.optimization_barrier((second, sent_in))
    final = lax.all_to_all(second, ("y", "zl"), 0, 0, tiled=True)
    g_q, g_k, g_v, g_gate, g_up, g_eo, g_ed, g_xo, g_xd, wide_qkv, wide_gu = call(
        gather_gradients,
        (final,),
        (
            shaped(4, 384, dtype=F32),
            shaped(4, 192, dtype=F32),
            shaped(4, 192, dtype=F32),
            shaped(4, 1024, dtype=F32),
            shaped(4, 1024, dtype=F32),
            shaped(4, 384, dtype=F32),
            shaped(4, 1024, dtype=F32),
            shaped(4, WIDE, dtype=F32),
            shaped(4, WIDE, dtype=F32),
            shaped(48, 384, dtype=F32),
            shaped(48, 256, dtype=F32),
        ),
        1e6,
        10,
        scratch=(pltpu.VMEM((624, LANES), F32), pltpu.VMEM((4, 384), F32)),
    )

    gots = jnp.stack([sent_mixed, sent_in])
    rests = core_swap(gots)

    def share(value, n):
        got, rest = gots[n], rests[n]
        first, second = jnp.where(core == 0, got, rest), jnp.where(core == 0, rest, got)
        other = jnp.concatenate([first, second], axis=0)
        return jnp.stack([jnp.where(own_high, value, other), jnp.where(own_high, other, value)])

    return (
        share(mixed, 0),
        share(grad_in, 1),
        wide_qkv,
        g_q,
        g_k,
        g_v,
        g_eo.T,
        g_xo,
        wide_gu,
        g_gate,
        g_up,
        g_ed.T,
        g_xd,
    )


def solution(mesh):
    fine = Mesh(mesh.devices.reshape(SIZES), AXES)
    dp, mp = ("y", "zl", "x"), ("zh", "c")
    return jax.shard_map(
        per_device,
        mesh=fine,
        in_specs=(
            P(dp, None, None),
            P(dp, None, None),
            P(),
            P(),
            P(),
            P(),
            P(),
            P(dp, mp),
            P(dp, mp),
            P(dp, mp),
            P(mp, dp),
            P(dp, mp),
            P(dp, mp),
            P(mp, dp),
            P(dp, None),
            P(dp, mp),
            P(dp, mp),
            P(dp, mp),
            P(mp, dp),
            P(dp, None),
            P(dp, None),
            P(dp, mp),
            P(dp, mp),
            P(mp, dp),
            P(dp, None),
        ),
        out_specs=(
            P(dp, None, None),
            P(dp, None, None),
            P(dp, None),
            P(dp, mp),
            P(dp, mp),
            P(dp, mp),
            P(mp, dp),
            P(dp, None),
            P(dp, None),
            P(dp, mp),
            P(dp, mp),
            P(mp, dp),
            P(dp, None),
        ),
        check_vma=False,
    )
```

```python
import jax
import jax.numpy as jnp
from jax import lax
from jax.experimental import pallas as pl
from jax.experimental.pallas import tpu as pltpu
from jax.sharding import Mesh, PartitionSpec as P

HEAD_DIM = 96
RANK = 16
EPS = 1e-05
THETA = 100000.0
BF = jnp.bfloat16
F32 = jnp.float32

AXES = ("y", "zl", "x", "zh", "c")
SIZES = (4, 2, 4, 2, 2)
PARTS = (
    (0, 32, (("z", "y"), ("y", "x"), ("x", "z")), ((1, 1), (3, 3))),
    (32, 16, (("x", "x"), ("z", "z"), ("y", "y")), ((1, 3), (3, 1))),
)
ATTN, MLP = 2048, 3072
WIDTHS = (ATTN, MLP)


def device_index(y, z, x, c):
    return (((y * 2 + z % 2) * 4 + x) * 2 + z // 2) * 2 + c


def flip_pairs(axes, flips):
    pairs = []
    for y in range(4):
        for z in range(4):
            for x in range(4):
                for c in range(2):
                    to = {"x": x, "y": y, "z": z}
                    to[axes[c]] ^= flips[c]
                    pairs.append(
                        (device_index(y, z, x, c), device_index(to["y"], to["z"], to["x"], c))
                    )
    return pairs


def core_swap(value):
    pairs = [(i, i ^ 1) for i in range(128)]
    return lax.ppermute(value, AXES, pairs)


class Links:
    def __init__(self):
        self.last = ()

    def __call__(self, values, axes, flips):
        values, _ = lax.optimization_barrier((tuple(values), self.last))
        out = tuple(
            lax.ppermute(v, AXES, flip_pairs(a, f)) for v, a, f in zip(values, axes, flips)
        )
        self.last = out
        return out


def ring_stage(send, blocks, stage, forward, between=None):
    a, b = blocks
    (p, q) = (PARTS[i][2][stage] for i in range(2))
    (s0, s1), (t0, t1) = (PARTS[i][3] for i in range(2))
    if not forward:
        an, bn, af, bf, ao, bo = send(
            (a, b, a, b, a, b), (p, q, p, q, p, q), (s0, t0, s1, t1, (2, 2), (2, 2))
        )
        return [[a, an, ao, af], [b, bn, bo, bf]]
    an, af, bn, bf = send((a, a, b, b), (p, p, q, q), (s0, s1, t0, t1))
    if between is not None:
        send.last = (send.last, between())
    half = a.shape[0] // 2
    al, ah, bl, bh = send(
        (an[:half], af[half:], bn[:half], bf[half:]), (p, p, q, q), (s1, s0, t1, t0)
    )
    return [[a, an, al, ah, af], [b, bn, bl, bh, bf]]


def fetch(coords, pieces, out, sem):
    own = {"y": coords[0], "z": coords[1], "x": coords[2]}
    core = coords[3]

    def choose(first, second):
        return jnp.where(core == 0, first, second)

    def row(axis, j):
        at = own[axis] ^ j
        if axis == "z":
            return lax.rem(at, 2) * 192
        return at * (384 if axis == "y" else 48)

    for part, (start, count, axes, steps) in enumerate(PARTS):
        rows, highs = [], []
        for axis in axes:
            swapped = steps[0][1] == 3
            far = [(j, (4 - j) % 4 if swapped else j) for j in range(4)]
            rows.append([choose(row(axis[0], u), row(axis[1], v)) for u, v in far])
            highs.append(
                [
                    choose(
                        lax.div(own["z"] ^ u, 2) if axis[0] == "z" else 0,
                        lax.div(own["z"] ^ v, 2) if axis[1] == "z" else 0,
                    )
                    for u, v in far
                ]
            )
        for q, (j3, k0, many) in enumerate(
            ((0, 0, 16), (1, 0, 16), (2, 0, 8), (2, 8, 8), (3, 0, 16))
        ):
            for k in range(many):
                j2, j1 = (k0 + k) // 4, (k0 + k) % 4
                first = rows[0][j1] + rows[1][j2] + rows[2][j3] + start
                high = highs[0][j1] + highs[1][j2] + highs[2][j3]
                pltpu.make_async_copy(
                    pieces[part * 5 + q].at[k],
                    out.at[high, pl.ds(pl.multiple_of(first, 16), count), :],
                    sem.at[high],
                ).start()


def ones_where(condition):
    return jnp.where(condition, 1.0, 0.0).astype(BF)


def iota2(rows, cols):
    return (
        lax.broadcasted_iota(jnp.int32, (rows, cols), 0),
        lax.broadcasted_iota(jnp.int32, (rows, cols), 1),
    )


def matmul(left, right):
    return jnp.dot(left, right, preferred_element_type=F32)


def inner_rows(left, right):
    return lax.dot_general(left, right, (((0,), (0,)), ((), ())), preferred_element_type=F32)


def inner_cols(left, right):
    return lax.dot_general(left, right, (((1,), (1,)), ((), ())), preferred_element_type=F32)


ROWS = 384
WIDE = 1536
LANES = 128
PART = WIDE + LANES
FACTOR = HEAD_DIM ** (-0.5)


def row_blocks(body):
    @pl.loop(0, ROWS // 128)
    def _(i):
        body(pl.ds(pl.multiple_of(i * 128, 128), 128))


def row_scale(values):
    return lax.rsqrt(jnp.mean(values * values, axis=-1, keepdims=True) + EPS)


def back_of_norm(inputs, gain, grad):
    scale = row_scale(inputs)
    weighted = gain * grad
    return scale * weighted - inputs * (
        scale * scale * scale * jnp.mean(inputs * weighted, axis=-1, keepdims=True)
    )


def live_rows(length, rows):
    at = lax.broadcasted_iota(jnp.int32, (128, 1), 0) + rows.start
    return at < length


def spin(values, cosine, sine):
    return values * cosine + pltpu.roll(values, 64, 1) * sine


def project_cols(out, parts, rank_parts):
    for n in range(2):
        cols = pl.ds(n * 768, 768)
        out[:, cols] = sum(inner_cols(left(), right(cols)) for left, right in parts).astype(BF)

    out[:, WIDE:] = sum(inner_cols(left(), right()) for left, right in rank_parts).astype(BF)


def attention_forward(ready, flush, coords, tok, gain, cosine, sine, *refs):
    pieces = refs[:10]
    w_far, ot_far, probs_far, ent, ent_gu, exits, x_gu, entry_o, e_down, x_od = refs[10:20]
    normed, ranks, q, k, v, att, part = refs[20:27]
    raw, w, ot, probs, sem = refs[27:]
    fetch(coords, pieces, raw, sem)
    chosen, length = coords[4], coords[5]

    def start(rows):
        x = tok[rows, :].astype(F32)
        normed[rows, :] = (x * row_scale(x) * gain[...]).astype(BF)

    row_blocks(start)
    i, j = iota2(384, 512)
    spread = ones_where(j == i + 16 * lax.div(i, 48))
    i, j = iota2(384, 128)
    picks = []
    for h in range(2):
        col = i + 320 * h
        third, rank = lax.div(col, 128), lax.rem(col, 16)
        ours = (lax.div(lax.rem(col, 128), 16) == chosen) & (i < 320)
        picks.append(
            (
                ones_where(ours & (third < 3) & (j == third * 16 + rank)),
                ones_where(ours & (third >= 3) & (j == (third - 3) * 16 + rank)),
            )
        )
    for h in range(2):
        pltpu.make_async_copy(raw.at[h], raw.at[h], sem.at[h]).wait()

    @pl.loop(0, 3)
    def _(n):
        rows = pl.ds(pl.multiple_of(n * 512, 512), 512)
        for h in range(2):
            for b in range(2):
                w[h, rows, b * 512 : b * 512 + 512] = matmul(
                    raw[h, rows, b * 384 : b * 384 + 384], spread
                ).astype(BF)
            ot[h, rows, :] = matmul(raw[h, rows, 768:1152], spread).astype(BF)
        for out, which in ((ent, 0), (ent_gu, 1)):
            out[rows, :] = sum(
                matmul(raw[h, rows, 1152:1536], picks[h][which]) for h in range(2)
            ).astype(BF)

    keep = [
        pltpu.make_async_copy(w, w_far, sem.at[2]),
        pltpu.make_async_copy(ot, ot_far, sem.at[3]),
    ]
    for copy in keep:
        copy.start()
    i, j = iota2(128, 192)
    lane = lax.broadcasted_iota(jnp.int32, (128, 512), 1)
    mine = pl.ds(pl.multiple_of(chosen * 192, 16), 192)
    for h in range(2):
        block = raw[h, mine, 1536:2048]

        def line(t, first):
            take = ones_where((j == 12 * (i - first) + t) & (i >= first) & (i < first + 16))
            return matmul(take, block).astype(BF)

        for t in range(2):
            x_gu[h, :, t * 512 : t * 512 + 512] = line(t, 0)
            x_gu[h, :, 1024 + t * 512 : 1536 + t * 512] = line(2 + t, 16)
            e_down[h, :, t * 512 : t * 512 + 512] = line(4 + t, 0)
        for t in range(3):
            x_od[h, :, t * 512 : t * 512 + 512] = line(6 + t, 0)
        exits[h, :, :512] = matmul(line(9, 0)[:, :384], spread).astype(BF)
        key = matmul(line(10, 16)[:, :384], spread)
        value = matmul(line(10, 32)[:, :384], spread)
        exits[h, :, 512:] = jnp.where(lane < 256, key, value).astype(BF)
        entry_o[h] = matmul(line(11, 0)[:, :384], spread).astype(BF)

    ranks[...] = matmul(normed[...], ent[...]).astype(BF)
    for h in range(2):
        for n in range(4):
            cols = slice(n * 256, n * 256 + 256)
            t = matmul(normed[...], w[h, :, cols]) + matmul(ranks[...], exits[h, :, cols])
            for i in range(2):
                head = t[:, i * 128 : i * 128 + 128]
                if n < 2:
                    q[h * 4 + n * 2 + i] = spin(head, cosine[...], sine[...]).astype(BF)
                elif n == 2:
                    k[h * 2 + i] = spin(head, cosine[...], sine[...]).astype(BF)
                else:
                    v[h * 2 + i] = head.astype(BF)
    at_q, at_k = iota2(ROWS, ROWS)
    allowed = (at_k <= at_q) & (at_k < length)
    for h in range(2):

        @pl.loop(0, 4)
        def _(i):
            g = h * 2 + i // 2
            s = inner_cols(q[h * 4 + i], k[g]) * FACTOR
            s = jnp.where(allowed, s, -1e30)
            e = jnp.exp(s - jnp.max(s, axis=-1, keepdims=True))
            p = e / jnp.sum(e, axis=-1, keepdims=True)
            probs[h * 4 + i] = p
            att[h, :, pl.ds(pl.multiple_of(i * 128, 128), 128)] = matmul(p.astype(BF), v[g]).astype(BF)

    flush(*range(3, 16))
    keep.append(pltpu.make_async_copy(probs, probs_far, sem.at[4]))
    keep[-1].start()
    project_cols(
        part,
        [(lambda h=h: att[h], lambda cols, h=h: ot[h, cols, :]) for h in range(2)],
        [(lambda h=h: att[h], lambda h=h: entry_o[h]) for h in range(2)],
    )
    for copy in keep:
        copy.wait()


def mlp_start(
    ready, flush, scalars, tok, own, other, cot, gain, exit_o, ent, exit_d,
    middle, rank_out, hidden, g2, ranks, drank,
):
    ready(0)

    def start(rows):
        total = own[rows, :].astype(F32) + other[rows, :].astype(F32)
        r = total[:, WIDE:].astype(BF)
        rank_out[rows, :] = r
        mid = tok[rows, :].astype(F32) + total[:, :WIDE] + matmul(r, exit_o[...])
        middle[rows, :] = mid
        hidden[rows, :] = (mid * row_scale(mid) * gain[...]).astype(BF)
        g2[rows, :] = jnp.where(live_rows(scalars[0], rows), cot[rows, :].astype(F32), 0.0).astype(BF)

    row_blocks(start)
    flush(0, 1, 2, 3)
    ranks[...] = matmul(hidden[...], ent[...]).astype(BF)
    drank[...] = inner_cols(g2[...], exit_d[...]).astype(BF)


def mlp(ready, flush, coords, hidden, g2, ranks, drank, exits, entry_d, *refs):
    pieces = refs[:10]
    parts, exit_grads, entry_grads = refs[10:13]
    grads, act, w, sem = refs[13:]
    fetch(coords, pieces, w, sem)
    ready(0)
    for h in range(2):
        pltpu.make_async_copy(w.at[h], w.at[h], sem.at[h]).wait()
        for n in range(4):
            cols = pl.ds(n * 256, 256)
            ups = pl.ds(n * 256 + 1024, 256)
            downs = pl.ds(n * 256 + 2048, 256)
            gate = matmul(hidden[...], w[h, :, cols]) + matmul(ranks[...], exits[h, :, cols])
            up = matmul(hidden[...], w[h, :, ups]) + matmul(ranks[...], exits[h, :, ups])
            grad = matmul(g2[...], w[h, :, downs]) + matmul(drank[...], entry_d[h, :, cols])
            sigma = 1.0 / (1.0 + jnp.exp(-gate))
            silu = gate * sigma
            act[h, :, cols] = (silu * up).astype(BF)
            grads[h, :, ups] = (grad * silu).astype(BF)
            grads[h, :, cols] = (grad * (up * sigma * (1.0 + gate - silu))).astype(BF)

    project_cols(
        parts.at[0],
        [(lambda h=h: grads[h], lambda cols, h=h: w[h, cols, :2048]) for h in range(2)],
        [(lambda h=h: grads[h], lambda h=h: exits[h]) for h in range(2)],
    )
    project_cols(
        parts.at[1],
        [(lambda h=h: act[h], lambda cols, h=h: w[h, cols, 2048:]) for h in range(2)],
        [(lambda h=h: act[h], lambda h=h: entry_d[h]) for h in range(2)],
    )
    flush(0)
    for h in range(2):
        exit_grads[h] = inner_rows(ranks[...], grads[h])[:32].astype(BF)
        entry_grads[h] = inner_rows(drank[...], act[h])[:16].astype(BF)


def attention_backward(
    ready, flush, scalars, g2, own, other, middle, gain, ent, exit_o, entry_o, exits, cosine, sine, q, k, v, probs, ot, w,
    own_down, other_down, exit_d, rank_out, hidden_in, ranks, att,
    grad_middle, part, mixed, exit_grads, entry_grads, shared, wide, mixed_half,
    g1, drank_gu, drank_out, grads, grad_att, sum_k, sum_v, rank_down, half_sem,
):
    ready(0)

    def start(rows):
        total = own[rows, :].astype(F32) + other[rows, :].astype(F32)
        d = total[:, WIDE:].astype(BF)
        drank_gu[rows, :] = d
        hidden = total[:, :WIDE] + inner_cols(d, ent[...])
        mid = g2[rows, :].astype(F32) + back_of_norm(middle[rows, :], gain[...], hidden)
        grad_middle[rows, :] = mid
        g1[rows, :] = mid.astype(BF)

    row_blocks(start)
    ready(1)
    drank_out[...] = inner_cols(g1[...], exit_o[...]).astype(BF)
    flush(0)
    for h in range(2):
        for n in range(2):
            cols = slice(n * 256, n * 256 + 256)
            t = matmul(g1[...], ot[h, :, cols]) + matmul(drank_out[...], entry_o[h, :, cols])
            for i in range(2):
                grad_att[h * 4 + n * 2 + i] = t[:, i * 128 : i * 128 + 128].astype(BF)
    ready(2)
    for h in range(2):

        @pl.loop(0, 2)
        def _(j):
            g = h * 2 + j
            for i in range(2):
                head = h * 4 + j * 2 + i
                p = probs[head]
                ga = grad_att[head]
                gp = inner_cols(ga, v[g])
                delta = jnp.sum(p * gp, axis=-1, keepdims=True)
                gs = (p * (gp - delta)).astype(BF)
                gq = matmul(gs, k[g]) * FACTOR
                grads[h, :, pl.ds(pl.multiple_of((j * 2 + i) * 128, 128), 128)] = spin(
                    gq, cosine[...], -sine[...]
                ).astype(BF)
                gk = inner_rows(gs, q[head])
                gv = inner_rows(p.astype(BF), ga)
                if i == 0:
                    sum_k[...] = gk
                    sum_v[...] = gv
                else:
                    gk = (sum_k[...] + gk) * FACTOR
                    gv = sum_v[...] + gv
                    grads[h, :, pl.ds(pl.multiple_of(512 + j * 128, 128), 128)] = spin(
                        gk, cosine[...], -sine[...]
                    ).astype(BF)
                    grads[h, :, pl.ds(pl.multiple_of(768 + j * 128, 128), 128)] = gv.astype(BF)

    ready(3)

    def finish(rows):
        total = own_down[rows, :].astype(F32) + other_down[rows, :].astype(F32)
        r = total[:, WIDE:].astype(BF)
        rank_down[rows, :] = r
        result = middle[rows, :] + total[:, :WIDE] + matmul(r, exit_d[...])
        mixed[rows, :] = jnp.where(live_rows(scalars[0], rows), result, 0.0).astype(BF)

    row_blocks(finish)
    flush(2)
    half = half_of(scalars, mixed, mixed_half, half_sem)
    project_cols(
        part,
        [(lambda h=h: grads[h], lambda cols, h=h: w[h, cols, :]) for h in range(2)],
        [(lambda h=h: grads[h], lambda h=h: exits[h]) for h in range(2)],
    )
    flush(1)
    for h in range(2):
        exit_grads[h] = inner_rows(ranks[...], grads[h])[:48].astype(BF)
        entry_grads[h] = inner_rows(drank_out[...], att[h])[:16].astype(BF)
    shared[0] = inner_rows(rank_out[...], g1[...])[:16].astype(BF)
    shared[1] = inner_rows(rank_down[...], g2[...])[:16].astype(BF)
    wide[...] = inner_rows(drank_gu[...], hidden_in[...])[:32].astype(BF)
    half.wait()


def half_of(scalars, value, out, sem):
    first = pl.multiple_of(scalars[1] * 192, 16)
    copy = pltpu.make_async_copy(value.at[pl.ds(first, 192), :], out, sem)
    copy.start()
    return copy


def pack(blocks):
    lane = lax.broadcasted_iota(jnp.int32, (48, 128), 1)
    full, last = [], blocks[1]
    for p in range(4):
        odd = blocks[2 * p + 1]
        full.append(jnp.where(lane < 80, blocks[2 * p], pltpu.roll(odd, 80, 1)))
        moved = pltpu.roll(odd, (32 * p - 48) % 128, 1)
        last = jnp.where((lane >= 32 * p) & (lane < 32 * p + 32), moved, last)
    return [*full, last]


def unpack(full, n):
    if n % 2 == 0:
        return full(n // 2)
    lane = lax.broadcasted_iota(jnp.int32, (48, 128), 1)
    first = pltpu.roll(full(n // 2), 48, 1)
    return jnp.where(lane < 48, first, pltpu.roll(full(4), (48 - 32 * (n // 2)) % 128, 1))


def input_backward(
    ready, flush, scalars, tok, own, other, grad_middle, gain, ent, normed, wide_gu, head,
    grad_in, lines, in_half,
    drank, half_sem,
):
    ready(0)

    def start(rows):
        total = own[rows, :].astype(F32) + other[rows, :].astype(F32)
        d = total[:, WIDE:].astype(BF)
        drank[rows, :] = d
        grad = total[:, :WIDE] + inner_cols(d, ent[...])
        back = back_of_norm(tok[rows, :].astype(F32), gain[...], grad)
        grad_in[rows, :] = (grad_middle[rows, :] + back).astype(BF)

    row_blocks(start)
    flush(0)
    half = half_of(scalars, grad_in, in_half, half_sem)
    ready(1)
    wide = jnp.concatenate(
        [
            inner_rows(drank[...], normed[...])[:48],
            wide_gu[...].astype(F32),
            jnp.zeros((48, WIDE), F32),
        ],
        axis=0,
    ).T
    for x in range(4):
        full = pack([wide[(d * 4 + x) * 48 : (d * 4 + x) * 48 + 48] for d in range(8)])
        for h in range(2):
            lines[h * 4 + x, :240, :] = head[h * 4 + x]
            for t in range(5):
                lines[h * 4 + x, 240 + t * 48 : 288 + t * 48, :] = full[t].astype(BF)
    flush(1)
    half.wait()


def regroup(ready, flush, adapters, got, out, total):
    total[...] = jnp.zeros_like(total)
    ready(0)
    for n in range(8):
        a = adapters[n]
        total[a] = total[a] + got[n].astype(F32)
    for d in range(8):
        out[d, :240, :] = total[d, :240].astype(BF)
        blocks = [
            unpack(lambda t, a=a: total[a, 240 + t * 48 : 288 + t * 48, :], d) for a in range(8)
        ]
        for t, tile in enumerate(pack(blocks)):
            out[d, 240 + t * 48 : 288 + t * 48, :] = tile.astype(BF)


def gather_gradients(ready, flush, final, g_q, g_k, g_v, g_gate, g_up, g_eo, g_ed, g_xo, g_xd, wide_qkv, wide_gu, total, kv):
    @pl.loop(0, 3)
    def _(i):
        rows = pl.ds(pl.multiple_of(i * 160, 16), 160)
        total[rows, :] = sum(final[g, rows, :].astype(F32) for g in range(8))

    at = 0
    for out, blocks in ((g_q, 3), (kv, 3), (g_gate, 8), (g_up, 8), (g_eo, 3), (g_ed, 8)):
        for n in range(blocks):
            for r in range(4):
                line = r * 33 + at + n
                out[r : r + 1, n * 128 : n * 128 + 128] = total[line : line + 1, :]
        at += blocks
    both_kv = kv[...]
    g_k[...] = both_kv[:, :192]
    g_v[...] = both_kv[:, 192:]
    for m, out in enumerate((g_xo, g_xd)):
        for n in range(12):
            for r in range(4):
                line = 132 + r * 24 + m * 12 + n
                out[r : r + 1, n * 128 : n * 128 + 128] = total[line : line + 1, :]
    lane = lax.broadcasted_iota(jnp.int32, (48, 128), 1)
    for third in range(5):
        columns = jnp.zeros((48, 128), F32)
        for a in range(8):
            block = unpack(lambda t: total[240 + 48 * t : 288 + 48 * t, :], a)
            moved = pltpu.roll(block, (a * 16 - third * 16) % 128, 1)
            columns = jnp.where((lane >= a * 16) & (lane < a * 16 + 16), moved, columns)
        out, n = (wide_qkv, third) if third < 3 else (wide_gu, third - 3)
        out[:, n * 128 : n * 128 + 128] = columns


def shaped(*extent, dtype=BF):
    return jax.ShapeDtypeStruct(extent, dtype)


def call(
    body, args, outs, flops, scratch=(), scalars=(), far_in=(), far_out=(), late=None, sent=()
):
    whole = pl.BlockSpec(memory_space=pltpu.VMEM)
    small = pl.BlockSpec(memory_space=pltpu.SMEM)
    far = pl.BlockSpec(memory_space=pltpu.HBM)
    late = late or {}
    order = sorted(late, key=lambda i: late[i])
    block = [a[1] if isinstance(a, tuple) else None for a in args]
    args = [a[0] if isinstance(a, tuple) else a for a in args]
    shapes = [a.shape if i is None else a.shape[1:] for a, i in zip(args, block)]
    extra = len(order) + len(sent) + 2

    def kernel(*refs):
        spare, sem, out_sem = refs[len(refs) - extra : -2], refs[-2], refs[-1]
        refs = list(refs[: len(refs) - extra])
        copies = []
        for n, i in enumerate(order):
            source = refs[i] if block[i] is None else refs[i].at[block[i]]
            copies.append(pltpu.make_async_copy(source, spare[n], sem.at[n]))
            copies[-1].start()
            refs[i] = spare[n]
        leaving = {}
        for n, i in enumerate(sent):
            held = spare[len(order) + n]
            leaving[i] = pltpu.make_async_copy(held, refs[len(args) + i], out_sem.at[n])
            refs[len(args) + i] = held

        def ready(group):
            for n, i in enumerate(order):
                if late[i] == group:
                    copies[n].wait()

        started = []

        def flush(*which):
            for i in which:
                leaving[i].start()
                started.append(i)

        body(ready, flush, *refs)
        flush(*(i for i in sent if i not in started))
        for i in sent:
            leaving[i].wait()

    spares = [pltpu.VMEM(shapes[i], args[i].dtype) for i in order]
    spares += [pltpu.VMEM(outs[i].shape, outs[i].dtype) for i in sent]
    spares.append(pltpu.SemaphoreType.DMA((max(1, len(order)),)))
    spares.append(pltpu.SemaphoreType.DMA((max(1, len(sent)),)))
    return pl.pallas_call(
        kernel,
        out_shape=list(outs),
        in_specs=[
            small if i in scalars else far if i in far_in or i in late else whole
            for i in range(len(args))
        ],
        out_specs=[far if i in far_out or i in sent else whole for i in range(len(outs))],
        scratch_shapes=[*scratch, *spares],
        compiler_params=pltpu.CompilerParams(vmem_limit_bytes=59 << 20),
        cost_estimate=pl.CostEstimate(
            flops=int(flops),
            transcendentals=0,
            bytes_accessed=sum(a.size * a.dtype.itemsize for a in args),
        ),
    )(*args)


def lookup(table, index):
    return jnp.sum(jnp.where(jnp.arange(table.shape[0]) == index, table, 0))


def rope_tables(first):
    half = HEAD_DIM // 2
    freq = jnp.power(THETA, -2.0 * jnp.arange(half, dtype=F32) / HEAD_DIM)
    angle = (jnp.arange(ROWS) + first).astype(F32)[:, None] * freq[None, :]
    cosine, sine, pad = jnp.cos(angle), jnp.sin(angle), jnp.zeros((ROWS, 16), F32)
    return (
        jnp.concatenate([cosine, pad, cosine, pad], axis=1),
        jnp.concatenate([-sine, pad, sine, pad], axis=1),
    )


def cut_heads(array):
    lead = array.shape[:-1]
    return array.reshape(*lead, -1, 64)[..., :48].reshape(*lead, -1)


def per_device(
    tokens,
    cotangent,
    lengths,
    dealing,
    adapter_choice,
    attention_gain,
    feedforward_gain,
    query_weight,
    key_weight,
    value_weight,
    output_weight,
    gate_weight,
    up_weight,
    down_weight,
    entry_qkv,
    exit_query,
    exit_key,
    exit_value,
    entry_out,
    exit_out,
    entry_gate_up,
    exit_gate,
    exit_up,
    entry_down,
    exit_down,
):
    y, zl, x, zh, core = (lax.axis_index(a) for a in AXES)
    own_high = zh == 0
    entries = jnp.concatenate([entry_qkv, entry_gate_up], axis=1)
    entries = jnp.where(own_high, entries[:, :320], entries[:, 320:])
    pad = jnp.zeros((4, 128), BF)
    exits = jnp.concatenate(
        [
            exit_gate,
            exit_up,
            entry_down.T,
            jnp.where(own_high, exit_out, exit_down),
            exit_query,
            pad,
            exit_key,
            exit_value,
            pad,
            entry_out.T,
            pad,
        ],
        axis=1,
    ).reshape(48, 512)
    payload = jnp.concatenate(
        [
            query_weight,
            key_weight,
            value_weight,
            output_weight.T,
            entries,
            jnp.zeros((48, 64), BF),
            exits,
            gate_weight,
            up_weight,
            down_weight.T,
        ],
        axis=1,
    )
    send = Links()
    blocks = [payload[None, first : first + count] for first, count, _, _ in PARTS]
    blocks = [jnp.concatenate(p, 0) for p in ring_stage(send, blocks, 0, False)]
    zero, tokens, cotangent, lengths, dealing, adapter_choice, _ = lax.optimization_barrier(
        (jnp.int32(0), tokens, cotangent, lengths, dealing, adapter_choice, send.last)
    )
    slot = ((y * 2 + zl) * 4 + x) * 2 + zh
    sequence = lookup(dealing, slot)
    length = lookup(lengths, sequence)
    chosen = lookup(adapter_choice, sequence)
    coords = jnp.stack([y, zh * 2 + zl, x, core, chosen, length]).astype(jnp.int32)
    second = ring_stage(send, blocks, 1, True)

    def group(start, width):
        return [jnp.concatenate([q[:, :, start : start + width] for q in p], 0) for p in second]

    rows = lax.dynamic_index_in_dim(tokens, zh, 0, keepdims=False)
    cot = lax.dynamic_index_in_dim(cotangent, zh, 0, keepdims=False)
    cosine, sine = rope_tables(zero)
    scalars = jnp.stack([length, core]).astype(jnp.int32)
    gain1, gain2 = attention_gain[None], feedforward_gain[None]
    peers = ((y * 2 + zl) * 4 + jnp.tile(jnp.arange(4), 2)) * 2 + jnp.repeat(jnp.arange(2), 4)
    match = (jnp.arange(64)[None, :] == peers[:, None]).astype(jnp.int32)
    peer_seq = jnp.sum(match * dealing[None, :], axis=1)
    match = (jnp.arange(64)[None, :] == peer_seq[:, None]).astype(jnp.int32)
    peer_adapter = jnp.sum(match * adapter_choice[None, :], axis=1).astype(jnp.int32)
    early = (coords, rows, cot, cosine, sine, scalars, gain1, gain2, peer_adapter)
    early = lax.optimization_barrier(early)
    coords, rows, cot, cosine, sine, scalars, gain1, gain2, peer_adapter = early
    send.last = (send.last, early)
    attn_pieces = sum(ring_stage(send, group(0, ATTN), 2, True), [])
    (
        w_qkv, w_out, probs, ent_qkv, ent_gu, x_qkv, x_gu, e_out, e_down, x_od,
        normed, ranks, q, k, v, att, part,
    ) = call(
        attention_forward,
        (coords, rows, gain1, cosine, sine, *attn_pieces),
        (
            shaped(2, WIDE, 1024),
            shaped(2, WIDE, 512),
            shaped(8, ROWS, ROWS, dtype=F32),
            shaped(WIDE, LANES),
            shaped(WIDE, LANES),
            shaped(2, LANES, 1024),
            shaped(2, LANES, 2048),
            shaped(2, LANES, 512),
            shaped(2, LANES, 1024),
            shaped(2, LANES, WIDE),
            shaped(ROWS, WIDE),
            shaped(ROWS, LANES),
            shaped(8, ROWS, LANES),
            shaped(4, ROWS, LANES),
            shaped(4, ROWS, LANES),
            shaped(2, ROWS, 512),
            shaped(ROWS, PART),
        ),
        12e9,
        scratch=(
            pltpu.VMEM((2, WIDE, ATTN), BF),
            pltpu.VMEM((2, WIDE, 1024), BF),
            pltpu.VMEM((2, WIDE, 512), BF),
            pltpu.VMEM((8, ROWS, ROWS), F32),
            pltpu.SemaphoreType.DMA((5,)),
        ),
        scalars=(0,),
        far_in=tuple(range(5, 15)),
        far_out=(0, 1, 2),
        sent=tuple(range(3, 17)),
    )
    x_out, x_down = x_od[0], x_od[1]
    mlp_pieces = sum(ring_stage(send, group(ATTN, MLP), 2, True, lambda: part), [])
    middle, rank_out, hidden, g2, ranks_gu, drank_down = call(
        mlp_start,
        (scalars, rows, part, core_swap(part), cot, gain2, x_out, ent_gu, x_down),
        (
            shaped(ROWS, WIDE, dtype=F32),
            shaped(ROWS, LANES),
            shaped(ROWS, WIDE),
            shaped(ROWS, WIDE),
            shaped(ROWS, LANES),
            shaped(ROWS, LANES),
        ),
        1e9,
        scalars=(0,),
        late={1: 0, 2: 0, 3: 0, 4: 0, 6: 0, 7: 0, 8: 0},
        sent=(0, 1, 2, 3, 4, 5),
    )
    parts, gx_gu, ge_down = call(
        mlp,
        (coords, hidden, g2, ranks_gu, drank_down, x_gu, e_down, *mlp_pieces),
        (shaped(2, ROWS, PART), shaped(2, 32, 2048), shaped(2, 16, 1024)),
        15e9,
        scratch=(
            pltpu.VMEM((2, ROWS, 2048), BF),
            pltpu.VMEM((2, ROWS, 1024), BF),
            pltpu.VMEM((2, WIDE, MLP), BF),
            pltpu.SemaphoreType.DMA((2,)),
        ),
        scalars=(0,),
        far_in=tuple(range(7, 17)),
        late={1: 0, 2: 0, 3: 0, 4: 0, 5: 0, 6: 0},
        sent=(0, 1, 2),
    )
    others = core_swap(parts)
    grad_middle, part_qkv, mixed, gx_qkv, ge_out, shared, wide_gu, mixed_half = call(
        attention_backward,
        (
            scalars, g2, (parts, 0), (others, 0), middle, gain2, ent_gu, x_out, e_out, x_qkv, cosine, sine,
            q, k, v, probs, w_out, w_qkv, (parts, 1), (others, 1), x_down, rank_out, hidden, ranks, att,
        ),
        (
            shaped(ROWS, WIDE, dtype=F32),
            shaped(ROWS, PART),
            shaped(ROWS, WIDE),
            shaped(2, 48, 1024),
            shaped(2, 16, 512),
            shaped(2, 16, WIDE),
            shaped(32, WIDE),
            shaped(192, WIDE),
        ),
        8e9,
        scratch=(
            pltpu.VMEM((ROWS, WIDE), BF),
            pltpu.VMEM((ROWS, LANES), BF),
            pltpu.VMEM((ROWS, LANES), BF),
            pltpu.VMEM((2, ROWS, 1024), BF),
            pltpu.VMEM((8, ROWS, LANES), BF),
            pltpu.VMEM((ROWS, LANES), F32),
            pltpu.VMEM((ROWS, LANES), F32),
            pltpu.VMEM((ROWS, LANES), BF),
            pltpu.SemaphoreType.DMA(()),
        ),
        scalars=(0,),
        far_out=(7,),
        late={
            1: 0, 2: 0, 3: 0, 4: 0, 6: 0, 7: 1, 8: 1, 16: 1, 10: 2, 11: 2, 12: 2, 13: 2, 14: 2, 15: 2,
            9: 3, 17: 3, 18: 3, 19: 3, 20: 3, 21: 3, 22: 3, 23: 3, 24: 3,
        },
        sent=(0, 1, 2, 3, 4, 5, 6),
    )
    other_qkv = core_swap(part_qkv)
    columns = jnp.concatenate(
        [
            cut_heads(gx_qkv[:, :16, :512]),
            cut_heads(gx_qkv[:, 16:32, 512:768]),
            cut_heads(gx_qkv[:, 32:48, 768:]),
            gx_gu[:, :16, :1024],
            gx_gu[:, 16:, 1024:],
            cut_heads(ge_out),
            ge_down,
        ],
        axis=2,
    )
    shared = jnp.concatenate([shared[0], shared[1]], axis=1)
    head = jnp.concatenate(
        [
            columns.reshape(2, 4, 132, 128),
            jnp.broadcast_to(shared.reshape(1, 4, 96, 128), (2, 4, 96, 128)),
            jnp.zeros((2, 4, 12, 128), BF),
        ],
        axis=2,
    ).reshape(8, 240, 128)
    grad_in, lines, in_half = call(
        input_backward,
        (scalars, rows, part_qkv, other_qkv, grad_middle, gain1, ent_qkv, normed, wide_gu, head),
        (shaped(ROWS, WIDE), shaped(8, 480, 128), shaped(192, WIDE)),
        1e9,
        scratch=(pltpu.VMEM((ROWS, LANES), BF), pltpu.SemaphoreType.DMA(())),
        scalars=(0,),
        far_out=(2,),
        late={1: 0, 2: 0, 3: 0, 4: 0, 6: 0, 7: 1, 8: 1, 9: 1},
        sent=(0, 1),
    )
    to_other_chip = flip_pairs("zz", (2, 2))
    sent_mixed = lax.ppermute(mixed_half, AXES, to_other_chip)
    sent_in = lax.ppermute(in_half, AXES, to_other_chip)
    lines, sent_mixed = lax.optimization_barrier((lines, sent_mixed))
    got = lax.all_to_all(lines, ("zh", "x"), 0, 0, tiled=True)
    (second,) = call(
        regroup,
        (peer_adapter, got),
        (shaped(8, 480, 128),),
        1e6,
        scratch=(pltpu.VMEM((8, 480, 128), F32),),
        scalars=(0,),
        late={1: 0},
        sent=(0,),
    )
    final = lax.all_to_all(second, ("y", "zl"), 0, 0, tiled=True)

    def share(value, got):
        rest = core_swap(got)
        first, second = jnp.where(core == 0, got, rest), jnp.where(core == 0, rest, got)
        other = jnp.concatenate([first, second], axis=0)
        return jnp.stack([jnp.where(own_high, value, other), jnp.where(own_high, other, value)])

    mixed, grad_in = share(mixed, sent_mixed), share(grad_in, sent_in)
    final, mixed, grad_in = lax.optimization_barrier((final, mixed, grad_in))
    g_q, g_k, g_v, g_gate, g_up, g_eo, g_ed, g_xo, g_xd, wide_qkv, wide_gu = call(
        gather_gradients,
        (final,),
        (
            shaped(4, 384, dtype=F32),
            shaped(4, 192, dtype=F32),
            shaped(4, 192, dtype=F32),
            shaped(4, 1024, dtype=F32),
            shaped(4, 1024, dtype=F32),
            shaped(4, 384, dtype=F32),
            shaped(4, 1024, dtype=F32),
            shaped(4, WIDE, dtype=F32),
            shaped(4, WIDE, dtype=F32),
            shaped(48, 384, dtype=F32),
            shaped(48, 256, dtype=F32),
        ),
        1e6,
        scratch=(pltpu.VMEM((480, LANES), F32), pltpu.VMEM((4, 384), F32)),
    )

    return (
        mixed,
        grad_in,
        wide_qkv,
        g_q,
        g_k,
        g_v,
        g_eo.T,
        g_xo,
        wide_gu,
        g_gate,
        g_up,
        g_ed.T,
        g_xd,
    )


def solution(mesh):
    fine = Mesh(mesh.devices.reshape(SIZES), AXES)
    dp, mp = ("y", "zl", "x"), ("zh", "c")
    return jax.shard_map(
        per_device,
        mesh=fine,
        in_specs=(
            P(dp, None, None),
            P(dp, None, None),
            P(),
            P(),
            P(),
            P(),
            P(),
            P(dp, mp),
            P(dp, mp),
            P(dp, mp),
            P(mp, dp),
            P(dp, mp),
            P(dp, mp),
            P(mp, dp),
            P(dp, None),
            P(dp, mp),
            P(dp, mp),
            P(dp, mp),
            P(mp, dp),
            P(dp, None),
            P(dp, None),
            P(dp, mp),
            P(dp, mp),
            P(mp, dp),
            P(dp, None),
        ),
        out_specs=(
            P(dp, None, None),
            P(dp, None, None),
            P(dp, None),
            P(dp, mp),
            P(dp, mp),
            P(dp, mp),
            P(mp, dp),
            P(dp, None),
            P(dp, None),
            P(dp, mp),
            P(dp, mp),
            P(mp, dp),
            P(dp, None),
        ),
        check_vma=False,
    )
```

```python
import jax
import jax.numpy as jnp
from jax import lax
from jax.experimental import pallas as pl
from jax.experimental.pallas import tpu as pltpu
from jax.sharding import Mesh, PartitionSpec as P

HEAD_DIM = 96
RANK = 16
EPS = 1e-05
THETA = 100000.0
BF = jnp.bfloat16
F32 = jnp.float32

AXES = ("y", "zl", "x", "zh", "c")
SIZES = (4, 2, 4, 2, 2)
PARTS = (
    (0, 32, (("z", "y"), ("y", "x"), ("x", "z")), ((1, 1), (3, 3))),
    (32, 16, (("x", "x"), ("z", "z"), ("y", "y")), ((1, 3), (3, 1))),
)
ATTN, MLP = 2048, 3072
WIDTHS = (ATTN, MLP)


def device_index(y, z, x, c):
    return (((y * 2 + z % 2) * 4 + x) * 2 + z // 2) * 2 + c


def flip_pairs(axes, flips):
    pairs = []
    for y in range(4):
        for z in range(4):
            for x in range(4):
                for c in range(2):
                    to = {"x": x, "y": y, "z": z}
                    to[axes[c]] ^= flips[c]
                    pairs.append(
                        (device_index(y, z, x, c), device_index(to["y"], to["z"], to["x"], c))
                    )
    return pairs


def core_swap(value):
    pairs = [(i, i ^ 1) for i in range(128)]
    return lax.ppermute(value, AXES, pairs)


class Links:
    def __init__(self):
        self.last = ()

    def __call__(self, values, axes, flips):
        values, _ = lax.optimization_barrier((tuple(values), self.last))
        out = tuple(
            lax.ppermute(v, AXES, flip_pairs(a, f)) for v, a, f in zip(values, axes, flips)
        )
        self.last = out
        return out


def ring_stage(send, blocks, stage, forward, between=None):
    a, b = blocks
    (p, q) = (PARTS[i][2][stage] for i in range(2))
    (s0, s1), (t0, t1) = (PARTS[i][3] for i in range(2))
    if not forward:
        an, bn, af, bf, ao, bo = send(
            (a, b, a, b, a, b), (p, q, p, q, p, q), (s0, t0, s1, t1, (2, 2), (2, 2))
        )
        return [[a, an, ao, af], [b, bn, bo, bf]]
    an, af, bn, bf = send((a, a, b, b), (p, p, q, q), (s0, s1, t0, t1))
    if between is not None:
        send.last = (send.last, between())
    half = a.shape[0] // 2
    al, ah, bl, bh = send(
        (an[:half], af[half:], bn[:half], bf[half:]), (p, p, q, q), (s1, s0, t1, t0)
    )
    return [[a, an, al, ah, af], [b, bn, bl, bh, bf]]


def fetch(coords, pieces, out, sem):
    own = {"y": coords[0], "z": coords[1], "x": coords[2]}

    def start_all(core):
        for high in range(2):
            for part, (start, count, axes, steps) in enumerate(PARTS):
                swapped = core == 1 and steps[0][1] == 3
                for q, (j3, k0, many) in enumerate(
                    ((0, 0, 16), (1, 0, 16), (2, 0, 8), (2, 8, 8), (3, 0, 16))
                ):
                    for k in range(many):
                        labels = ((k0 + k) % 4, (k0 + k) // 4, j3)
                        far = {
                            axis[core]: (4 - j) % 4 if swapped else j
                            for axis, j in zip(axes, labels)
                        }
                        if far["z"] // 2 != high:
                            continue
                        at = {axis: own[axis] ^ j for axis, j in far.items()}
                        first = (
                            at["y"] * 384 + lax.rem(at["z"], 2) * 192 + at["x"] * 48 + start
                        )
                        pltpu.make_async_copy(
                            pieces[part * 5 + q].at[k],
                            out.at[lax.div(at["z"], 2), pl.ds(pl.multiple_of(first, 16), count), :],
                            sem.at[high],
                        ).start()

    for core in range(2):

        @pl.when(coords[3] == core)
        def _():
            start_all(core)


def ones_where(condition):
    return jnp.where(condition, 1.0, 0.0).astype(BF)


def iota2(rows, cols):
    return (
        lax.broadcasted_iota(jnp.int32, (rows, cols), 0),
        lax.broadcasted_iota(jnp.int32, (rows, cols), 1),
    )


def matmul(left, right):
    return jnp.dot(left, right, preferred_element_type=F32)


def inner_rows(left, right):
    return lax.dot_general(left, right, (((0,), (0,)), ((), ())), preferred_element_type=F32)


def inner_cols(left, right):
    return lax.dot_general(left, right, (((1,), (1,)), ((), ())), preferred_element_type=F32)


ROWS = 384
WIDE = 1536
LANES = 128
PART = WIDE + LANES
FACTOR = HEAD_DIM ** (-0.5)


def row_blocks(body):
    @pl.loop(0, ROWS // 128)
    def _(i):
        body(pl.ds(pl.multiple_of(i * 128, 128), 128))


def row_scale(values):
    return lax.rsqrt(jnp.mean(values * values, axis=-1, keepdims=True) + EPS)


def back_of_norm(inputs, gain, grad):
    scale = row_scale(inputs)
    weighted = gain * grad
    return scale * weighted - inputs * (
        scale * scale * scale * jnp.mean(inputs * weighted, axis=-1, keepdims=True)
    )


def live_rows(length, rows):
    at = lax.broadcasted_iota(jnp.int32, (128, 1), 0) + rows.start
    return at < length


def spin(values, cosine, sine):
    return values * cosine + pltpu.roll(values, 64, 1) * sine


def project_cols(out, parts, rank_parts):
    for n in range(2):
        cols = pl.ds(n * 768, 768)
        out[:, cols] = sum(inner_cols(left(), right(cols)) for left, right in parts).astype(BF)

    out[:, WIDE:] = sum(inner_cols(left(), right()) for left, right in rank_parts).astype(BF)


def attention_forward(ready, flush, coords, tok, gain, cosine, sine, *refs):
    pieces = refs[:10]
    w_far, ot_far, probs_far, ent, ent_gu, exits, x_gu, entry_o, e_down, x_od = refs[10:20]
    normed, ranks, q, k, v, att, part = refs[20:27]
    raw, w, ot, probs, sem = refs[27:]
    fetch(coords, pieces, raw, sem)
    chosen, length = coords[4], coords[5]

    def start(rows):
        x = tok[rows, :].astype(F32)
        normed[rows, :] = (x * row_scale(x) * gain[...]).astype(BF)

    row_blocks(start)
    i, j = iota2(384, 512)
    spread = ones_where(j == i + 16 * lax.div(i, 48))
    i, j = iota2(384, 128)
    picks = []
    for h in range(2):
        col = i + 320 * h
        third, rank = lax.div(col, 128), lax.rem(col, 16)
        ours = (lax.div(lax.rem(col, 128), 16) == chosen) & (i < 320)
        picks.append(
            (
                ones_where(ours & (third < 3) & (j == third * 16 + rank)),
                ones_where(ours & (third >= 3) & (j == (third - 3) * 16 + rank)),
            )
        )
    for h in range(2):
        pltpu.make_async_copy(raw.at[h], raw.at[h], sem.at[h]).wait()

    @pl.loop(0, 3)
    def _(n):
        rows = pl.ds(pl.multiple_of(n * 512, 512), 512)
        for h in range(2):
            for b in range(2):
                w[h, rows, b * 512 : b * 512 + 512] = matmul(
                    raw[h, rows, b * 384 : b * 384 + 384], spread
                ).astype(BF)
            ot[h, rows, :] = matmul(raw[h, rows, 768:1152], spread).astype(BF)
        for out, which in ((ent, 0), (ent_gu, 1)):
            out[rows, :] = sum(
                matmul(raw[h, rows, 1152:1536], picks[h][which]) for h in range(2)
            ).astype(BF)

    keep = [
        pltpu.make_async_copy(w, w_far, sem.at[2]),
        pltpu.make_async_copy(ot, ot_far, sem.at[3]),
    ]
    for copy in keep:
        copy.start()
    i, j = iota2(128, 192)
    lane = lax.broadcasted_iota(jnp.int32, (128, 512), 1)
    mine = pl.ds(pl.multiple_of(chosen * 192, 16), 192)
    for h in range(2):
        block = raw[h, mine, 1536:2048]

        def line(t, first):
            take = ones_where((j == 12 * (i - first) + t) & (i >= first) & (i < first + 16))
            return matmul(take, block).astype(BF)

        for t in range(2):
            x_gu[h, :, t * 512 : t * 512 + 512] = line(t, 0)
            x_gu[h, :, 1024 + t * 512 : 1536 + t * 512] = line(2 + t, 16)
            e_down[h, :, t * 512 : t * 512 + 512] = line(4 + t, 0)
        for t in range(3):
            x_od[h, :, t * 512 : t * 512 + 512] = line(6 + t, 0)
        exits[h, :, :512] = matmul(line(9, 0)[:, :384], spread).astype(BF)
        key = matmul(line(10, 16)[:, :384], spread)
        value = matmul(line(10, 32)[:, :384], spread)
        exits[h, :, 512:] = jnp.where(lane < 256, key, value).astype(BF)
        entry_o[h] = matmul(line(11, 0)[:, :384], spread).astype(BF)

    ranks[...] = matmul(normed[...], ent[...]).astype(BF)
    for h in range(2):
        for n in range(4):
            cols = slice(n * 256, n * 256 + 256)
            t = matmul(normed[...], w[h, :, cols]) + matmul(ranks[...], exits[h, :, cols])
            for i in range(2):
                head = t[:, i * 128 : i * 128 + 128]
                if n < 2:
                    q[h * 4 + n * 2 + i] = spin(head, cosine[...], sine[...]).astype(BF)
                elif n == 2:
                    k[h * 2 + i] = spin(head, cosine[...], sine[...]).astype(BF)
                else:
                    v[h * 2 + i] = head.astype(BF)
    at_q, at_k = iota2(ROWS, ROWS)
    allowed = (at_k <= at_q) & (at_k < length)
    for h in range(2):

        @pl.loop(0, 4)
        def _(i):
            g = h * 2 + i // 2
            s = inner_cols(q[h * 4 + i], k[g]) * FACTOR
            s = jnp.where(allowed, s, -1e30)
            e = jnp.exp(s - jnp.max(s, axis=-1, keepdims=True))
            p = e / jnp.sum(e, axis=-1, keepdims=True)
            probs[h * 4 + i] = p
            att[h, :, pl.ds(pl.multiple_of(i * 128, 128), 128)] = matmul(p.astype(BF), v[g]).astype(BF)

    flush(*range(3, 16))
    keep.append(pltpu.make_async_copy(probs, probs_far, sem.at[4]))
    keep[-1].start()
    project_cols(
        part,
        [(lambda h=h: att[h], lambda cols, h=h: ot[h, cols, :]) for h in range(2)],
        [(lambda h=h: att[h], lambda h=h: entry_o[h]) for h in range(2)],
    )
    for copy in keep:
        copy.wait()


def mlp_start(
    ready, flush, scalars, tok, own, other, cot, gain, exit_o, ent, exit_d,
    middle, rank_out, hidden, g2, ranks, drank,
):
    ready(0)

    def start(rows):
        total = own[rows, :].astype(F32) + other[rows, :].astype(F32)
        r = total[:, WIDE:].astype(BF)
        rank_out[rows, :] = r
        mid = tok[rows, :].astype(F32) + total[:, :WIDE] + matmul(r, exit_o[...])
        middle[rows, :] = mid
        hidden[rows, :] = (mid * row_scale(mid) * gain[...]).astype(BF)
        g2[rows, :] = jnp.where(live_rows(scalars[0], rows), cot[rows, :].astype(F32), 0.0).astype(BF)

    row_blocks(start)
    flush(0, 1, 2, 3)
    ranks[...] = matmul(hidden[...], ent[...]).astype(BF)
    drank[...] = inner_cols(g2[...], exit_d[...]).astype(BF)


def mlp(ready, flush, coords, hidden, g2, ranks, drank, exits, entry_d, *refs):
    pieces = refs[:10]
    parts, exit_grads, entry_grads = refs[10:13]
    grads, act, w, sem = refs[13:]
    fetch(coords, pieces, w, sem)
    ready(0)
    for step in range(2):
        h = lax.rem(lax.div(coords[1], 2) + step, 2)
        pltpu.make_async_copy(w.at[h], w.at[h], sem.at[step]).wait()
        for n in range(4):
            cols = pl.ds(n * 256, 256)
            ups = pl.ds(n * 256 + 1024, 256)
            downs = pl.ds(n * 256 + 2048, 256)
            gate = matmul(hidden[...], w[h, :, cols]) + matmul(ranks[...], exits[h, :, cols])
            up = matmul(hidden[...], w[h, :, ups]) + matmul(ranks[...], exits[h, :, ups])
            grad = matmul(g2[...], w[h, :, downs]) + matmul(drank[...], entry_d[h, :, cols])
            sigma = 1.0 / (1.0 + jnp.exp(-gate))
            silu = gate * sigma
            act[h, :, cols] = (silu * up).astype(BF)
            grads[h, :, ups] = (grad * silu).astype(BF)
            grads[h, :, cols] = (grad * (up * sigma * (1.0 + gate - silu))).astype(BF)

    project_cols(
        parts.at[0],
        [(lambda h=h: grads[h], lambda cols, h=h: w[h, cols, :2048]) for h in range(2)],
        [(lambda h=h: grads[h], lambda h=h: exits[h]) for h in range(2)],
    )
    project_cols(
        parts.at[1],
        [(lambda h=h: act[h], lambda cols, h=h: w[h, cols, 2048:]) for h in range(2)],
        [(lambda h=h: act[h], lambda h=h: entry_d[h]) for h in range(2)],
    )
    flush(0)
    for h in range(2):
        exit_grads[h] = inner_rows(ranks[...], grads[h])[:32].astype(BF)
        entry_grads[h] = inner_rows(drank[...], act[h])[:16].astype(BF)


def attention_backward(
    ready, flush, scalars, g2, own, other, middle, gain, ent, exit_o, entry_o, exits, cosine, sine, q, k, v, probs, ot, w,
    own_down, other_down, exit_d, rank_out, hidden_in, ranks, att,
    grad_middle, part, mixed, exit_grads, entry_grads, shared, wide, mixed_half,
    g1, drank_gu, drank_out, grads, grad_att, sum_k, sum_v, rank_down, half_sem,
):
    ready(0)

    def start(rows):
        total = own[rows, :].astype(F32) + other[rows, :].astype(F32)
        d = total[:, WIDE:].astype(BF)
        drank_gu[rows, :] = d
        hidden = total[:, :WIDE] + inner_cols(d, ent[...])
        mid = g2[rows, :].astype(F32) + back_of_norm(middle[rows, :], gain[...], hidden)
        grad_middle[rows, :] = mid
        g1[rows, :] = mid.astype(BF)

    row_blocks(start)
    ready(1)
    drank_out[...] = inner_cols(g1[...], exit_o[...]).astype(BF)
    flush(0)
    for h in range(2):
        for n in range(2):
            cols = slice(n * 256, n * 256 + 256)
            t = matmul(g1[...], ot[h, :, cols]) + matmul(drank_out[...], entry_o[h, :, cols])
            for i in range(2):
                grad_att[h * 4 + n * 2 + i] = t[:, i * 128 : i * 128 + 128].astype(BF)
    ready(2)
    for h in range(2):

        @pl.loop(0, 2)
        def _(j):
            g = h * 2 + j
            for i in range(2):
                head = h * 4 + j * 2 + i
                p = probs[head]
                ga = grad_att[head]
                gp = inner_cols(ga, v[g])
                delta = jnp.sum(p * gp, axis=-1, keepdims=True)
                gs = (p * (gp - delta)).astype(BF)
                gq = matmul(gs, k[g]) * FACTOR
                grads[h, :, pl.ds(pl.multiple_of((j * 2 + i) * 128, 128), 128)] = spin(
                    gq, cosine[...], -sine[...]
                ).astype(BF)
                gk = inner_rows(gs, q[head])
                gv = inner_rows(p.astype(BF), ga)
                if i == 0:
                    sum_k[...] = gk
                    sum_v[...] = gv
                else:
                    gk = (sum_k[...] + gk) * FACTOR
                    gv = sum_v[...] + gv
                    grads[h, :, pl.ds(pl.multiple_of(512 + j * 128, 128), 128)] = spin(
                        gk, cosine[...], -sine[...]
                    ).astype(BF)
                    grads[h, :, pl.ds(pl.multiple_of(768 + j * 128, 128), 128)] = gv.astype(BF)

    ready(3)

    def finish(rows):
        total = own_down[rows, :].astype(F32) + other_down[rows, :].astype(F32)
        r = total[:, WIDE:].astype(BF)
        rank_down[rows, :] = r
        result = middle[rows, :] + total[:, :WIDE] + matmul(r, exit_d[...])
        mixed[rows, :] = jnp.where(live_rows(scalars[0], rows), result, 0.0).astype(BF)

    row_blocks(finish)
    flush(2)
    half = half_of(scalars, mixed, mixed_half, half_sem)
    project_cols(
        part,
        [(lambda h=h: grads[h], lambda cols, h=h: w[h, cols, :]) for h in range(2)],
        [(lambda h=h: grads[h], lambda h=h: exits[h]) for h in range(2)],
    )
    flush(1)
    for h in range(2):
        exit_grads[h] = inner_rows(ranks[...], grads[h])[:48].astype(BF)
        entry_grads[h] = inner_rows(drank_out[...], att[h])[:16].astype(BF)
    shared[0] = inner_rows(rank_out[...], g1[...])[:16].astype(BF)
    shared[1] = inner_rows(rank_down[...], g2[...])[:16].astype(BF)
    wide[...] = inner_rows(drank_gu[...], hidden_in[...])[:32].astype(BF)
    half.wait()


def half_of(scalars, value, out, sem):
    first = pl.multiple_of(scalars[1] * 192, 16)
    copy = pltpu.make_async_copy(value.at[pl.ds(first, 192), :], out, sem)
    copy.start()
    return copy


def head_lines(ready, flush, gx_qkv, gx_gu, ge_out, ge_down, shared, out, cols, head):
    ready(0)
    i, j = iota2(512, 384)
    squeeze = ones_where(i == j + 16 * lax.div(j, 48))
    lane = lax.broadcasted_iota(jnp.int32, (16, 384), 1)
    head[...] = jnp.zeros_like(head)
    for m in range(2):
        cols[:, 4224 + m * WIDE : 4224 + m * WIDE + WIDE] = shared[m].astype(F32)
    for h in range(2):
        cols[:, :384] = matmul(gx_qkv[h, :16, :512], squeeze)
        key = matmul(gx_qkv[h, 16:32, 512:], squeeze)
        value = matmul(gx_qkv[h, 32:48, 512:], squeeze)
        cols[:, 384:768] = jnp.where(lane < 192, key, value)
        cols[:, 768:1792] = gx_gu[h, :16, :1024].astype(F32)
        cols[:, 1792:2816] = gx_gu[h, 16:32, 1024:].astype(F32)
        cols[:, 2816:3200] = matmul(ge_out[h], squeeze)
        cols[:, 3200:4224] = ge_down[h].astype(F32)
        for x in range(4):
            for n in range(57):
                head[n * 4 : n * 4 + 4, :] = cols[x * 4 : x * 4 + 4, n * 128 : n * 128 + 128]
            out[h * 4 + x] = head[...].astype(BF)


def pack(blocks):
    lane = lax.broadcasted_iota(jnp.int32, (48, 128), 1)
    full, last = [], blocks[1]
    for p in range(4):
        odd = blocks[2 * p + 1]
        full.append(jnp.where(lane < 80, blocks[2 * p], pltpu.roll(odd, 80, 1)))
        moved = pltpu.roll(odd, (32 * p - 48) % 128, 1)
        last = jnp.where((lane >= 32 * p) & (lane < 32 * p + 32), moved, last)
    return [*full, last]


def unpack(full, n):
    if n % 2 == 0:
        return full(n // 2)
    lane = lax.broadcasted_iota(jnp.int32, (48, 128), 1)
    first = pltpu.roll(full(n // 2), 48, 1)
    return jnp.where(lane < 48, first, pltpu.roll(full(4), (48 - 32 * (n // 2)) % 128, 1))


def input_backward(
    ready, flush, scalars, tok, own, other, grad_middle, gain, ent, normed, wide_gu, head,
    grad_in, lines, in_half,
    drank, half_sem,
):
    ready(0)

    def start(rows):
        total = own[rows, :].astype(F32) + other[rows, :].astype(F32)
        d = total[:, WIDE:].astype(BF)
        drank[rows, :] = d
        grad = total[:, :WIDE] + inner_cols(d, ent[...])
        back = back_of_norm(tok[rows, :].astype(F32), gain[...], grad)
        grad_in[rows, :] = (grad_middle[rows, :] + back).astype(BF)

    row_blocks(start)
    flush(0)
    half = half_of(scalars, grad_in, in_half, half_sem)
    ready(1)
    wide = jnp.concatenate(
        [
            inner_rows(drank[...], normed[...])[:48],
            wide_gu[...].astype(F32),
            jnp.zeros((48, WIDE), F32),
        ],
        axis=0,
    ).T
    for x in range(4):
        full = pack([wide[(d * 4 + x) * 48 : (d * 4 + x) * 48 + 48] for d in range(8)])
        for h in range(2):
            lines[h * 4 + x, :240, :] = head[h * 4 + x]
            for t in range(5):
                lines[h * 4 + x, 240 + t * 48 : 288 + t * 48, :] = full[t].astype(BF)
    flush(1)
    half.wait()


def regroup(ready, flush, adapters, got, out, total):
    total[...] = jnp.zeros_like(total)
    ready(0)
    for n in range(8):
        a = adapters[n]
        total[a] = total[a] + got[n].astype(F32)
    for d in range(8):
        out[d, :240, :] = total[d, :240].astype(BF)
        blocks = [
            unpack(lambda t, a=a: total[a, 240 + t * 48 : 288 + t * 48, :], d) for a in range(8)
        ]
        for t, tile in enumerate(pack(blocks)):
            out[d, 240 + t * 48 : 288 + t * 48, :] = tile.astype(BF)


def gather_gradients(ready, flush, final, g_q, g_k, g_v, g_gate, g_up, g_eo, g_ed, g_xo, g_xd, wide_qkv, wide_gu, total, kv):
    @pl.loop(0, 3)
    def _(i):
        rows = pl.ds(pl.multiple_of(i * 160, 16), 160)
        total[rows, :] = sum(final[g, rows, :].astype(F32) for g in range(8))

    at = 0
    for out, blocks in (
        (g_q, 3), (kv, 3), (g_gate, 8), (g_up, 8), (g_eo, 3), (g_ed, 8), (g_xo, 12), (g_xd, 12),
    ):
        for n in range(blocks):
            line = (at + n) * 4
            out[:, n * 128 : n * 128 + 128] = total[line : line + 4, :]
        at += blocks
    both_kv = kv[...]
    g_k[...] = both_kv[:, :192]
    g_v[...] = both_kv[:, 192:]
    lane = lax.broadcasted_iota(jnp.int32, (48, 128), 1)
    for third in range(5):
        columns = jnp.zeros((48, 128), F32)
        for a in range(8):
            block = unpack(lambda t: total[240 + 48 * t : 288 + 48 * t, :], a)
            moved = pltpu.roll(block, (a * 16 - third * 16) % 128, 1)
            columns = jnp.where((lane >= a * 16) & (lane < a * 16 + 16), moved, columns)
        out, n = (wide_qkv, third) if third < 3 else (wide_gu, third - 3)
        out[:, n * 128 : n * 128 + 128] = columns


def shaped(*extent, dtype=BF):
    return jax.ShapeDtypeStruct(extent, dtype)


def call(
    body, args, outs, flops, scratch=(), scalars=(), far_in=(), far_out=(), late=None, sent=()
):
    whole = pl.BlockSpec(memory_space=pltpu.VMEM)
    small = pl.BlockSpec(memory_space=pltpu.SMEM)
    far = pl.BlockSpec(memory_space=pltpu.HBM)
    late = late or {}
    order = sorted(late, key=lambda i: late[i])
    block = [a[1] if isinstance(a, tuple) else None for a in args]
    args = [a[0] if isinstance(a, tuple) else a for a in args]
    shapes = [a.shape if i is None else a.shape[1:] for a, i in zip(args, block)]
    extra = len(order) + len(sent) + 2

    def kernel(*refs):
        spare, sem, out_sem = refs[len(refs) - extra : -2], refs[-2], refs[-1]
        refs = list(refs[: len(refs) - extra])
        copies = []
        for n, i in enumerate(order):
            source = refs[i] if block[i] is None else refs[i].at[block[i]]
            copies.append(pltpu.make_async_copy(source, spare[n], sem.at[n]))
            copies[-1].start()
            refs[i] = spare[n]
        leaving = {}
        for n, i in enumerate(sent):
            held = spare[len(order) + n]
            leaving[i] = pltpu.make_async_copy(held, refs[len(args) + i], out_sem.at[n])
            refs[len(args) + i] = held

        def ready(group):
            for n, i in enumerate(order):
                if late[i] == group:
                    copies[n].wait()

        started = []

        def flush(*which):
            for i in which:
                leaving[i].start()
                started.append(i)

        body(ready, flush, *refs)
        flush(*(i for i in sent if i not in started))
        for i in sent:
            leaving[i].wait()

    limit = 20 if body in (regroup, gather_gradients) else 59
    spares = [pltpu.VMEM(shapes[i], args[i].dtype) for i in order]
    spares += [pltpu.VMEM(outs[i].shape, outs[i].dtype) for i in sent]
    spares.append(pltpu.SemaphoreType.DMA((max(1, len(order)),)))
    spares.append(pltpu.SemaphoreType.DMA((max(1, len(sent)),)))
    return pl.pallas_call(
        kernel,
        out_shape=list(outs),
        in_specs=[
            small if i in scalars else far if i in far_in or i in late else whole
            for i in range(len(args))
        ],
        out_specs=[far if i in far_out or i in sent else whole for i in range(len(outs))],
        scratch_shapes=[*scratch, *spares],
        compiler_params=pltpu.CompilerParams(vmem_limit_bytes=limit << 20),
        cost_estimate=pl.CostEstimate(
            flops=int(flops),
            transcendentals=0,
            bytes_accessed=sum(a.size * a.dtype.itemsize for a in args),
        ),
    )(*args)


def lookup(table, index):
    return jnp.sum(jnp.where(jnp.arange(table.shape[0]) == index, table, 0))


def rope_tables(first):
    half = HEAD_DIM // 2
    freq = jnp.power(THETA, -2.0 * jnp.arange(half, dtype=F32) / HEAD_DIM)
    angle = (jnp.arange(ROWS) + first).astype(F32)[:, None] * freq[None, :]
    cosine, sine, pad = jnp.cos(angle), jnp.sin(angle), jnp.zeros((ROWS, 16), F32)
    return (
        jnp.concatenate([cosine, pad, cosine, pad], axis=1),
        jnp.concatenate([-sine, pad, sine, pad], axis=1),
    )


def per_device(
    tokens,
    cotangent,
    lengths,
    dealing,
    adapter_choice,
    attention_gain,
    feedforward_gain,
    query_weight,
    key_weight,
    value_weight,
    output_weight,
    gate_weight,
    up_weight,
    down_weight,
    entry_qkv,
    exit_query,
    exit_key,
    exit_value,
    entry_out,
    exit_out,
    entry_gate_up,
    exit_gate,
    exit_up,
    entry_down,
    exit_down,
):
    y, zl, x, zh, core = (lax.axis_index(a) for a in AXES)
    own_high = zh == 0
    entries = jnp.concatenate([entry_qkv, entry_gate_up], axis=1)
    entries = jnp.where(own_high, entries[:, :320], entries[:, 320:])
    pad = jnp.zeros((4, 128), BF)
    exits = jnp.concatenate(
        [
            exit_gate,
            exit_up,
            entry_down.T,
            jnp.where(own_high, exit_out, exit_down),
            exit_query,
            pad,
            exit_key,
            exit_value,
            pad,
            entry_out.T,
            pad,
        ],
        axis=1,
    ).reshape(48, 512)
    payload = jnp.concatenate(
        [
            query_weight,
            key_weight,
            value_weight,
            output_weight.T,
            entries,
            jnp.zeros((48, 64), BF),
            exits,
            gate_weight,
            up_weight,
            down_weight.T,
        ],
        axis=1,
    )
    send = Links()
    blocks = [payload[None, first : first + count] for first, count, _, _ in PARTS]
    blocks = [jnp.concatenate(p, 0) for p in ring_stage(send, blocks, 0, False)]
    zero, tokens, cotangent, lengths, dealing, adapter_choice, _ = lax.optimization_barrier(
        (jnp.int32(0), tokens, cotangent, lengths, dealing, adapter_choice, send.last)
    )
    slot = ((y * 2 + zl) * 4 + x) * 2 + zh
    sequence = lookup(dealing, slot)
    length = lookup(lengths, sequence)
    chosen = lookup(adapter_choice, sequence)
    coords = jnp.stack([y, zh * 2 + zl, x, core, chosen, length]).astype(jnp.int32)
    second = ring_stage(send, blocks, 1, True)

    def group(start, width):
        return [jnp.concatenate([q[:, :, start : start + width] for q in p], 0) for p in second]

    rows = lax.dynamic_index_in_dim(tokens, zh, 0, keepdims=False)
    cot = lax.dynamic_index_in_dim(cotangent, zh, 0, keepdims=False)
    cosine, sine = rope_tables(zero)
    scalars = jnp.stack([length, core]).astype(jnp.int32)
    gain1, gain2 = attention_gain[None], feedforward_gain[None]
    peers = ((y * 2 + zl) * 4 + jnp.tile(jnp.arange(4), 2)) * 2 + jnp.repeat(jnp.arange(2), 4)
    match = (jnp.arange(64)[None, :] == peers[:, None]).astype(jnp.int32)
    peer_seq = jnp.sum(match * dealing[None, :], axis=1)
    match = (jnp.arange(64)[None, :] == peer_seq[:, None]).astype(jnp.int32)
    peer_adapter = jnp.sum(match * adapter_choice[None, :], axis=1).astype(jnp.int32)
    early = (coords, rows, cot, cosine, sine, scalars, gain1, gain2, peer_adapter)
    early = lax.optimization_barrier(early)
    coords, rows, cot, cosine, sine, scalars, gain1, gain2, peer_adapter = early
    send.last = (send.last, early)
    attn_pieces = sum(ring_stage(send, group(0, ATTN), 2, True), [])
    (
        w_qkv, w_out, probs, ent_qkv, ent_gu, x_qkv, x_gu, e_out, e_down, x_od,
        normed, ranks, q, k, v, att, part,
    ) = call(
        attention_forward,
        (coords, rows, gain1, cosine, sine, *attn_pieces),
        (
            shaped(2, WIDE, 1024),
            shaped(2, WIDE, 512),
            shaped(8, ROWS, ROWS, dtype=F32),
            shaped(WIDE, LANES),
            shaped(WIDE, LANES),
            shaped(2, LANES, 1024),
            shaped(2, LANES, 2048),
            shaped(2, LANES, 512),
            shaped(2, LANES, 1024),
            shaped(2, LANES, WIDE),
            shaped(ROWS, WIDE),
            shaped(ROWS, LANES),
            shaped(8, ROWS, LANES),
            shaped(4, ROWS, LANES),
            shaped(4, ROWS, LANES),
            shaped(2, ROWS, 512),
            shaped(ROWS, PART),
        ),
        12e9,
        scratch=(
            pltpu.VMEM((2, WIDE, ATTN), BF),
            pltpu.VMEM((2, WIDE, 1024), BF),
            pltpu.VMEM((2, WIDE, 512), BF),
            pltpu.VMEM((8, ROWS, ROWS), F32),
            pltpu.SemaphoreType.DMA((5,)),
        ),
        scalars=(0,),
        far_in=tuple(range(5, 15)),
        far_out=(0, 1, 2),
        sent=tuple(range(3, 17)),
    )
    x_out, x_down = x_od[0], x_od[1]
    mlp_pieces = sum(ring_stage(send, group(ATTN, MLP), 2, True, lambda: part), [])
    middle, rank_out, hidden, g2, ranks_gu, drank_down = call(
        mlp_start,
        (scalars, rows, part, core_swap(part), cot, gain2, x_out, ent_gu, x_down),
        (
            shaped(ROWS, WIDE, dtype=F32),
            shaped(ROWS, LANES),
            shaped(ROWS, WIDE),
            shaped(ROWS, WIDE),
            shaped(ROWS, LANES),
            shaped(ROWS, LANES),
        ),
        1e9,
        scalars=(0,),
        late={1: 0, 2: 0, 3: 0, 4: 0, 6: 0, 7: 0, 8: 0},
        sent=(0, 1, 2, 3, 4, 5),
    )
    parts, gx_gu, ge_down = call(
        mlp,
        (coords, hidden, g2, ranks_gu, drank_down, x_gu, e_down, *mlp_pieces),
        (shaped(2, ROWS, PART), shaped(2, 32, 2048), shaped(2, 16, 1024)),
        15e9,
        scratch=(
            pltpu.VMEM((2, ROWS, 2048), BF),
            pltpu.VMEM((2, ROWS, 1024), BF),
            pltpu.VMEM((2, WIDE, MLP), BF),
            pltpu.SemaphoreType.DMA((2,)),
        ),
        scalars=(0,),
        far_in=tuple(range(7, 17)),
        late={1: 0, 2: 0, 3: 0, 4: 0, 5: 0, 6: 0},
        sent=(0, 1, 2),
    )
    others = core_swap(parts)
    grad_middle, part_qkv, mixed, gx_qkv, ge_out, shared, wide_gu, mixed_half = call(
        attention_backward,
        (
            scalars, g2, (parts, 0), (others, 0), middle, gain2, ent_gu, x_out, e_out, x_qkv, cosine, sine,
            q, k, v, probs, w_out, w_qkv, (parts, 1), (others, 1), x_down, rank_out, hidden, ranks, att,
        ),
        (
            shaped(ROWS, WIDE, dtype=F32),
            shaped(ROWS, PART),
            shaped(ROWS, WIDE),
            shaped(2, 48, 1024),
            shaped(2, 16, 512),
            shaped(2, 16, WIDE),
            shaped(32, WIDE),
            shaped(192, WIDE),
        ),
        8e9,
        scratch=(
            pltpu.VMEM((ROWS, WIDE), BF),
            pltpu.VMEM((ROWS, LANES), BF),
            pltpu.VMEM((ROWS, LANES), BF),
            pltpu.VMEM((2, ROWS, 1024), BF),
            pltpu.VMEM((8, ROWS, LANES), BF),
            pltpu.VMEM((ROWS, LANES), F32),
            pltpu.VMEM((ROWS, LANES), F32),
            pltpu.VMEM((ROWS, LANES), BF),
            pltpu.SemaphoreType.DMA(()),
        ),
        scalars=(0,),
        far_out=(7,),
        late={
            1: 0, 2: 0, 3: 0, 4: 0, 6: 0, 7: 1, 8: 1, 16: 1, 10: 2, 11: 2, 12: 2, 13: 2, 14: 2, 15: 2,
            9: 3, 17: 3, 18: 3, 19: 3, 20: 3, 21: 3, 22: 3, 23: 3, 24: 3,
        },
        sent=(0, 1, 2, 3, 4, 5, 6),
    )
    other_qkv = core_swap(part_qkv)
    (head,) = call(
        head_lines,
        (gx_qkv, gx_gu, ge_out, ge_down, shared),
        (shaped(8, 240, 128),),
        1e8,
        scratch=(pltpu.VMEM((16, 7296), F32), pltpu.VMEM((240, 128), F32)),
        late={0: 0, 1: 0, 2: 0, 3: 0, 4: 0},
        sent=(0,),
    )
    grad_in, lines, in_half = call(
        input_backward,
        (scalars, rows, part_qkv, other_qkv, grad_middle, gain1, ent_qkv, normed, wide_gu, head),
        (shaped(ROWS, WIDE), shaped(8, 480, 128), shaped(192, WIDE)),
        1e9,
        scratch=(pltpu.VMEM((ROWS, LANES), BF), pltpu.SemaphoreType.DMA(())),
        scalars=(0,),
        far_out=(2,),
        late={1: 0, 2: 0, 3: 0, 4: 0, 6: 0, 7: 1, 8: 1, 9: 1},
        sent=(0, 1),
    )
    to_other_chip = flip_pairs("zz", (2, 2))
    sent_mixed = lax.ppermute(mixed_half, AXES, to_other_chip)
    lines, sent_mixed = lax.optimization_barrier((lines, sent_mixed))
    got = lax.all_to_all(lines, ("zh", "x"), 0, 0, tiled=True)
    in_half, got = lax.optimization_barrier((in_half, got))
    sent_in = lax.ppermute(in_half, AXES, to_other_chip)
    (second,) = call(
        regroup,
        (peer_adapter, got),
        (shaped(8, 480, 128),),
        1e6,
        scratch=(pltpu.VMEM((8, 480, 128), F32),),
        scalars=(0,),
        late={1: 0},
        sent=(0,),
    )
    final = lax.all_to_all(second, ("y", "zl"), 0, 0, tiled=True)

    def share(value, got):
        value, got, rest, _ = lax.optimization_barrier((value, got, core_swap(got), second))
        low, high = jnp.where(core == 0, got, rest), jnp.where(core == 0, rest, got)
        other = jnp.concatenate([low, high], axis=0)
        return jnp.stack([jnp.where(own_high, value, other), jnp.where(own_high, other, value)])

    mixed, grad_in = share(mixed, sent_mixed), share(grad_in, sent_in)
    final, mixed, grad_in = lax.optimization_barrier((final, mixed, grad_in))
    g_q, g_k, g_v, g_gate, g_up, g_eo, g_ed, g_xo, g_xd, wide_qkv, wide_gu = call(
        gather_gradients,
        (final,),
        (
            shaped(4, 384, dtype=F32),
            shaped(4, 192, dtype=F32),
            shaped(4, 192, dtype=F32),
            shaped(4, 1024, dtype=F32),
            shaped(4, 1024, dtype=F32),
            shaped(4, 384, dtype=F32),
            shaped(4, 1024, dtype=F32),
            shaped(4, WIDE, dtype=F32),
            shaped(4, WIDE, dtype=F32),
            shaped(48, 384, dtype=F32),
            shaped(48, 256, dtype=F32),
        ),
        1e6,
        scratch=(pltpu.VMEM((480, LANES), F32), pltpu.VMEM((4, 384), F32)),
    )

    return (
        mixed,
        grad_in,
        wide_qkv,
        g_q,
        g_k,
        g_v,
        g_eo.T,
        g_xo,
        wide_gu,
        g_gate,
        g_up,
        g_ed.T,
        g_xd,
    )


def solution(mesh):
    fine = Mesh(mesh.devices.reshape(SIZES), AXES)
    dp, mp = ("y", "zl", "x"), ("zh", "c")
    return jax.shard_map(
        per_device,
        mesh=fine,
        in_specs=(
            P(dp, None, None),
            P(dp, None, None),
            P(),
            P(),
            P(),
            P(),
            P(),
            P(dp, mp),
            P(dp, mp),
            P(dp, mp),
            P(mp, dp),
            P(dp, mp),
            P(dp, mp),
            P(mp, dp),
            P(dp, None),
            P(dp, mp),
            P(dp, mp),
            P(dp, mp),
            P(mp, dp),
            P(dp, None),
            P(dp, None),
            P(dp, mp),
            P(dp, mp),
            P(mp, dp),
            P(dp, None),
        ),
        out_specs=(
            P(dp, None, None),
            P(dp, None, None),
            P(dp, None),
            P(dp, mp),
            P(dp, mp),
            P(dp, mp),
            P(mp, dp),
            P(dp, None),
            P(dp, None),
            P(dp, mp),
            P(dp, mp),
            P(mp, dp),
            P(dp, None),
        ),
        check_vma=False,
    )
```

```python
import jax
import jax.numpy as jnp
from jax import lax
from jax.experimental import pallas as pl
from jax.experimental.pallas import tpu as pltpu
from jax.sharding import Mesh, PartitionSpec as P

HEAD_DIM = 96
RANK = 16
EPS = 1e-05
THETA = 100000.0
BF = jnp.bfloat16
F32 = jnp.float32

AXES = ("y", "zl", "x", "zh", "c")
SIZES = (4, 2, 4, 2, 2)
PARTS = (
    (0, 32, (("z", "y"), ("y", "x"), ("x", "z")), ((1, 1), (3, 3))),
    (32, 16, (("x", "x"), ("z", "z"), ("y", "y")), ((1, 3), (3, 1))),
)
ATTN, MLP = 2048, 3072
WIDTHS = (ATTN, MLP)


def device_index(y, z, x, c):
    return (((y * 2 + z % 2) * 4 + x) * 2 + z // 2) * 2 + c


def flip_pairs(axes, flips):
    pairs = []
    for y in range(4):
        for z in range(4):
            for x in range(4):
                for c in range(2):
                    to = {"x": x, "y": y, "z": z}
                    to[axes[c]] ^= flips[c]
                    pairs.append(
                        (device_index(y, z, x, c), device_index(to["y"], to["z"], to["x"], c))
                    )
    return pairs


def core_swap(value):
    pairs = [(i, i ^ 1) for i in range(128)]
    return lax.ppermute(value, AXES, pairs)


class Links:
    def __init__(self):
        self.last = ()

    def __call__(self, values, axes, flips):
        values, _ = lax.optimization_barrier((tuple(values), self.last))
        out = tuple(
            lax.ppermute(v, AXES, flip_pairs(a, f)) for v, a, f in zip(values, axes, flips)
        )
        self.last = out
        return out


def ring_stage(send, blocks, stage, forward, between=None):
    a, b = blocks
    (p, q) = (PARTS[i][2][stage] for i in range(2))
    (s0, s1), (t0, t1) = (PARTS[i][3] for i in range(2))
    if not forward:
        an, bn, af, bf, ao, bo = send(
            (a, b, a, b, a, b), (p, q, p, q, p, q), (s0, t0, s1, t1, (2, 2), (2, 2))
        )
        return [[a, an, ao, af], [b, bn, bo, bf]]
    an, af, bn, bf = send((a, a, b, b), (p, p, q, q), (s0, s1, t0, t1))
    if between is not None:
        send.last = (send.last, between())
    half = a.shape[0] // 2
    al, ah, bl, bh = send(
        (an[:half], af[half:], bn[:half], bf[half:]), (p, p, q, q), (s1, s0, t1, t0)
    )
    return [[a, an, al, ah, af], [b, bn, bl, bh, bf]]


def fetch(coords, pieces, out, sem):
    own = {"y": coords[0], "z": coords[1], "x": coords[2]}

    def start_all(core):
        for high in range(2):
            for part, (start, count, axes, steps) in enumerate(PARTS):
                swapped = core == 1 and steps[0][1] == 3
                for q, (j3, k0, many) in enumerate(
                    ((0, 0, 16), (1, 0, 16), (2, 0, 8), (2, 8, 8), (3, 0, 16))
                ):
                    for k in range(many):
                        labels = ((k0 + k) % 4, (k0 + k) // 4, j3)
                        far = {
                            axis[core]: (4 - j) % 4 if swapped else j
                            for axis, j in zip(axes, labels)
                        }
                        if far["z"] // 2 != high:
                            continue
                        at = {axis: own[axis] ^ j for axis, j in far.items()}
                        first = (
                            at["y"] * 384 + lax.rem(at["z"], 2) * 192 + at["x"] * 48 + start
                        )
                        pltpu.make_async_copy(
                            pieces[part * 5 + q].at[k],
                            out.at[lax.div(at["z"], 2), pl.ds(pl.multiple_of(first, 16), count), :],
                            sem.at[high],
                        ).start()

    for core in range(2):

        @pl.when(coords[3] == core)
        def _():
            start_all(core)


def ones_where(condition):
    return jnp.where(condition, 1.0, 0.0).astype(BF)


def iota2(rows, cols):
    return (
        lax.broadcasted_iota(jnp.int32, (rows, cols), 0),
        lax.broadcasted_iota(jnp.int32, (rows, cols), 1),
    )


def matmul(left, right):
    return jnp.dot(left, right, preferred_element_type=F32)


def inner_rows(left, right):
    return lax.dot_general(left, right, (((0,), (0,)), ((), ())), preferred_element_type=F32)


def inner_cols(left, right):
    return lax.dot_general(left, right, (((1,), (1,)), ((), ())), preferred_element_type=F32)


ROWS = 384
WIDE = 1536
LANES = 128
PART = WIDE + LANES
FACTOR = HEAD_DIM ** (-0.5)


def row_blocks(body):
    @pl.loop(0, ROWS // 128)
    def _(i):
        body(pl.ds(pl.multiple_of(i * 128, 128), 128))


def row_scale(values):
    return lax.rsqrt(jnp.mean(values * values, axis=-1, keepdims=True) + EPS)


def back_of_norm(inputs, gain, grad):
    scale = row_scale(inputs)
    weighted = gain * grad
    return scale * weighted - inputs * (
        scale * scale * scale * jnp.mean(inputs * weighted, axis=-1, keepdims=True)
    )


def live_rows(length, rows):
    at = lax.broadcasted_iota(jnp.int32, (128, 1), 0) + rows.start
    return at < length


def spin(values, cosine, sine):
    return values * cosine + pltpu.roll(values, 64, 1) * sine


def project_cols(out, parts, rank_parts):
    for n in range(2):
        cols = pl.ds(n * 768, 768)
        out[:, cols] = sum(inner_cols(left(), right(cols)) for left, right in parts).astype(BF)

    out[:, WIDE:] = sum(inner_cols(left(), right()) for left, right in rank_parts).astype(BF)


def attention_forward(ready, flush, coords, tok, gain, cosine, sine, *refs):
    pieces = refs[:10]
    w_far, ot_far, probs_far, ent, ent_gu, exits, x_gu, entry_o, e_down, x_od = refs[10:20]
    normed, ranks, q, k, v, att, part = refs[20:27]
    raw, w, ot, probs, sem = refs[27:]
    fetch(coords, pieces, raw, sem)
    chosen, length = coords[4], coords[5]
    ready(0)

    def start(rows):
        x = tok[rows, :].astype(F32)
        normed[rows, :] = (x * row_scale(x) * gain[...]).astype(BF)

    row_blocks(start)
    i, j = iota2(384, 512)
    spread = ones_where(j == i + 16 * lax.div(i, 48))
    i, j = iota2(384, 128)
    picks = []
    for h in range(2):
        col = i + 320 * h
        third, rank = lax.div(col, 128), lax.rem(col, 16)
        ours = (lax.div(lax.rem(col, 128), 16) == chosen) & (i < 320)
        picks.append(
            (
                ones_where(ours & (third < 3) & (j == third * 16 + rank)),
                ones_where(ours & (third >= 3) & (j == (third - 3) * 16 + rank)),
            )
        )
    for h in range(2):
        pltpu.make_async_copy(raw.at[h], raw.at[h], sem.at[h]).wait()

    @pl.loop(0, 3)
    def _(n):
        rows = pl.ds(pl.multiple_of(n * 512, 512), 512)
        for h in range(2):
            for b in range(2):
                w[h, rows, b * 512 : b * 512 + 512] = matmul(
                    raw[h, rows, b * 384 : b * 384 + 384], spread
                ).astype(BF)
            ot[h, rows, :] = matmul(raw[h, rows, 768:1152], spread).astype(BF)
        for out, which in ((ent, 0), (ent_gu, 1)):
            out[rows, :] = sum(
                matmul(raw[h, rows, 1152:1536], picks[h][which]) for h in range(2)
            ).astype(BF)

    keep = [
        pltpu.make_async_copy(w, w_far, sem.at[2]),
        pltpu.make_async_copy(ot, ot_far, sem.at[3]),
    ]
    for copy in keep:
        copy.start()
    i, j = iota2(128, 192)
    lane = lax.broadcasted_iota(jnp.int32, (128, 512), 1)
    mine = pl.ds(pl.multiple_of(chosen * 192, 16), 192)
    for h in range(2):
        block = raw[h, mine, 1536:2048]

        def line(t, first):
            take = ones_where((j == 12 * (i - first) + t) & (i >= first) & (i < first + 16))
            return matmul(take, block).astype(BF)

        for t in range(2):
            x_gu[h, :, t * 512 : t * 512 + 512] = line(t, 0)
            x_gu[h, :, 1024 + t * 512 : 1536 + t * 512] = line(2 + t, 16)
            e_down[h, :, t * 512 : t * 512 + 512] = line(4 + t, 0)
        for t in range(3):
            x_od[h, :, t * 512 : t * 512 + 512] = line(6 + t, 0)
        exits[h, :, :512] = matmul(line(9, 0)[:, :384], spread).astype(BF)
        key = matmul(line(10, 16)[:, :384], spread)
        value = matmul(line(10, 32)[:, :384], spread)
        exits[h, :, 512:] = jnp.where(lane < 256, key, value).astype(BF)
        entry_o[h] = matmul(line(11, 0)[:, :384], spread).astype(BF)

    ranks[...] = matmul(normed[...], ent[...]).astype(BF)
    for h in range(2):
        for n in range(4):
            cols = slice(n * 256, n * 256 + 256)
            t = matmul(normed[...], w[h, :, cols]) + matmul(ranks[...], exits[h, :, cols])
            for i in range(2):
                head = t[:, i * 128 : i * 128 + 128]
                if n < 2:
                    q[h * 4 + n * 2 + i] = spin(head, cosine[...], sine[...]).astype(BF)
                elif n == 2:
                    k[h * 2 + i] = spin(head, cosine[...], sine[...]).astype(BF)
                else:
                    v[h * 2 + i] = head.astype(BF)
    at_q, at_k = iota2(ROWS, ROWS)
    allowed = (at_k <= at_q) & (at_k < length)
    for h in range(2):

        @pl.loop(0, 4)
        def _(i):
            g = h * 2 + i // 2
            s = inner_cols(q[h * 4 + i], k[g]) * FACTOR
            s = jnp.where(allowed, s, -1e30)
            e = jnp.exp(s - jnp.max(s, axis=-1, keepdims=True))
            p = e / jnp.sum(e, axis=-1, keepdims=True)
            probs[h * 4 + i] = p
            att[h, :, pl.ds(pl.multiple_of(i * 128, 128), 128)] = matmul(p.astype(BF), v[g]).astype(BF)

    flush(*range(3, 16))
    keep.append(pltpu.make_async_copy(probs, probs_far, sem.at[4]))
    keep[-1].start()
    project_cols(
        part,
        [(lambda h=h: att[h], lambda cols, h=h: ot[h, cols, :]) for h in range(2)],
        [(lambda h=h: att[h], lambda h=h: entry_o[h]) for h in range(2)],
    )
    for copy in keep:
        copy.wait()


def mlp_start(
    ready, flush, scalars, tok, own, other, cot, gain, exit_o, ent, exit_d,
    middle, rank_out, hidden, g2, ranks, drank,
):
    ready(0)

    def start(rows):
        total = own[rows, :].astype(F32) + other[rows, :].astype(F32)
        r = total[:, WIDE:].astype(BF)
        rank_out[rows, :] = r
        mid = tok[rows, :].astype(F32) + total[:, :WIDE] + matmul(r, exit_o[...])
        middle[rows, :] = mid
        hidden[rows, :] = (mid * row_scale(mid) * gain[...]).astype(BF)
        g2[rows, :] = jnp.where(live_rows(scalars[0], rows), cot[rows, :].astype(F32), 0.0).astype(BF)

    row_blocks(start)
    flush(0, 1, 2, 3)
    ranks[...] = matmul(hidden[...], ent[...]).astype(BF)
    drank[...] = inner_cols(g2[...], exit_d[...]).astype(BF)


def mlp(ready, flush, coords, hidden, g2, ranks, drank, exits, entry_d, *refs):
    pieces = refs[:10]
    parts, exit_grads, entry_grads = refs[10:13]
    grads, act, w, sem = refs[13:]
    fetch(coords, pieces, w, sem)
    ready(0)
    for step in range(2):
        h = lax.rem(lax.div(coords[1], 2) + step, 2)
        pltpu.make_async_copy(w.at[h], w.at[h], sem.at[step]).wait()
        for n in range(4):
            cols = pl.ds(n * 256, 256)
            ups = pl.ds(n * 256 + 1024, 256)
            downs = pl.ds(n * 256 + 2048, 256)
            gate = matmul(hidden[...], w[h, :, cols]) + matmul(ranks[...], exits[h, :, cols])
            up = matmul(hidden[...], w[h, :, ups]) + matmul(ranks[...], exits[h, :, ups])
            grad = matmul(g2[...], w[h, :, downs]) + matmul(drank[...], entry_d[h, :, cols])
            sigma = 1.0 / (1.0 + jnp.exp(-gate))
            silu = gate * sigma
            act[h, :, cols] = (silu * up).astype(BF)
            grads[h, :, ups] = (grad * silu).astype(BF)
            grads[h, :, cols] = (grad * (up * sigma * (1.0 + gate - silu))).astype(BF)

    project_cols(
        parts.at[0],
        [(lambda h=h: grads[h], lambda cols, h=h: w[h, cols, :2048]) for h in range(2)],
        [(lambda h=h: grads[h], lambda h=h: exits[h]) for h in range(2)],
    )
    project_cols(
        parts.at[1],
        [(lambda h=h: act[h], lambda cols, h=h: w[h, cols, 2048:]) for h in range(2)],
        [(lambda h=h: act[h], lambda h=h: entry_d[h]) for h in range(2)],
    )
    flush(0)
    for h in range(2):
        exit_grads[h] = inner_rows(ranks[...], grads[h])[:32].astype(BF)
        entry_grads[h] = inner_rows(drank[...], act[h])[:16].astype(BF)


def attention_backward(
    ready, flush, scalars, g2, own, other, middle, gain, ent, exit_o, entry_o, exits, cosine, sine, q, k, v, probs, ot, w,
    own_down, other_down, exit_d, rank_out, hidden_in, ranks, att,
    grad_middle, part, mixed, exit_grads, entry_grads, shared, wide, mixed_half,
    g1, drank_gu, drank_out, grads, grad_att, sum_k, sum_v, rank_down, half_sem,
):
    ready(0)

    def start(rows):
        total = own[rows, :].astype(F32) + other[rows, :].astype(F32)
        d = total[:, WIDE:].astype(BF)
        drank_gu[rows, :] = d
        hidden = total[:, :WIDE] + inner_cols(d, ent[...])
        mid = g2[rows, :].astype(F32) + back_of_norm(middle[rows, :], gain[...], hidden)
        grad_middle[rows, :] = mid
        g1[rows, :] = mid.astype(BF)

    row_blocks(start)
    ready(1)
    drank_out[...] = inner_cols(g1[...], exit_o[...]).astype(BF)
    flush(0)
    for h in range(2):
        for n in range(2):
            cols = slice(n * 256, n * 256 + 256)
            t = matmul(g1[...], ot[h, :, cols]) + matmul(drank_out[...], entry_o[h, :, cols])
            for i in range(2):
                grad_att[h * 4 + n * 2 + i] = t[:, i * 128 : i * 128 + 128].astype(BF)
    ready(2)
    for h in range(2):

        @pl.loop(0, 2)
        def _(j):
            g = h * 2 + j
            for i in range(2):
                head = h * 4 + j * 2 + i
                p = probs[head]
                ga = grad_att[head]
                gp = inner_cols(ga, v[g])
                delta = jnp.sum(p * gp, axis=-1, keepdims=True)
                gs = (p * (gp - delta)).astype(BF)
                gq = matmul(gs, k[g]) * FACTOR
                grads[h, :, pl.ds(pl.multiple_of((j * 2 + i) * 128, 128), 128)] = spin(
                    gq, cosine[...], -sine[...]
                ).astype(BF)
                gk = inner_rows(gs, q[head])
                gv = inner_rows(p.astype(BF), ga)
                if i == 0:
                    sum_k[...] = gk
                    sum_v[...] = gv
                else:
                    gk = (sum_k[...] + gk) * FACTOR
                    gv = sum_v[...] + gv
                    grads[h, :, pl.ds(pl.multiple_of(512 + j * 128, 128), 128)] = spin(
                        gk, cosine[...], -sine[...]
                    ).astype(BF)
                    grads[h, :, pl.ds(pl.multiple_of(768 + j * 128, 128), 128)] = gv.astype(BF)

    ready(3)

    def finish(rows):
        total = own_down[rows, :].astype(F32) + other_down[rows, :].astype(F32)
        r = total[:, WIDE:].astype(BF)
        rank_down[rows, :] = r
        result = middle[rows, :] + total[:, :WIDE] + matmul(r, exit_d[...])
        mixed[rows, :] = jnp.where(live_rows(scalars[0], rows), result, 0.0).astype(BF)

    row_blocks(finish)
    flush(2)
    half = half_of(scalars, mixed, mixed_half, half_sem)
    project_cols(
        part,
        [(lambda h=h: grads[h], lambda cols, h=h: w[h, cols, :]) for h in range(2)],
        [(lambda h=h: grads[h], lambda h=h: exits[h]) for h in range(2)],
    )
    flush(1)
    for h in range(2):
        exit_grads[h] = inner_rows(ranks[...], grads[h])[:48].astype(BF)
        entry_grads[h] = inner_rows(drank_out[...], att[h])[:16].astype(BF)
    shared[0] = inner_rows(rank_out[...], g1[...])[:16].astype(BF)
    shared[1] = inner_rows(rank_down[...], g2[...])[:16].astype(BF)
    wide[...] = inner_rows(drank_gu[...], hidden_in[...])[:32].astype(BF)
    half.wait()


def half_of(scalars, value, out, sem):
    first = pl.multiple_of(scalars[1] * 192, 16)
    copy = pltpu.make_async_copy(value.at[pl.ds(first, 192), :], out, sem)
    copy.start()
    return copy


def head_lines(ready, flush, gx_qkv, gx_gu, ge_out, ge_down, shared, out, cols, head):
    ready(0)
    i, j = iota2(512, 384)
    squeeze = ones_where(i == j + 16 * lax.div(j, 48))
    lane = lax.broadcasted_iota(jnp.int32, (16, 384), 1)
    head[...] = jnp.zeros_like(head)
    for m in range(2):
        cols[:, 4224 + m * WIDE : 4224 + m * WIDE + WIDE] = shared[m].astype(F32)
    for h in range(2):
        cols[:, :384] = matmul(gx_qkv[h, :16, :512], squeeze)
        key = matmul(gx_qkv[h, 16:32, 512:], squeeze)
        value = matmul(gx_qkv[h, 32:48, 512:], squeeze)
        cols[:, 384:768] = jnp.where(lane < 192, key, value)
        cols[:, 768:1792] = gx_gu[h, :16, :1024].astype(F32)
        cols[:, 1792:2816] = gx_gu[h, 16:32, 1024:].astype(F32)
        cols[:, 2816:3200] = matmul(ge_out[h], squeeze)
        cols[:, 3200:4224] = ge_down[h].astype(F32)
        for x in range(4):
            for n in range(57):
                head[n * 4 : n * 4 + 4, :] = cols[x * 4 : x * 4 + 4, n * 128 : n * 128 + 128]
            out[h * 4 + x] = head[...].astype(BF)


def pack(blocks):
    lane = lax.broadcasted_iota(jnp.int32, (48, 128), 1)
    full, last = [], blocks[1]
    for p in range(4):
        odd = blocks[2 * p + 1]
        full.append(jnp.where(lane < 80, blocks[2 * p], pltpu.roll(odd, 80, 1)))
        moved = pltpu.roll(odd, (32 * p - 48) % 128, 1)
        last = jnp.where((lane >= 32 * p) & (lane < 32 * p + 32), moved, last)
    return [*full, last]


def unpack(full, n):
    if n % 2 == 0:
        return full(n // 2)
    lane = lax.broadcasted_iota(jnp.int32, (48, 128), 1)
    first = pltpu.roll(full(n // 2), 48, 1)
    return jnp.where(lane < 48, first, pltpu.roll(full(4), (48 - 32 * (n // 2)) % 128, 1))


def input_backward(
    ready, flush, scalars, tok, own, other, grad_middle, gain, ent, normed, wide_gu, head,
    grad_in, lines, in_half,
    drank, half_sem,
):
    ready(0)

    def start(rows):
        total = own[rows, :].astype(F32) + other[rows, :].astype(F32)
        d = total[:, WIDE:].astype(BF)
        drank[rows, :] = d
        grad = total[:, :WIDE] + inner_cols(d, ent[...])
        back = back_of_norm(tok[rows, :].astype(F32), gain[...], grad)
        grad_in[rows, :] = (grad_middle[rows, :] + back).astype(BF)

    row_blocks(start)
    flush(0)
    half = half_of(scalars, grad_in, in_half, half_sem)
    ready(1)
    wide = jnp.concatenate(
        [
            inner_rows(drank[...], normed[...])[:48],
            wide_gu[...].astype(F32),
            jnp.zeros((48, WIDE), F32),
        ],
        axis=0,
    ).T
    for x in range(4):
        full = pack([wide[(d * 4 + x) * 48 : (d * 4 + x) * 48 + 48] for d in range(8)])
        for h in range(2):
            lines[h * 4 + x, :240, :] = head[h * 4 + x]
            for t in range(5):
                lines[h * 4 + x, 240 + t * 48 : 288 + t * 48, :] = full[t].astype(BF)
    flush(1)
    half.wait()


def regroup(ready, flush, adapters, got, out, total):
    total[...] = jnp.zeros_like(total)
    ready(0)
    for n in range(8):
        a = adapters[n]
        total[a] = total[a] + got[n].astype(F32)
    for d in range(8):
        out[d, :240, :] = total[d, :240].astype(BF)
        blocks = [
            unpack(lambda t, a=a: total[a, 240 + t * 48 : 288 + t * 48, :], d) for a in range(8)
        ]
        for t, tile in enumerate(pack(blocks)):
            out[d, 240 + t * 48 : 288 + t * 48, :] = tile.astype(BF)


def gather_gradients(ready, flush, final, g_q, g_k, g_v, g_gate, g_up, g_eo, g_ed, g_xo, g_xd, wide_qkv, wide_gu, total, kv):
    @pl.loop(0, 3)
    def _(i):
        rows = pl.ds(pl.multiple_of(i * 160, 16), 160)
        total[rows, :] = sum(final[g, rows, :].astype(F32) for g in range(8))

    at = 0
    for out, blocks in (
        (g_q, 3), (kv, 3), (g_gate, 8), (g_up, 8), (g_eo, 3), (g_ed, 8), (g_xo, 12), (g_xd, 12),
    ):
        for n in range(blocks):
            line = (at + n) * 4
            out[:, n * 128 : n * 128 + 128] = total[line : line + 4, :]
        at += blocks
    both_kv = kv[...]
    g_k[...] = both_kv[:, :192]
    g_v[...] = both_kv[:, 192:]
    lane = lax.broadcasted_iota(jnp.int32, (48, 128), 1)
    for third in range(5):
        columns = jnp.zeros((48, 128), F32)
        for a in range(8):
            block = unpack(lambda t: total[240 + 48 * t : 288 + 48 * t, :], a)
            moved = pltpu.roll(block, (a * 16 - third * 16) % 128, 1)
            columns = jnp.where((lane >= a * 16) & (lane < a * 16 + 16), moved, columns)
        out, n = (wide_qkv, third) if third < 3 else (wide_gu, third - 3)
        out[:, n * 128 : n * 128 + 128] = columns


def shaped(*extent, dtype=BF):
    return jax.ShapeDtypeStruct(extent, dtype)


def call(
    body, args, outs, flops, scratch=(), scalars=(), far_in=(), far_out=(), late=None, sent=(), high=None
):
    whole = pl.BlockSpec(memory_space=pltpu.VMEM)
    small = pl.BlockSpec(memory_space=pltpu.SMEM)
    far = pl.BlockSpec(memory_space=pltpu.HBM)
    late = late or {}
    order = sorted(late, key=lambda i: late[i])
    block = [a[1:] if isinstance(a, tuple) else None for a in args]
    args = [a[0] if isinstance(a, tuple) else a for a in args]
    shapes = [a.shape if i is None else a.shape[1:] for a, i in zip(args, block)]
    extra = len(order) + len(sent) + 2

    def kernel(*refs):
        spare, sem, out_sem = refs[len(refs) - extra : -2], refs[-2], refs[-1]
        refs = list(refs[: len(refs) - extra])
        copies = []
        for n, i in enumerate(order):
            source = refs[i]
            if block[i] is not None:
                source = source.at[refs[0][high] if block[i][0] is None else block[i][0]]
            copies.append(pltpu.make_async_copy(source, spare[n], sem.at[n]))
            copies[-1].start()
            refs[i] = spare[n]
        leaving = {}
        for n, i in enumerate(sent):
            held = spare[len(order) + n]
            leaving[i] = pltpu.make_async_copy(held, refs[len(args) + i], out_sem.at[n])
            refs[len(args) + i] = held

        def ready(group):
            for n, i in enumerate(order):
                if late[i] == group:
                    copies[n].wait()

        started = []

        def flush(*which):
            for i in which:
                leaving[i].start()
                started.append(i)

        body(ready, flush, *refs)
        flush(*(i for i in sent if i not in started))
        for i in sent:
            leaving[i].wait()

    limit = 20 if body in (regroup, gather_gradients) else 59
    spares = [pltpu.VMEM(shapes[i], args[i].dtype) for i in order]
    spares += [pltpu.VMEM(outs[i].shape, outs[i].dtype) for i in sent]
    spares.append(pltpu.SemaphoreType.DMA((max(1, len(order)),)))
    spares.append(pltpu.SemaphoreType.DMA((max(1, len(sent)),)))
    return pl.pallas_call(
        kernel,
        out_shape=list(outs),
        in_specs=[
            small if i in scalars else far if i in far_in or i in late else whole
            for i in range(len(args))
        ],
        out_specs=[far if i in far_out or i in sent else whole for i in range(len(outs))],
        scratch_shapes=[*scratch, *spares],
        compiler_params=pltpu.CompilerParams(vmem_limit_bytes=limit << 20),
        cost_estimate=pl.CostEstimate(
            flops=int(flops),
            transcendentals=0,
            bytes_accessed=sum(a.size * a.dtype.itemsize for a in args),
        ),
    )(*args)


def lookup(table, index):
    return jnp.sum(jnp.where(jnp.arange(table.shape[0]) == index, table, 0))


def vector(*values):
    at = jnp.arange(len(values), dtype=jnp.int32)
    return sum(jnp.where(at == n, value, 0) for n, value in enumerate(values)).astype(jnp.int32)


def rope_tables(first):
    lane = lax.broadcasted_iota(jnp.int32, (ROWS, LANES), 1)
    position = lax.broadcasted_iota(jnp.int32, (ROWS, LANES), 0) + first
    index = lax.rem(lane, 64)
    freq = jnp.power(THETA, -2.0 * index.astype(F32) / HEAD_DIM)
    angle = position.astype(F32) * freq
    used = index < 48
    sign = jnp.where(lane < 64, -1.0, 1.0)
    return jnp.where(used, jnp.cos(angle), 0.0), jnp.where(used, sign * jnp.sin(angle), 0.0)


def per_device(
    tokens,
    cotangent,
    lengths,
    dealing,
    adapter_choice,
    attention_gain,
    feedforward_gain,
    query_weight,
    key_weight,
    value_weight,
    output_weight,
    gate_weight,
    up_weight,
    down_weight,
    entry_qkv,
    exit_query,
    exit_key,
    exit_value,
    entry_out,
    exit_out,
    entry_gate_up,
    exit_gate,
    exit_up,
    entry_down,
    exit_down,
):
    y, zl, x, zh, core = (lax.axis_index(a) for a in AXES)
    own_high = zh == 0
    entries = jnp.concatenate([entry_qkv, entry_gate_up], axis=1)
    entries = jnp.where(own_high, entries[:, :320], entries[:, 320:])
    pad = jnp.zeros((4, 128), BF)
    exits = jnp.concatenate(
        [
            exit_gate,
            exit_up,
            entry_down.T,
            jnp.where(own_high, exit_out, exit_down),
            exit_query,
            pad,
            exit_key,
            exit_value,
            pad,
            entry_out.T,
            pad,
        ],
        axis=1,
    ).reshape(48, 512)
    payload = jnp.concatenate(
        [
            query_weight,
            key_weight,
            value_weight,
            output_weight.T,
            entries,
            jnp.zeros((48, 64), BF),
            exits,
            gate_weight,
            up_weight,
            down_weight.T,
        ],
        axis=1,
    )
    send = Links()
    blocks = [payload[None, first : first + count] for first, count, _, _ in PARTS]
    blocks = [jnp.concatenate(p, 0) for p in ring_stage(send, blocks, 0, False)]
    zero, lengths, dealing, adapter_choice, _ = lax.optimization_barrier(
        (jnp.int32(0), lengths, dealing, adapter_choice, send.last)
    )
    slot = ((y * 2 + zl) * 4 + x) * 2 + zh
    sequence = lookup(dealing, slot)
    length = lookup(lengths, sequence)
    chosen = lookup(adapter_choice, sequence)
    coords = vector(y, zh * 2 + zl, x, core, chosen, length, zh)
    second = ring_stage(send, blocks, 1, True)

    def group(start, width):
        return [jnp.concatenate([q[:, :, start : start + width] for q in p], 0) for p in second]

    cosine, sine = rope_tables(zero)
    scalars = vector(length, core, zh)
    gain1, gain2 = attention_gain[None], feedforward_gain[None]
    eight = jnp.arange(8)
    peers = ((y * 2 + zl) * 4 + eight % 4) * 2 + eight // 4
    match = (jnp.arange(64)[None, :] == peers[:, None]).astype(jnp.int32)
    peer_seq = jnp.sum(match * dealing[None, :], axis=1)
    match = (jnp.arange(64)[None, :] == peer_seq[:, None]).astype(jnp.int32)
    peer_adapter = jnp.sum(match * adapter_choice[None, :], axis=1).astype(jnp.int32)
    early = (coords, cosine, sine, scalars, gain1, gain2, peer_adapter)
    early = lax.optimization_barrier(early)
    coords, cosine, sine, scalars, gain1, gain2, peer_adapter = early
    send.last = (send.last, early)
    attn_pieces = sum(ring_stage(send, group(0, ATTN), 2, True), [])
    (
        w_qkv, w_out, probs, ent_qkv, ent_gu, x_qkv, x_gu, e_out, e_down, x_od,
        normed, ranks, q, k, v, att, part,
    ) = call(
        attention_forward,
        (coords, (tokens, None), gain1, cosine, sine, *attn_pieces),
        (
            shaped(2, WIDE, 1024),
            shaped(2, WIDE, 512),
            shaped(8, ROWS, ROWS, dtype=F32),
            shaped(WIDE, LANES),
            shaped(WIDE, LANES),
            shaped(2, LANES, 1024),
            shaped(2, LANES, 2048),
            shaped(2, LANES, 512),
            shaped(2, LANES, 1024),
            shaped(2, LANES, WIDE),
            shaped(ROWS, WIDE),
            shaped(ROWS, LANES),
            shaped(8, ROWS, LANES),
            shaped(4, ROWS, LANES),
            shaped(4, ROWS, LANES),
            shaped(2, ROWS, 512),
            shaped(ROWS, PART),
        ),
        12e9,
        scratch=(
            pltpu.VMEM((2, WIDE, ATTN), BF),
            pltpu.VMEM((2, WIDE, 1024), BF),
            pltpu.VMEM((2, WIDE, 512), BF),
            pltpu.VMEM((8, ROWS, ROWS), F32),
            pltpu.SemaphoreType.DMA((5,)),
        ),
        scalars=(0,),
        far_in=tuple(range(5, 15)),
        far_out=(0, 1, 2),
        sent=tuple(range(3, 17)),
        late={1: 0},
        high=6,
    )
    x_out, x_down = x_od[0], x_od[1]
    mlp_pieces = sum(ring_stage(send, group(ATTN, MLP), 2, True, lambda: part), [])
    middle, rank_out, hidden, g2, ranks_gu, drank_down = call(
        mlp_start,
        (scalars, (tokens, None), part, core_swap(part), (cotangent, None), gain2, x_out, ent_gu, x_down),
        (
            shaped(ROWS, WIDE, dtype=F32),
            shaped(ROWS, LANES),
            shaped(ROWS, WIDE),
            shaped(ROWS, WIDE),
            shaped(ROWS, LANES),
            shaped(ROWS, LANES),
        ),
        1e9,
        scalars=(0,),
        late={1: 0, 2: 0, 3: 0, 4: 0, 6: 0, 7: 0, 8: 0},
        sent=(0, 1, 2, 3, 4, 5),
        high=2,
    )
    parts, gx_gu, ge_down = call(
        mlp,
        (coords, hidden, g2, ranks_gu, drank_down, x_gu, e_down, *mlp_pieces),
        (shaped(2, ROWS, PART), shaped(2, 32, 2048), shaped(2, 16, 1024)),
        15e9,
        scratch=(
            pltpu.VMEM((2, ROWS, 2048), BF),
            pltpu.VMEM((2, ROWS, 1024), BF),
            pltpu.VMEM((2, WIDE, MLP), BF),
            pltpu.SemaphoreType.DMA((2,)),
        ),
        scalars=(0,),
        far_in=tuple(range(7, 17)),
        late={1: 0, 2: 0, 3: 0, 4: 0, 5: 0, 6: 0},
        sent=(0, 1, 2),
    )
    others = core_swap(parts)
    grad_middle, part_qkv, mixed, gx_qkv, ge_out, shared, wide_gu, mixed_half = call(
        attention_backward,
        (
            scalars, g2, (parts, 0), (others, 0), middle, gain2, ent_gu, x_out, e_out, x_qkv, cosine, sine,
            q, k, v, probs, w_out, w_qkv, (parts, 1), (others, 1), x_down, rank_out, hidden, ranks, att,
        ),
        (
            shaped(ROWS, WIDE, dtype=F32),
            shaped(ROWS, PART),
            shaped(ROWS, WIDE),
            shaped(2, 48, 1024),
            shaped(2, 16, 512),
            shaped(2, 16, WIDE),
            shaped(32, WIDE),
            shaped(192, WIDE),
        ),
        8e9,
        scratch=(
            pltpu.VMEM((ROWS, WIDE), BF),
            pltpu.VMEM((ROWS, LANES), BF),
            pltpu.VMEM((ROWS, LANES), BF),
            pltpu.VMEM((2, ROWS, 1024), BF),
            pltpu.VMEM((8, ROWS, LANES), BF),
            pltpu.VMEM((ROWS, LANES), F32),
            pltpu.VMEM((ROWS, LANES), F32),
            pltpu.VMEM((ROWS, LANES), BF),
            pltpu.SemaphoreType.DMA(()),
        ),
        scalars=(0,),
        far_out=(7,),
        late={
            1: 0, 2: 0, 3: 0, 4: 0, 6: 0, 7: 1, 8: 1, 16: 1, 10: 2, 11: 2, 12: 2, 13: 2, 14: 2, 15: 2,
            9: 3, 17: 3, 18: 3, 19: 3, 20: 3, 21: 3, 22: 3, 23: 3, 24: 3,
        },
        sent=(0, 1, 2, 3, 4, 5, 6),
    )
    other_qkv = core_swap(part_qkv)
    (head,) = call(
        head_lines,
        (gx_qkv, gx_gu, ge_out, ge_down, shared),
        (shaped(8, 240, 128),),
        1e8,
        scratch=(pltpu.VMEM((16, 7296), F32), pltpu.VMEM((240, 128), F32)),
        late={0: 0, 1: 0, 2: 0, 3: 0, 4: 0},
        sent=(0,),
    )
    grad_in, lines, in_half = call(
        input_backward,
        (scalars, (tokens, None), part_qkv, other_qkv, grad_middle, gain1, ent_qkv, normed, wide_gu, head),
        (shaped(ROWS, WIDE), shaped(8, 480, 128), shaped(192, WIDE)),
        1e9,
        scratch=(pltpu.VMEM((ROWS, LANES), BF), pltpu.SemaphoreType.DMA(())),
        scalars=(0,),
        far_out=(2,),
        late={1: 0, 2: 0, 3: 0, 4: 0, 6: 0, 7: 1, 8: 1, 9: 1},
        sent=(0, 1),
        high=2,
    )
    to_other_chip = flip_pairs("zz", (2, 2))
    sent_mixed = lax.ppermute(mixed_half, AXES, to_other_chip)
    lines, sent_mixed = lax.optimization_barrier((lines, sent_mixed))
    got = lax.all_to_all(lines, ("zh", "x"), 0, 0, tiled=True)
    in_half, got = lax.optimization_barrier((in_half, got))
    sent_in = lax.ppermute(in_half, AXES, to_other_chip)
    (second,) = call(
        regroup,
        (peer_adapter, got),
        (shaped(8, 480, 128),),
        1e6,
        scratch=(pltpu.VMEM((8, 480, 128), F32),),
        scalars=(0,),
        late={1: 0},
        sent=(0,),
    )
    final = lax.all_to_all(second, ("y", "zl"), 0, 0, tiled=True)

    def share(value, got):
        value, got, _ = lax.optimization_barrier((value, got, second))
        rest = core_swap(got)
        low, high = jnp.where(core == 0, got, rest), jnp.where(core == 0, rest, got)
        other = jnp.concatenate([low, high], axis=0)
        return jnp.stack([jnp.where(own_high, value, other), jnp.where(own_high, other, value)])

    mixed, grad_in = share(mixed, sent_mixed), share(grad_in, sent_in)
    final, mixed, grad_in = lax.optimization_barrier((final, mixed, grad_in))
    g_q, g_k, g_v, g_gate, g_up, g_eo, g_ed, g_xo, g_xd, wide_qkv, wide_gu = call(
        gather_gradients,
        (final,),
        (
            shaped(4, 384, dtype=F32),
            shaped(4, 192, dtype=F32),
            shaped(4, 192, dtype=F32),
            shaped(4, 1024, dtype=F32),
            shaped(4, 1024, dtype=F32),
            shaped(4, 384, dtype=F32),
            shaped(4, 1024, dtype=F32),
            shaped(4, WIDE, dtype=F32),
            shaped(4, WIDE, dtype=F32),
            shaped(48, 384, dtype=F32),
            shaped(48, 256, dtype=F32),
        ),
        1e6,
        scratch=(pltpu.VMEM((480, LANES), F32), pltpu.VMEM((4, 384), F32)),
    )

    return (
        mixed,
        grad_in,
        wide_qkv,
        g_q,
        g_k,
        g_v,
        g_eo.T,
        g_xo,
        wide_gu,
        g_gate,
        g_up,
        g_ed.T,
        g_xd,
    )


def solution(mesh):
    fine = Mesh(mesh.devices.reshape(SIZES), AXES)
    dp, mp = ("y", "zl", "x"), ("zh", "c")
    return jax.shard_map(
        per_device,
        mesh=fine,
        in_specs=(
            P(dp, None, None),
            P(dp, None, None),
            P(),
            P(),
            P(),
            P(),
            P(),
            P(dp, mp),
            P(dp, mp),
            P(dp, mp),
            P(mp, dp),
            P(dp, mp),
            P(dp, mp),
            P(mp, dp),
            P(dp, None),
            P(dp, mp),
            P(dp, mp),
            P(dp, mp),
            P(mp, dp),
            P(dp, None),
            P(dp, None),
            P(dp, mp),
            P(dp, mp),
            P(mp, dp),
            P(dp, None),
        ),
        out_specs=(
            P(dp, None, None),
            P(dp, None, None),
            P(dp, None),
            P(dp, mp),
            P(dp, mp),
            P(dp, mp),
            P(mp, dp),
            P(dp, None),
            P(dp, None),
            P(dp, mp),
            P(dp, mp),
            P(mp, dp),
            P(dp, None),
        ),
        check_vma=False,
    )
```

```python
import jax
import jax.numpy as jnp
from jax import lax
from jax.experimental import pallas as pl
from jax.experimental.pallas import tpu as pltpu
from jax.sharding import Mesh, PartitionSpec as P

HEAD_DIM = 96
RANK = 16
EPS = 1e-05
THETA = 100000.0
BF = jnp.bfloat16
F32 = jnp.float32

AXES = ("y", "zl", "x", "zh", "c")
SIZES = (4, 2, 4, 2, 2)
PARTS = (
    (0, 32, (("z", "y"), ("y", "x"), ("x", "z")), ((1, 1), (3, 3))),
    (32, 16, (("x", "x"), ("z", "z"), ("y", "y")), ((1, 3), (3, 1))),
)
ATTN, MLP = 2048, 3072
WIDTHS = (ATTN, MLP)


def device_index(y, z, x, c):
    return (((y * 2 + z % 2) * 4 + x) * 2 + z // 2) * 2 + c


def flip_pairs(axes, flips):
    pairs = []
    for y in range(4):
        for z in range(4):
            for x in range(4):
                for c in range(2):
                    to = {"x": x, "y": y, "z": z}
                    to[axes[c]] ^= flips[c]
                    pairs.append(
                        (device_index(y, z, x, c), device_index(to["y"], to["z"], to["x"], c))
                    )
    return pairs


def core_swap(value):
    pairs = [(i, i ^ 1) for i in range(128)]
    return lax.ppermute(value, AXES, pairs)


class Links:
    def __init__(self):
        self.last = ()

    def __call__(self, values, axes, flips):
        values, _ = lax.optimization_barrier((tuple(values), self.last))
        out = tuple(
            lax.ppermute(v, AXES, flip_pairs(a, f)) for v, a, f in zip(values, axes, flips)
        )
        self.last = out
        return out


def ring_stage(send, blocks, stage, forward, between=None):
    a, b = blocks
    (p, q) = (PARTS[i][2][stage] for i in range(2))
    (s0, s1), (t0, t1) = (PARTS[i][3] for i in range(2))
    if not forward:
        an, bn, af, bf, ao, bo = send(
            (a, b, a, b, a, b), (p, q, p, q, p, q), (s0, t0, s1, t1, (2, 2), (2, 2))
        )
        return [[a, an, ao, af], [b, bn, bo, bf]]
    an, af, bn, bf = send((a, a, b, b), (p, p, q, q), (s0, s1, t0, t1))
    if between is not None:
        send.last = (send.last, between())
    half = a.shape[0] // 2
    al, ah, bl, bh = send(
        (an[:half], af[half:], bn[:half], bf[half:]), (p, p, q, q), (s1, s0, t1, t0)
    )
    return [[a, an, al, ah, af], [b, bn, bl, bh, bf]]


def fetch(coords, pieces, out, sem):
    own = {"y": coords[0], "z": coords[1], "x": coords[2]}

    def start_all(core):
        for high in range(2):
            for part, (start, count, axes, steps) in enumerate(PARTS):
                swapped = core == 1 and steps[0][1] == 3
                for q, (j3, k0, many) in enumerate(
                    ((0, 0, 16), (1, 0, 16), (2, 0, 8), (2, 8, 8), (3, 0, 16))
                ):
                    for k in range(many):
                        labels = ((k0 + k) % 4, (k0 + k) // 4, j3)
                        far = {
                            axis[core]: (4 - j) % 4 if swapped else j
                            for axis, j in zip(axes, labels)
                        }
                        if far["z"] // 2 != high:
                            continue
                        at = {axis: own[axis] ^ j for axis, j in far.items()}
                        first = (
                            at["y"] * 384 + lax.rem(at["z"], 2) * 192 + at["x"] * 48 + start
                        )
                        pltpu.make_async_copy(
                            pieces[part * 5 + q].at[k],
                            out.at[lax.div(at["z"], 2), pl.ds(pl.multiple_of(first, 16), count), :],
                            sem.at[high],
                        ).start()

    for core in range(2):

        @pl.when(coords[3] == core)
        def _():
            start_all(core)


def ones_where(condition):
    return jnp.where(condition, 1.0, 0.0).astype(BF)


def iota2(rows, cols):
    return (
        lax.broadcasted_iota(jnp.int32, (rows, cols), 0),
        lax.broadcasted_iota(jnp.int32, (rows, cols), 1),
    )


def matmul(left, right):
    return jnp.dot(left, right, preferred_element_type=F32)


def inner_rows(left, right):
    return lax.dot_general(left, right, (((0,), (0,)), ((), ())), preferred_element_type=F32)


def inner_cols(left, right):
    return lax.dot_general(left, right, (((1,), (1,)), ((), ())), preferred_element_type=F32)


ROWS = 384
WIDE = 1536
LANES = 128
PART = WIDE + LANES
FACTOR = HEAD_DIM ** (-0.5)


def row_blocks(body):
    @pl.loop(0, ROWS // 128)
    def _(i):
        body(pl.ds(pl.multiple_of(i * 128, 128), 128))


def row_scale(values):
    return lax.rsqrt(jnp.mean(values * values, axis=-1, keepdims=True) + EPS)


def back_of_norm(inputs, gain, grad):
    scale = row_scale(inputs)
    weighted = gain * grad
    return scale * weighted - inputs * (
        scale * scale * scale * jnp.mean(inputs * weighted, axis=-1, keepdims=True)
    )


def live_rows(length, rows):
    at = lax.broadcasted_iota(jnp.int32, (128, 1), 0) + rows.start
    return at < length


def spin(values, cosine, sine):
    return values * cosine + pltpu.roll(values, 64, 1) * sine


def project_cols(out, parts, rank_parts):
    for n in range(2):
        cols = pl.ds(n * 768, 768)
        out[:, cols] = sum(inner_cols(left(), right(cols)) for left, right in parts).astype(BF)

    out[:, WIDE:] = sum(inner_cols(left(), right()) for left, right in rank_parts).astype(BF)


def attention_forward(ready, flush, coords, tok, gain, cosine, sine, *refs):
    pieces = refs[:10]
    w_far, ot_far, probs_far, ent, ent_gu, exits, x_gu, entry_o, e_down, x_od = refs[10:20]
    normed, ranks, q, k, v, att, part = refs[20:27]
    raw, w, ot, probs, sem = refs[27:]
    fetch(coords, pieces, raw, sem)
    chosen, length = coords[4], coords[5]
    ready(0)

    def start(rows):
        x = tok[rows, :].astype(F32)
        normed[rows, :] = (x * row_scale(x) * gain[...]).astype(BF)

    row_blocks(start)
    i, j = iota2(384, 512)
    spread = ones_where(j == i + 16 * lax.div(i, 48))
    i, j = iota2(384, 128)
    picks = []
    for h in range(2):
        col = i + 320 * h
        third, rank = lax.div(col, 128), lax.rem(col, 16)
        ours = (lax.div(lax.rem(col, 128), 16) == chosen) & (i < 320)
        picks.append(
            (
                ones_where(ours & (third < 3) & (j == third * 16 + rank)),
                ones_where(ours & (third >= 3) & (j == (third - 3) * 16 + rank)),
            )
        )
    for h in range(2):
        pltpu.make_async_copy(raw.at[h], raw.at[h], sem.at[h]).wait()

    @pl.loop(0, 3)
    def _(n):
        rows = pl.ds(pl.multiple_of(n * 512, 512), 512)
        for h in range(2):
            for b in range(2):
                w[h, rows, b * 512 : b * 512 + 512] = matmul(
                    raw[h, rows, b * 384 : b * 384 + 384], spread
                ).astype(BF)
            ot[h, rows, :] = matmul(raw[h, rows, 768:1152], spread).astype(BF)
        for out, which in ((ent, 0), (ent_gu, 1)):
            out[rows, :] = sum(
                matmul(raw[h, rows, 1152:1536], picks[h][which]) for h in range(2)
            ).astype(BF)

    keep = [
        pltpu.make_async_copy(w, w_far, sem.at[2]),
        pltpu.make_async_copy(ot, ot_far, sem.at[3]),
    ]
    for copy in keep:
        copy.start()
    i, j = iota2(128, 192)
    lane = lax.broadcasted_iota(jnp.int32, (128, 512), 1)
    mine = pl.ds(pl.multiple_of(chosen * 192, 16), 192)
    for h in range(2):
        block = raw[h, mine, 1536:2048]

        def line(t, first):
            take = ones_where((j == 12 * (i - first) + t) & (i >= first) & (i < first + 16))
            return matmul(take, block).astype(BF)

        for t in range(2):
            x_gu[h, :, t * 512 : t * 512 + 512] = line(t, 0)
            x_gu[h, :, 1024 + t * 512 : 1536 + t * 512] = line(2 + t, 16)
            e_down[h, :, t * 512 : t * 512 + 512] = line(4 + t, 0)
        for t in range(3):
            x_od[h, :, t * 512 : t * 512 + 512] = line(6 + t, 0)
        exits[h, :, :512] = matmul(line(9, 0)[:, :384], spread).astype(BF)
        key = matmul(line(10, 16)[:, :384], spread)
        value = matmul(line(10, 32)[:, :384], spread)
        exits[h, :, 512:] = jnp.where(lane < 256, key, value).astype(BF)
        entry_o[h] = matmul(line(11, 0)[:, :384], spread).astype(BF)

    ranks[...] = matmul(normed[...], ent[...]).astype(BF)
    for h in range(2):
        for n in range(4):
            cols = slice(n * 256, n * 256 + 256)
            t = matmul(normed[...], w[h, :, cols]) + matmul(ranks[...], exits[h, :, cols])
            for i in range(2):
                head = t[:, i * 128 : i * 128 + 128]
                if n < 2:
                    q[h * 4 + n * 2 + i] = spin(head, cosine[...], sine[...]).astype(BF)
                elif n == 2:
                    k[h * 2 + i] = spin(head, cosine[...], sine[...]).astype(BF)
                else:
                    v[h * 2 + i] = head.astype(BF)
    at_q, at_k = iota2(ROWS, ROWS)
    allowed = (at_k <= at_q) & (at_k < length)
    for h in range(2):

        @pl.loop(0, 4)
        def _(i):
            g = h * 2 + i // 2
            s = inner_cols(q[h * 4 + i], k[g]) * FACTOR
            s = jnp.where(allowed, s, -1e30)
            e = jnp.exp(s - jnp.max(s, axis=-1, keepdims=True))
            p = e / jnp.sum(e, axis=-1, keepdims=True)
            probs[h * 4 + i] = p
            att[h, :, pl.ds(pl.multiple_of(i * 128, 128), 128)] = matmul(p.astype(BF), v[g]).astype(BF)

    flush(*range(3, 16))
    keep.append(pltpu.make_async_copy(probs, probs_far, sem.at[4]))
    keep[-1].start()
    project_cols(
        part,
        [(lambda h=h: att[h], lambda cols, h=h: ot[h, cols, :]) for h in range(2)],
        [(lambda h=h: att[h], lambda h=h: entry_o[h]) for h in range(2)],
    )
    for copy in keep:
        copy.wait()


def mlp_start(
    ready, flush, scalars, tok, own, other, cot, gain, exit_o, ent, exit_d,
    middle, rank_out, hidden, g2, ranks, drank,
):
    ready(0)

    def start(rows):
        total = own[rows, :].astype(F32) + other[rows, :].astype(F32)
        r = total[:, WIDE:].astype(BF)
        rank_out[rows, :] = r
        mid = tok[rows, :].astype(F32) + total[:, :WIDE] + matmul(r, exit_o[...])
        middle[rows, :] = mid
        hidden[rows, :] = (mid * row_scale(mid) * gain[...]).astype(BF)
        g2[rows, :] = jnp.where(live_rows(scalars[0], rows), cot[rows, :].astype(F32), 0.0).astype(BF)

    row_blocks(start)
    flush(0, 1, 2, 3)
    ranks[...] = matmul(hidden[...], ent[...]).astype(BF)
    drank[...] = inner_cols(g2[...], exit_d[...]).astype(BF)


def mlp(ready, flush, coords, hidden, g2, ranks, drank, exits, entry_d, *refs):
    pieces = refs[:10]
    parts, exit_grads, entry_grads = refs[10:13]
    grads, act, w, sem = refs[13:]
    fetch(coords, pieces, w, sem)
    ready(0)
    for step in range(2):
        h = lax.rem(lax.div(coords[1], 2) + step, 2)
        pltpu.make_async_copy(w.at[h], w.at[h], sem.at[step]).wait()
        for n in range(4):
            cols = pl.ds(n * 256, 256)
            ups = pl.ds(n * 256 + 1024, 256)
            downs = pl.ds(n * 256 + 2048, 256)
            gate = matmul(hidden[...], w[h, :, cols]) + matmul(ranks[...], exits[h, :, cols])
            up = matmul(hidden[...], w[h, :, ups]) + matmul(ranks[...], exits[h, :, ups])
            grad = matmul(g2[...], w[h, :, downs]) + matmul(drank[...], entry_d[h, :, cols])
            sigma = 1.0 / (1.0 + jnp.exp(-gate))
            silu = gate * sigma
            act[h, :, cols] = (silu * up).astype(BF)
            grads[h, :, ups] = (grad * silu).astype(BF)
            grads[h, :, cols] = (grad * (up * sigma * (1.0 + gate - silu))).astype(BF)

    project_cols(
        parts.at[0],
        [(lambda h=h: grads[h], lambda cols, h=h: w[h, cols, :2048]) for h in range(2)],
        [(lambda h=h: grads[h], lambda h=h: exits[h]) for h in range(2)],
    )
    project_cols(
        parts.at[1],
        [(lambda h=h: act[h], lambda cols, h=h: w[h, cols, 2048:]) for h in range(2)],
        [(lambda h=h: act[h], lambda h=h: entry_d[h]) for h in range(2)],
    )
    flush(0)
    for h in range(2):
        exit_grads[h] = inner_rows(ranks[...], grads[h])[:32].astype(BF)
        entry_grads[h] = inner_rows(drank[...], act[h])[:16].astype(BF)


def attention_backward(
    ready, flush, scalars, g2, own, other, middle, gain, ent, exit_o, entry_o, exits, cosine, sine, q, k, v, probs, ot, w,
    own_down, other_down, exit_d, rank_out, hidden_in, ranks, att,
    grad_middle, part, mixed, exit_grads, entry_grads, shared, wide, mixed_half,
    g1, drank_gu, drank_out, grads, grad_att, sum_k, sum_v, rank_down, half_sem,
):
    ready(0)

    def start(rows):
        total = own[rows, :].astype(F32) + other[rows, :].astype(F32)
        d = total[:, WIDE:].astype(BF)
        drank_gu[rows, :] = d
        hidden = total[:, :WIDE] + inner_cols(d, ent[...])
        mid = g2[rows, :].astype(F32) + back_of_norm(middle[rows, :], gain[...], hidden)
        grad_middle[rows, :] = mid
        g1[rows, :] = mid.astype(BF)

    row_blocks(start)
    ready(1)
    drank_out[...] = inner_cols(g1[...], exit_o[...]).astype(BF)
    flush(0)
    for h in range(2):
        for n in range(2):
            cols = slice(n * 256, n * 256 + 256)
            t = matmul(g1[...], ot[h, :, cols]) + matmul(drank_out[...], entry_o[h, :, cols])
            for i in range(2):
                grad_att[h * 4 + n * 2 + i] = t[:, i * 128 : i * 128 + 128].astype(BF)
    ready(2)
    for h in range(2):
        for j in range(2):
            g = h * 2 + j
            for i in range(2):
                head = h * 4 + j * 2 + i
                p = probs[head]
                ga = grad_att[head]
                gp = inner_cols(ga, v[g])
                delta = jnp.sum(p * gp, axis=-1, keepdims=True)
                gs = (p * (gp - delta)).astype(BF)
                gq = matmul(gs, k[g]) * FACTOR
                grads[h, :, pl.ds((j * 2 + i) * 128, 128)] = spin(
                    gq, cosine[...], -sine[...]
                ).astype(BF)
                gk = inner_rows(gs, q[head])
                gv = inner_rows(p.astype(BF), ga)
                if i == 0:
                    sum_k[...] = gk
                    sum_v[...] = gv
                else:
                    gk = (sum_k[...] + gk) * FACTOR
                    gv = sum_v[...] + gv
                    grads[h, :, pl.ds(512 + j * 128, 128)] = spin(
                        gk, cosine[...], -sine[...]
                    ).astype(BF)
                    grads[h, :, pl.ds(768 + j * 128, 128)] = gv.astype(BF)

    ready(3)

    def finish(rows):
        total = own_down[rows, :].astype(F32) + other_down[rows, :].astype(F32)
        r = total[:, WIDE:].astype(BF)
        rank_down[rows, :] = r
        result = middle[rows, :] + total[:, :WIDE] + matmul(r, exit_d[...])
        mixed[rows, :] = jnp.where(live_rows(scalars[0], rows), result, 0.0).astype(BF)

    row_blocks(finish)
    flush(2)
    half = half_of(scalars, mixed, mixed_half, half_sem)
    project_cols(
        part,
        [(lambda h=h: grads[h], lambda cols, h=h: w[h, cols, :]) for h in range(2)],
        [(lambda h=h: grads[h], lambda h=h: exits[h]) for h in range(2)],
    )
    flush(1)
    for h in range(2):
        exit_grads[h] = inner_rows(ranks[...], grads[h])[:48].astype(BF)
        entry_grads[h] = inner_rows(drank_out[...], att[h])[:16].astype(BF)
    shared[0] = inner_rows(rank_out[...], g1[...])[:16].astype(BF)
    shared[1] = inner_rows(rank_down[...], g2[...])[:16].astype(BF)
    wide[...] = inner_rows(drank_gu[...], hidden_in[...])[:32].astype(BF)
    half.wait()


def half_of(scalars, value, out, sem):
    first = pl.multiple_of(scalars[1] * 192, 16)
    copy = pltpu.make_async_copy(value.at[pl.ds(first, 192), :], out, sem)
    copy.start()
    return copy


def head_lines(ready, flush, gx_qkv, gx_gu, ge_out, ge_down, shared, out, cols, head):
    ready(0)
    i, j = iota2(512, 384)
    squeeze = ones_where(i == j + 16 * lax.div(j, 48))
    lane = lax.broadcasted_iota(jnp.int32, (16, 384), 1)
    head[...] = jnp.zeros_like(head)
    for m in range(2):
        cols[:, 4224 + m * WIDE : 4224 + m * WIDE + WIDE] = shared[m].astype(F32)
    for h in range(2):
        cols[:, :384] = matmul(gx_qkv[h, :16, :512], squeeze)
        key = matmul(gx_qkv[h, 16:32, 512:], squeeze)
        value = matmul(gx_qkv[h, 32:48, 512:], squeeze)
        cols[:, 384:768] = jnp.where(lane < 192, key, value)
        cols[:, 768:1792] = gx_gu[h, :16, :1024].astype(F32)
        cols[:, 1792:2816] = gx_gu[h, 16:32, 1024:].astype(F32)
        cols[:, 2816:3200] = matmul(ge_out[h], squeeze)
        cols[:, 3200:4224] = ge_down[h].astype(F32)
        for x in range(4):
            for n in range(57):
                head[n * 4 : n * 4 + 4, :] = cols[x * 4 : x * 4 + 4, n * 128 : n * 128 + 128]
            out[h * 4 + x] = head[...].astype(BF)


def pack(blocks):
    lane = lax.broadcasted_iota(jnp.int32, (48, 128), 1)
    full, last = [], blocks[1]
    for p in range(4):
        odd = blocks[2 * p + 1]
        full.append(jnp.where(lane < 80, blocks[2 * p], pltpu.roll(odd, 80, 1)))
        moved = pltpu.roll(odd, (32 * p - 48) % 128, 1)
        last = jnp.where((lane >= 32 * p) & (lane < 32 * p + 32), moved, last)
    return [*full, last]


def unpack(full, n):
    if n % 2 == 0:
        return full(n // 2)
    lane = lax.broadcasted_iota(jnp.int32, (48, 128), 1)
    first = pltpu.roll(full(n // 2), 48, 1)
    return jnp.where(lane < 48, first, pltpu.roll(full(4), (48 - 32 * (n // 2)) % 128, 1))


def input_backward(
    ready, flush, scalars, tok, own, other, grad_middle, gain, ent, normed, wide_gu, head,
    grad_in, lines, in_half,
    drank, half_sem,
):
    ready(0)

    def start(rows):
        total = own[rows, :].astype(F32) + other[rows, :].astype(F32)
        d = total[:, WIDE:].astype(BF)
        drank[rows, :] = d
        grad = total[:, :WIDE] + inner_cols(d, ent[...])
        back = back_of_norm(tok[rows, :].astype(F32), gain[...], grad)
        grad_in[rows, :] = (grad_middle[rows, :] + back).astype(BF)

    row_blocks(start)
    flush(0)
    half = half_of(scalars, grad_in, in_half, half_sem)
    ready(1)
    wide = jnp.concatenate(
        [
            inner_rows(drank[...], normed[...])[:48],
            wide_gu[...].astype(F32),
            jnp.zeros((48, WIDE), F32),
        ],
        axis=0,
    ).T
    for x in range(4):
        full = pack([wide[(d * 4 + x) * 48 : (d * 4 + x) * 48 + 48] for d in range(8)])
        for h in range(2):
            lines[h * 4 + x, :240, :] = head[h * 4 + x]
            for t in range(5):
                lines[h * 4 + x, 240 + t * 48 : 288 + t * 48, :] = full[t].astype(BF)
    flush(1)
    half.wait()


def regroup(ready, flush, adapters, got, out, total):
    total[...] = jnp.zeros_like(total)
    ready(0)
    for n in range(8):
        a = adapters[n]
        total[a] = total[a] + got[n].astype(F32)
    for d in range(8):
        out[d, :240, :] = total[d, :240].astype(BF)
        blocks = [
            unpack(lambda t, a=a: total[a, 240 + t * 48 : 288 + t * 48, :], d) for a in range(8)
        ]
        for t, tile in enumerate(pack(blocks)):
            out[d, 240 + t * 48 : 288 + t * 48, :] = tile.astype(BF)


def gather_gradients(ready, flush, final, g_q, g_k, g_v, g_gate, g_up, g_eo, g_ed, g_xo, g_xd, wide_qkv, wide_gu, total, kv):
    @pl.loop(0, 3)
    def _(i):
        rows = pl.ds(pl.multiple_of(i * 160, 16), 160)
        total[rows, :] = sum(final[g, rows, :].astype(F32) for g in range(8))

    at = 0
    for out, blocks in (
        (g_q, 3), (kv, 3), (g_gate, 8), (g_up, 8), (g_eo, 3), (g_ed, 8), (g_xo, 12), (g_xd, 12),
    ):
        for n in range(blocks):
            line = (at + n) * 4
            out[:, n * 128 : n * 128 + 128] = total[line : line + 4, :]
        at += blocks
    both_kv = kv[...]
    g_k[...] = both_kv[:, :192]
    g_v[...] = both_kv[:, 192:]
    lane = lax.broadcasted_iota(jnp.int32, (48, 128), 1)
    for third in range(5):
        columns = jnp.zeros((48, 128), F32)
        for a in range(8):
            block = unpack(lambda t: total[240 + 48 * t : 288 + 48 * t, :], a)
            moved = pltpu.roll(block, (a * 16 - third * 16) % 128, 1)
            columns = jnp.where((lane >= a * 16) & (lane < a * 16 + 16), moved, columns)
        out, n = (wide_qkv, third) if third < 3 else (wide_gu, third - 3)
        out[:, n * 128 : n * 128 + 128] = columns


def shaped(*extent, dtype=BF):
    return jax.ShapeDtypeStruct(extent, dtype)


def call(
    body, args, outs, flops, scratch=(), scalars=(), far_in=(), far_out=(), late=None, sent=(), high=None
):
    whole = pl.BlockSpec(memory_space=pltpu.VMEM)
    small = pl.BlockSpec(memory_space=pltpu.SMEM)
    far = pl.BlockSpec(memory_space=pltpu.HBM)
    late = late or {}
    order = sorted(late, key=lambda i: late[i])
    block = [a[1:] if isinstance(a, tuple) else None for a in args]
    args = [a[0] if isinstance(a, tuple) else a for a in args]
    shapes = [a.shape if i is None else a.shape[1:] for a, i in zip(args, block)]
    extra = len(order) + len(sent) + 2

    def kernel(*refs):
        spare, sem, out_sem = refs[len(refs) - extra : -2], refs[-2], refs[-1]
        refs = list(refs[: len(refs) - extra])
        copies = []
        for n, i in enumerate(order):
            source = refs[i]
            if block[i] is not None:
                source = source.at[refs[0][high] if block[i][0] is None else block[i][0]]
            copies.append(pltpu.make_async_copy(source, spare[n], sem.at[n]))
            copies[-1].start()
            refs[i] = spare[n]
        leaving = {}
        for n, i in enumerate(sent):
            held = spare[len(order) + n]
            leaving[i] = pltpu.make_async_copy(held, refs[len(args) + i], out_sem.at[n])
            refs[len(args) + i] = held

        def ready(group):
            for n, i in enumerate(order):
                if late[i] == group:
                    copies[n].wait()

        started = []

        def flush(*which):
            for i in which:
                leaving[i].start()
                started.append(i)

        body(ready, flush, *refs)
        flush(*(i for i in sent if i not in started))
        for i in sent:
            leaving[i].wait()

    limit = 20 if body in (regroup, gather_gradients) else 59
    spares = [pltpu.VMEM(shapes[i], args[i].dtype) for i in order]
    spares += [pltpu.VMEM(outs[i].shape, outs[i].dtype) for i in sent]
    spares.append(pltpu.SemaphoreType.DMA((max(1, len(order)),)))
    spares.append(pltpu.SemaphoreType.DMA((max(1, len(sent)),)))
    return pl.pallas_call(
        kernel,
        out_shape=list(outs),
        in_specs=[
            small if i in scalars else far if i in far_in or i in late else whole
            for i in range(len(args))
        ],
        out_specs=[far if i in far_out or i in sent else whole for i in range(len(outs))],
        scratch_shapes=[*scratch, *spares],
        compiler_params=pltpu.CompilerParams(vmem_limit_bytes=limit << 20),
        cost_estimate=pl.CostEstimate(
            flops=int(flops),
            transcendentals=0,
            bytes_accessed=sum(a.size * a.dtype.itemsize for a in args),
        ),
    )(*args)


def lookup(table, index):
    return jnp.sum(jnp.where(jnp.arange(table.shape[0]) == index, table, 0))


def vector(*values):
    at = jnp.arange(len(values), dtype=jnp.int32)
    return sum(jnp.where(at == n, value, 0) for n, value in enumerate(values)).astype(jnp.int32)


def rope_tables(first):
    lane = lax.broadcasted_iota(jnp.int32, (ROWS, LANES), 1)
    position = lax.broadcasted_iota(jnp.int32, (ROWS, LANES), 0) + first
    index = lax.rem(lane, 64)
    freq = jnp.power(THETA, -2.0 * index.astype(F32) / HEAD_DIM)
    angle = position.astype(F32) * freq
    used = index < 48
    sign = jnp.where(lane < 64, -1.0, 1.0)
    return jnp.where(used, jnp.cos(angle), 0.0), jnp.where(used, sign * jnp.sin(angle), 0.0)


def per_device(
    tokens,
    cotangent,
    lengths,
    dealing,
    adapter_choice,
    attention_gain,
    feedforward_gain,
    query_weight,
    key_weight,
    value_weight,
    output_weight,
    gate_weight,
    up_weight,
    down_weight,
    entry_qkv,
    exit_query,
    exit_key,
    exit_value,
    entry_out,
    exit_out,
    entry_gate_up,
    exit_gate,
    exit_up,
    entry_down,
    exit_down,
):
    y, zl, x, zh, core = (lax.axis_index(a) for a in AXES)
    own_high = zh == 0
    entries = jnp.concatenate([entry_qkv, entry_gate_up], axis=1)
    entries = jnp.where(own_high, entries[:, :320], entries[:, 320:])
    pad = jnp.zeros((4, 128), BF)
    exits = jnp.concatenate(
        [
            exit_gate,
            exit_up,
            entry_down.T,
            jnp.where(own_high, exit_out, exit_down),
            exit_query,
            pad,
            exit_key,
            exit_value,
            pad,
            entry_out.T,
            pad,
        ],
        axis=1,
    ).reshape(48, 512)
    payload = jnp.concatenate(
        [
            query_weight,
            key_weight,
            value_weight,
            output_weight.T,
            entries,
            jnp.zeros((48, 64), BF),
            exits,
            gate_weight,
            up_weight,
            down_weight.T,
        ],
        axis=1,
    )
    send = Links()
    blocks = [payload[None, first : first + count] for first, count, _, _ in PARTS]
    blocks = [jnp.concatenate(p, 0) for p in ring_stage(send, blocks, 0, False)]
    zero, lengths, dealing, adapter_choice, _ = lax.optimization_barrier(
        (jnp.int32(0), lengths, dealing, adapter_choice, send.last)
    )
    slot = ((y * 2 + zl) * 4 + x) * 2 + zh
    sequence = lookup(dealing, slot)
    length = lookup(lengths, sequence)
    chosen = lookup(adapter_choice, sequence)
    coords = vector(y, zh * 2 + zl, x, core, chosen, length, zh)
    second = ring_stage(send, blocks, 1, True)

    def group(start, width):
        return [jnp.concatenate([q[:, :, start : start + width] for q in p], 0) for p in second]

    cosine, sine = rope_tables(zero)
    scalars = vector(length, core, zh)
    gain1, gain2 = attention_gain[None], feedforward_gain[None]
    eight = jnp.arange(8)
    peers = ((y * 2 + zl) * 4 + eight % 4) * 2 + eight // 4
    match = (jnp.arange(64)[None, :] == peers[:, None]).astype(jnp.int32)
    peer_seq = jnp.sum(match * dealing[None, :], axis=1)
    match = (jnp.arange(64)[None, :] == peer_seq[:, None]).astype(jnp.int32)
    peer_adapter = jnp.sum(match * adapter_choice[None, :], axis=1).astype(jnp.int32)
    early = (coords, cosine, sine, scalars, gain1, gain2, peer_adapter)
    early = lax.optimization_barrier(early)
    coords, cosine, sine, scalars, gain1, gain2, peer_adapter = early
    send.last = (send.last, early)
    attn_pieces = sum(ring_stage(send, group(0, ATTN), 2, True), [])
    (
        w_qkv, w_out, probs, ent_qkv, ent_gu, x_qkv, x_gu, e_out, e_down, x_od,
        normed, ranks, q, k, v, att, part,
    ) = call(
        attention_forward,
        (coords, (tokens, None), gain1, cosine, sine, *attn_pieces),
        (
            shaped(2, WIDE, 1024),
            shaped(2, WIDE, 512),
            shaped(8, ROWS, ROWS, dtype=F32),
            shaped(WIDE, LANES),
            shaped(WIDE, LANES),
            shaped(2, LANES, 1024),
            shaped(2, LANES, 2048),
            shaped(2, LANES, 512),
            shaped(2, LANES, 1024),
            shaped(2, LANES, WIDE),
            shaped(ROWS, WIDE),
            shaped(ROWS, LANES),
            shaped(8, ROWS, LANES),
            shaped(4, ROWS, LANES),
            shaped(4, ROWS, LANES),
            shaped(2, ROWS, 512),
            shaped(ROWS, PART),
        ),
        12e9,
        scratch=(
            pltpu.VMEM((2, WIDE, ATTN), BF),
            pltpu.VMEM((2, WIDE, 1024), BF),
            pltpu.VMEM((2, WIDE, 512), BF),
            pltpu.VMEM((8, ROWS, ROWS), F32),
            pltpu.SemaphoreType.DMA((5,)),
        ),
        scalars=(0,),
        far_in=tuple(range(5, 15)),
        far_out=(0, 1, 2),
        sent=tuple(range(3, 17)),
        late={1: 0},
        high=6,
    )
    x_out, x_down = x_od[0], x_od[1]
    mlp_pieces = sum(ring_stage(send, group(ATTN, MLP), 2, True, lambda: part), [])
    middle, rank_out, hidden, g2, ranks_gu, drank_down = call(
        mlp_start,
        (scalars, (tokens, None), part, core_swap(part), (cotangent, None), gain2, x_out, ent_gu, x_down),
        (
            shaped(ROWS, WIDE, dtype=F32),
            shaped(ROWS, LANES),
            shaped(ROWS, WIDE),
            shaped(ROWS, WIDE),
            shaped(ROWS, LANES),
            shaped(ROWS, LANES),
        ),
        1e9,
        scalars=(0,),
        late={1: 0, 2: 0, 3: 0, 4: 0, 6: 0, 7: 0, 8: 0},
        sent=(0, 1, 2, 3, 4, 5),
        high=2,
    )
    parts, gx_gu, ge_down = call(
        mlp,
        (coords, hidden, g2, ranks_gu, drank_down, x_gu, e_down, *mlp_pieces),
        (shaped(2, ROWS, PART), shaped(2, 32, 2048), shaped(2, 16, 1024)),
        15e9,
        scratch=(
            pltpu.VMEM((2, ROWS, 2048), BF),
            pltpu.VMEM((2, ROWS, 1024), BF),
            pltpu.VMEM((2, WIDE, MLP), BF),
            pltpu.SemaphoreType.DMA((2,)),
        ),
        scalars=(0,),
        far_in=tuple(range(7, 17)),
        late={1: 0, 2: 0, 3: 0, 4: 0, 5: 0, 6: 0},
        sent=(0, 1, 2),
    )
    others = core_swap(parts)
    grad_middle, part_qkv, mixed, gx_qkv, ge_out, shared, wide_gu, mixed_half = call(
        attention_backward,
        (
            scalars, g2, (parts, 0), (others, 0), middle, gain2, ent_gu, x_out, e_out, x_qkv, cosine, sine,
            q, k, v, probs, w_out, w_qkv, (parts, 1), (others, 1), x_down, rank_out, hidden, ranks, att,
        ),
        (
            shaped(ROWS, WIDE, dtype=F32),
            shaped(ROWS, PART),
            shaped(ROWS, WIDE),
            shaped(2, 48, 1024),
            shaped(2, 16, 512),
            shaped(2, 16, WIDE),
            shaped(32, WIDE),
            shaped(192, WIDE),
        ),
        8e9,
        scratch=(
            pltpu.VMEM((ROWS, WIDE), BF),
            pltpu.VMEM((ROWS, LANES), BF),
            pltpu.VMEM((ROWS, LANES), BF),
            pltpu.VMEM((2, ROWS, 1024), BF),
            pltpu.VMEM((8, ROWS, LANES), BF),
            pltpu.VMEM((ROWS, LANES), F32),
            pltpu.VMEM((ROWS, LANES), F32),
            pltpu.VMEM((ROWS, LANES), BF),
            pltpu.SemaphoreType.DMA(()),
        ),
        scalars=(0,),
        far_out=(7,),
        late={
            1: 0, 2: 0, 3: 0, 4: 0, 6: 0, 7: 1, 8: 1, 16: 1, 10: 2, 11: 2, 12: 2, 13: 2, 14: 2, 15: 2,
            9: 3, 17: 3, 18: 3, 19: 3, 20: 3, 21: 3, 22: 3, 23: 3, 24: 3,
        },
        sent=(0, 1, 2, 3, 4, 5, 6),
    )
    other_qkv = core_swap(part_qkv)
    (head,) = call(
        head_lines,
        (gx_qkv, gx_gu, ge_out, ge_down, shared),
        (shaped(8, 240, 128),),
        1e8,
        scratch=(pltpu.VMEM((16, 7296), F32), pltpu.VMEM((240, 128), F32)),
        late={0: 0, 1: 0, 2: 0, 3: 0, 4: 0},
        sent=(0,),
    )
    grad_in, lines, in_half = call(
        input_backward,
        (scalars, (tokens, None), part_qkv, other_qkv, grad_middle, gain1, ent_qkv, normed, wide_gu, head),
        (shaped(ROWS, WIDE), shaped(8, 480, 128), shaped(192, WIDE)),
        1e9,
        scratch=(pltpu.VMEM((ROWS, LANES), BF), pltpu.SemaphoreType.DMA(())),
        scalars=(0,),
        far_out=(2,),
        late={1: 0, 2: 0, 3: 0, 4: 0, 6: 0, 7: 1, 8: 1, 9: 1},
        sent=(0, 1),
        high=2,
    )
    to_other_chip = flip_pairs("zz", (2, 2))
    sent_mixed = lax.ppermute(mixed_half, AXES, to_other_chip)
    lines, sent_mixed = lax.optimization_barrier((lines, sent_mixed))
    got = lax.all_to_all(lines, ("zh", "x"), 0, 0, tiled=True)
    in_half, got = lax.optimization_barrier((in_half, got))
    sent_in = lax.ppermute(in_half, AXES, to_other_chip)
    (second,) = call(
        regroup,
        (peer_adapter, got),
        (shaped(8, 480, 128),),
        1e6,
        scratch=(pltpu.VMEM((8, 480, 128), F32),),
        scalars=(0,),
        late={1: 0},
        sent=(0,),
    )
    final = lax.all_to_all(second, ("y", "zl"), 0, 0, tiled=True)

    def share(value, got):
        value, got, _ = lax.optimization_barrier((value, got, second))
        rest = core_swap(got)
        low, high = jnp.where(core == 0, got, rest), jnp.where(core == 0, rest, got)
        other = jnp.concatenate([low, high], axis=0)
        return jnp.stack([jnp.where(own_high, value, other), jnp.where(own_high, other, value)])

    mixed, grad_in = share(mixed, sent_mixed), share(grad_in, sent_in)
    final, mixed, grad_in = lax.optimization_barrier((final, mixed, grad_in))
    g_q, g_k, g_v, g_gate, g_up, g_eo, g_ed, g_xo, g_xd, wide_qkv, wide_gu = call(
        gather_gradients,
        (final,),
        (
            shaped(4, 384, dtype=F32),
            shaped(4, 192, dtype=F32),
            shaped(4, 192, dtype=F32),
            shaped(4, 1024, dtype=F32),
            shaped(4, 1024, dtype=F32),
            shaped(4, 384, dtype=F32),
            shaped(4, 1024, dtype=F32),
            shaped(4, WIDE, dtype=F32),
            shaped(4, WIDE, dtype=F32),
            shaped(48, 384, dtype=F32),
            shaped(48, 256, dtype=F32),
        ),
        1e6,
        scratch=(pltpu.VMEM((480, LANES), F32), pltpu.VMEM((4, 384), F32)),
    )

    return (
        mixed,
        grad_in,
        wide_qkv,
        g_q,
        g_k,
        g_v,
        g_eo.T,
        g_xo,
        wide_gu,
        g_gate,
        g_up,
        g_ed.T,
        g_xd,
    )


def solution(mesh):
    fine = Mesh(mesh.devices.reshape(SIZES), AXES)
    dp, mp = ("y", "zl", "x"), ("zh", "c")
    return jax.shard_map(
        per_device,
        mesh=fine,
        in_specs=(
            P(dp, None, None),
            P(dp, None, None),
            P(),
            P(),
            P(),
            P(),
            P(),
            P(dp, mp),
            P(dp, mp),
            P(dp, mp),
            P(mp, dp),
            P(dp, mp),
            P(dp, mp),
            P(mp, dp),
            P(dp, None),
            P(dp, mp),
            P(dp, mp),
            P(dp, mp),
            P(mp, dp),
            P(dp, None),
            P(dp, None),
            P(dp, mp),
            P(dp, mp),
            P(mp, dp),
            P(dp, None),
        ),
        out_specs=(
            P(dp, None, None),
            P(dp, None, None),
            P(dp, None),
            P(dp, mp),
            P(dp, mp),
            P(dp, mp),
            P(mp, dp),
            P(dp, None),
            P(dp, None),
            P(dp, mp),
            P(dp, mp),
            P(mp, dp),
            P(dp, None),
        ),
        check_vma=False,
    )
```
